32 devices in a mesh: section: 2 (over core), dp: 4 (over y, x), ctx: 4 (over z).
Axes of the slice: x: 2, y: 2, z: 4, core: 2. Of those that a mesh axis runs over, the one named last changes fastest.
Arguments:
- ends: bfloat16 [2, 8, 1024, 768], P('section', 'dp', 'ctx'), may hold values from -6 to 6
- segment_ids: int32 [8, 1024], P('dp', 'ctx'), may hold values from 0 to 3, as said below
- ln1_gain: float32 [2, 768], P('section'), may hold values from 0.5 to 1.5
- ln1_bias: float32 [2, 768], P('section'), may hold values from -1.5 to 1.5
- qkv_weight: bfloat16 [2, 768, 1920], P('section'), may hold values from -0.21875 to 0.21875
- out_weight: bfloat16 [2, 768, 768], P('section'), may hold values from -0.875 to 0.875
- ln2_gain: float32 [2, 768], P('section'), may hold values from 0.5 to 1.5
- ln2_bias: float32 [2, 768], P('section'), may hold values from -1.5 to 1.5
- fc_weight: bfloat16 [2, 768, 3072], P('section'), may hold values from -0.21875 to 0.21875
- fc_bias: float32 [2, 3072], P('section'), may hold values from -2.5 to 2.5
- proj_weight: bfloat16 [2, 3072, 768], P('section'), may hold values from -0.109375 to 0.109375
- shared_weight: bfloat16 [768, 384], replicated, may hold values from -0.21875 to 0.21875
Outputs:
- block_ends: float32 [2, 8, 1024, 768], P('section', 'dp', 'ctx')
- qkv_grad: float32 [2, 768, 1920], P('section', ('dp', 'ctx'))
- out_grad: float32 [2, 768, 768], P('section', ('dp', 'ctx'))
- fc_grad: float32 [2, 768, 3072], P('section', ('dp', 'ctx'))
- fc_bias_grad: float32 [2, 3072], P('section', ('dp', 'ctx'))
- proj_grad: float32 [2, 3072, 768], P('section', ('dp', 'ctx'))
- shared_grad: float32 [768, 384], P(('dp', 'ctx'))
- ln1_gain_grad: float32 [2, 768], P('section', ('dp', 'ctx'))
- ln1_bias_grad: float32 [2, 768], P('section', ('dp', 'ctx'))
- ln2_gain_grad: float32 [2, 768], P('section', ('dp', 'ctx'))
- ln2_bias_grad: float32 [2, 768], P('section', ('dp', 'ctx'))
The draws below stay inside these ranges and needn't reach their ends.
Inputs may be any that keep to these rules, and one draw needn't show every extreme that they name: `segment_ids`: along each row the ids start at 0 and rise by 0 or 1 from one position to the next; each row holds either one document or exactly 4; in each aligned block of 2 rows exactly one row holds a single document.
All inputs are finite; a program needn't handle non-finite values.
Results may differ from the reference program's by a relative error of at most 0.024.
Values may be sent and summed in bfloat16 or wider, within the bound.
A program may use at most 256 MiB of HBM per device.

```python
import jax
import jax.numpy as jnp
from jax import lax

D = 768
HEADS = 12
HEAD = 64
FF = 3072
QKV = 1920
MICRO = 2
LEN = 1024
ROWS = 8


def draw_segment_ids(key, part):
    key = jax.random.fold_in(key, 11)
    pick_key, cut_key = jax.random.split(key)
    row_keys = jax.random.split(cut_key, ROWS)

    def row_cuts(row_key):
        return jax.random.choice(row_key, LEN - 1, (3,), replace=False).astype(jnp.int32) + 1
    cuts = jax.vmap(row_cuts)(row_keys)
    positions = jnp.arange(LEN, dtype=jnp.int32)
    cut_flags = jnp.sum((positions[None, None, :] == cuts[:, :, None]).astype(jnp.int32), axis=1)
    chosen = jax.random.randint(pick_key, (ROWS // MICRO,), 0, MICRO)
    row_in_block = jnp.arange(ROWS) % MICRO
    single = row_in_block == jnp.repeat(chosen, MICRO)
    cut_flags = jnp.where(single[:, None], 0, cut_flags)
    return jnp.cumsum(cut_flags, axis=1).astype(jnp.int32)


def block_scale(own_key, dims, shards, least, high):
    factor_of, own = 1.0, jax.random.fold_in(own_key, 6)
    for axis_at, parts in shards:
        heights = jnp.exp(jax.random.uniform(jax.random.fold_in(own, axis_at), (parts,), jnp.float32, least / len(shards), high / len(shards)))
        factor_of = factor_of * jnp.repeat(heights, dims[axis_at] // parts).reshape([-1 if axis == axis_at else 1 for axis in range(len(dims))])
    return factor_of


def scatter_about(rng, shape, scale, most, pieces=(), kind=jnp.bfloat16):
    drawn = jax.random.normal(rng, shape, jnp.float32) * scale
    if len(pieces) > 0:
        drawn = block_scale(rng, shape, pieces, -0.22, 0.18) * drawn
    return jnp.clip(drawn, min=-most, max=most).astype(kind)


def setup_inputs(seed: int = 0) -> dict:
    key_list = jax.random.split(jax.random.key(seed), 13)
    return {
        "ends": scatter_about(key_list[0], (2, ROWS, LEN, D), 1.0, 6.0, ((0, 2), (1, 4), (2, 4))),
        "segment_ids": draw_segment_ids(jax.random.fold_in(key_list[12], 71), 0),
        "ln1_gain": jnp.clip(1.0 + 0.1 * jax.random.normal(key_list[2], (2, D), jnp.float32), 0.5, 1.5),
        "ln1_bias": scatter_about(key_list[3], (2, D), 0.3, 1.5, ((0, 2),), jnp.float32),
        "qkv_weight": scatter_about(key_list[4], (2, D, QKV), D ** -0.5, 0.21875, ((0, 2),)),
        "out_weight": scatter_about(key_list[5], (2, D, D), (D // 16) ** -0.5, 0.875, ((0, 2),)),
        "ln2_gain": jnp.clip(1.0 + 0.1 * jax.random.normal(key_list[6], (2, D), jnp.float32), 0.5, 1.5),
        "ln2_bias": scatter_about(key_list[7], (2, D), 0.3, 1.5, ((0, 2),), jnp.float32),
        "fc_weight": scatter_about(key_list[8], (2, D, FF), D ** -0.5, 0.21875, ((0, 2),)),
        "fc_bias": scatter_about(key_list[9], (2, FF), 0.5, 2.5, ((0, 2),), jnp.float32),
        "proj_weight": scatter_about(key_list[10], (2, FF, D), FF ** -0.5, 0.109375, ((0, 2),)),
        "shared_weight": scatter_about(key_list[11], (D, D // 2), D ** -0.5, 0.21875),
    }


EPSILON = 1e-05
MASKED = -1000000000.0
PRECISE = lax.Precision.HIGHEST

@jax.custom_vjp
def low(v):
    return lax.optimization_barrier(v.astype(jnp.bfloat16)).astype(jnp.float32)

@jax.custom_vjp
def low_back(v):
    return v

def low_keep(v):
    return (low(v), None)

def low_pass(kept, grad):
    return (grad,)

def back_keep(v):
    return (v, None)

def back_low(kept, grad):
    return (low(grad),)
low.defvjp(low_keep, low_pass)
low_back.defvjp(back_keep, back_low)

def layer_norm(values, gain, bias):
    row_mean = lax.optimization_barrier(jnp.mean(values, axis=-1, keepdims=True))
    centred = values - row_mean
    spread = lax.optimization_barrier(jnp.mean(centred * centred, axis=-1, keepdims=True))
    return centred * lax.rsqrt(spread + EPSILON) * gain + bias

def gelu_tanh(inputs):
    return 0.5 * inputs * (1.0 + jnp.tanh(0.7978845608028654 * (inputs + 0.044715 * inputs * inputs * inputs)))

def matmul(left, right):
    return jnp.dot(left, right, precision=PRECISE)

def attention(queries, keys_all, values, segment):
    length = queries.shape[0]
    query_heads = queries.reshape(length, HEADS, HEAD)
    key_heads = keys_all.reshape(length, HEADS, HEAD)
    value_heads = values.reshape(length, HEADS, HEAD)
    scores = jnp.einsum('qhd,khd->hqk', query_heads, key_heads, precision=PRECISE) * HEAD ** (-0.5)
    scores = low_back(scores)
    positions = jnp.arange(length)
    allowed = (positions[None, :] <= positions[:, None]) & (segment[None, :] == segment[:, None])
    scores = jnp.where(allowed[None], scores, MASKED)
    row_top = lax.optimization_barrier(jnp.max(scores, axis=-1, keepdims=True))
    exponent = jnp.exp(scores - row_top)
    attn_probs = low(exponent / lax.optimization_barrier(jnp.sum(exponent, axis=-1, keepdims=True)))
    attended = jnp.einsum('hqk,khd->qhd', attn_probs, value_heads, precision=PRECISE)
    return attended.reshape(length, HEADS * HEAD)

def layer(resid, source, weights, segment):
    gain1, bias1, qkv_w, out_w, gain2, bias2, fc_w, fc_b, proj_w, shared_w = weights
    normed = low(layer_norm(resid, gain1, bias1))
    if source is None:
        source = normed
    packed = low(low_back(matmul(normed, qkv_w)))
    reused = low(low_back(matmul(source, shared_w)))
    queries = packed[:, :D]
    keys_all = packed[:, D:2 * D]
    values = jnp.concatenate([reused, packed[:, 2 * D:]], axis=1)
    attended = low(low_back(attention(queries, keys_all, values, segment)))
    branch = low_back(matmul(attended, out_w))
    hidden = resid + branch
    normed2 = low(layer_norm(hidden, gain2, bias2))
    up_proj = low_back(matmul(normed2, fc_w) + fc_b)
    activated = low(gelu_tanh(up_proj))
    mlp_out = low_back(matmul(activated, proj_w))
    return (hidden + mlp_out, normed)

def two_layers(params, block_in, segment):
    gain1, bias1, qkv_w, out_w, gain2, bias2, fc_w, fc_b, proj_w, shared_w = params
    first_weights = (gain1[0], bias1[0], qkv_w[0], out_w[0], gain2[0], bias2[0], fc_w[0], fc_b[0], proj_w[0], shared_w)
    second_weights = (gain1[1], bias1[1], qkv_w[1], out_w[1], gain2[1], bias2[1], fc_w[1], fc_b[1], proj_w[1], shared_w)
    first_out, first_normed = layer(block_in, None, first_weights, segment)
    sent = low(first_out)
    second_out, second_normed = layer(sent, first_normed, second_weights, segment)
    return second_out

def reference(ends, segment_ids, ln1_gain, ln1_bias, qkv_weight, out_weight, ln2_gain, ln2_bias, fc_weight, fc_bias, proj_weight, shared_weight):
    params = (ln1_gain.astype(jnp.float32), ln1_bias.astype(jnp.float32), qkv_weight.astype(jnp.float32), out_weight.astype(jnp.float32), ln2_gain.astype(jnp.float32), ln2_bias.astype(jnp.float32), fc_weight.astype(jnp.float32), fc_bias.astype(jnp.float32), proj_weight.astype(jnp.float32), shared_weight.astype(jnp.float32))
    ends_wide = ends.astype(jnp.float32)

    def row_step(totals, row_data):
        block_in, cotangent, segment = row_data

        def row_fn(weights_in, inputs):
            return two_layers(weights_in, inputs, segment)
        result, back_fn = jax.vjp(row_fn, params, block_in)
        grads, grad_input = back_fn(cotangent)
        totals = jax.tree.map(jnp.add, totals, grads)
        return (totals, (result, grad_input))
    zeros = jax.tree.map(jnp.zeros_like, params)
    totals, (outputs, grad_inputs) = lax.scan(row_step, zeros, (ends_wide[0], ends_wide[1], segment_ids))
    g_gain1, g_bias1, g_qkv, g_out, g_gain2, g_bias2, g_fc, g_fcb, g_proj, g_shared = totals
    block_ends = jnp.stack([grad_inputs, outputs])
    return (block_ends, g_qkv, g_out, g_fc, g_fcb, g_proj, g_shared, g_gain1, g_bias1, g_gain2, g_bias2)
```

```python
import functools

import jax
import jax.numpy as jnp
from jax import lax
from jax.experimental import pallas as pl
from jax.experimental.pallas import tpu as pltpu
from jax.sharding import PartitionSpec as P

HEAD = 64
EPSILON = 1e-05
MASKED = -1000000000.0
F32 = jnp.float32
BF16 = jnp.bfloat16
VMEM_LIMIT = 56 * 2**20


def mm(left, right):
    return jnp.dot(left, right, preferred_element_type=F32)


def mm_nt(left, right):
    return lax.dot_general(left, right, (((1,), (1,)), ((), ())), preferred_element_type=F32)


def mm_tn(left, right):
    return lax.dot_general(left, right, (((0,), (0,)), ((), ())), preferred_element_type=F32)


def norm_parts(values):
    mean = jnp.mean(values, axis=-1, keepdims=True)
    centred = values - mean
    spread = jnp.mean(centred * centred, axis=-1, keepdims=True)
    rstd = lax.rsqrt(spread + EPSILON)
    return centred * rstd, rstd


def layer_norm(values, gain, bias):
    return norm_parts(values)[0] * gain + bias


def norm_back(values, gain, grad):
    unit, rstd = norm_parts(values)
    scaled = grad * gain
    m1 = jnp.mean(scaled, axis=-1, keepdims=True)
    m2 = jnp.mean(scaled * unit, axis=-1, keepdims=True)
    return rstd * (scaled - m1 - unit * m2), jnp.sum(grad * unit, axis=0), jnp.sum(grad, axis=0)


def gelu(u):
    return 0.5 * u * (1.0 + jnp.tanh(0.7978845608028654 * (u + 0.044715 * u * u * u)))


def gelu_grad(u):
    t = jnp.tanh(0.7978845608028654 * (u + 0.044715 * u * u * u))
    return 0.5 * (1.0 + t) + 0.5 * u * (1.0 - t * t) * 0.7978845608028654 * (1.0 + 3 * 0.044715 * u * u)


def swap(x):
    return lax.ppermute(x, "section", [(0, 1), (1, 0)])


def fwd_attention_kernel(T, q_ref, k_ref, v_ref, qpos_ref, qseg_ref, kseg_ref, o_ref, lse_ref, bias):
    L = k_ref.shape[0]

    @pl.when(pl.program_id(0) == 0)
    def _():
        kpos = lax.broadcasted_iota(jnp.int32, (2 * T, L), 1)
        allowed = (kpos <= qpos_ref[...]) & (kseg_ref[...] == qseg_ref[...])
        bias[...] = jnp.where(allowed, 0.0, MASKED)

    lane = lax.broadcasted_iota(jnp.int32, (T, 128), 1)
    for part in range(2):
        rows = slice(part * T, (part + 1) * T)
        keys = L // 2 if part == 0 else L
        q2 = q_ref[rows, :]
        outs, lses = [], []
        for h in range(2):
            qh = jnp.where((lane >= 64) == (h == 1), q2, jnp.zeros_like(q2)) * jnp.asarray(HEAD**-0.5, BF16)
            s = mm_nt(qh, k_ref[:keys, :]) + bias[rows, :keys]
            top = jnp.max(s, axis=-1, keepdims=True)
            e = jnp.exp(s - top)
            total = jnp.sum(e, axis=-1, keepdims=True)
            prob = (e * (1.0 / total)).astype(BF16)
            outs.append(mm(prob, v_ref[:keys, :]))
            lses.append(top + jnp.log(total))
        o_ref[rows, :] = jnp.where(lane < 64, outs[0], outs[1]).astype(BF16)
        lse_ref[0, rows, :] = jnp.where(lane < 64, lses[0], lses[1])


def fwd_attention(q, k, v, qpos, qseg, kseg):
    rows, width = q.shape
    T, L = rows // 2, k.shape[0]
    pairs = width // 128
    col = lambda n: pl.BlockSpec((n, 128), lambda i: (0, i))
    full = lambda a: pl.BlockSpec(a.shape, lambda i: (0, 0))
    return pl.pallas_call(
        functools.partial(fwd_attention_kernel, T),
        grid=(pairs,),
        in_specs=[col(rows), col(L), col(L), full(qpos), full(qseg), full(kseg)],
        out_specs=[col(rows), pl.BlockSpec((1, rows, 128), lambda i: (i, 0, 0))],
        out_shape=[jax.ShapeDtypeStruct((rows, width), BF16), jax.ShapeDtypeStruct((pairs, rows, 128), F32)],
        scratch_shapes=[pltpu.VMEM((rows, L), F32)],
        compiler_params=pltpu.CompilerParams(vmem_limit_bytes=VMEM_LIMIT),
        name="attention_forward",
    )(q, k, v, qpos, qseg, kseg)


def bwd_attention_kernel(T, q_ref, k_ref, v_ref, go_ref, o_ref, lse_ref, qpos_ref, qseg_ref, kseg_ref,
                         dq_ref, dk_ref, dv_ref, bias):
    L = k_ref.shape[0]

    @pl.when(pl.program_id(0) == 0)
    def _():
        kpos = lax.broadcasted_iota(jnp.int32, (2 * T, L), 1)
        allowed = (kpos <= qpos_ref[...]) & (kseg_ref[...] == qseg_ref[...])
        bias[...] = jnp.where(allowed, 0.0, MASKED)

    lane = lax.broadcasted_iota(jnp.int32, (T, 128), 1)
    lane_k = lax.broadcasted_iota(jnp.int32, (L, 128), 1)
    scale = jnp.asarray(HEAD**-0.5, BF16)
    for part in (1, 0):
        rows = slice(part * T, (part + 1) * T)
        keys = L // 2 if part == 0 else L
        q2 = q_ref[rows, :]
        go2 = go_ref[rows, :]
        prod = go2.astype(F32) * o_ref[rows, :].astype(F32)
        lse2 = lse_ref[0, rows, :]
        dqs, dks, dvs = [], [], []
        for h in range(2):
            sel = (lane >= 64) == (h == 1)
            qh = jnp.where(sel, q2, jnp.zeros_like(q2)) * scale
            goh = jnp.where(sel, go2, jnp.zeros_like(go2))
            delta = jnp.sum(jnp.where(sel, prod, 0.0), axis=-1, keepdims=True)
            s = mm_nt(qh, k_ref[:keys, :]) + bias[rows, :keys]
            prob = jnp.exp(s - lse2[:, 64 * h : 64 * h + 1])
            gp = mm_nt(goh, v_ref[:keys, :])
            gs = (prob * (gp - delta)).astype(BF16)
            dqs.append(mm(gs, k_ref[:keys, :]))
            dks.append(mm_tn(gs, qh))
            dvs.append(mm_tn(prob.astype(BF16), goh))
        dq_ref[rows, :] = (jnp.where(lane < 64, dqs[0], dqs[1]) * HEAD**-0.5).astype(BF16)
        dk = dks[0] + dks[1]
        dv = dvs[0] + dvs[1]
        if part == 1:
            dk_ref[...] = dk
            dv_ref[...] = dv
        else:
            dk_ref[:keys, :] += dk
            dv_ref[:keys, :] += dv


def bwd_attention(q, k, v, go, o, lse, qpos, qseg, kseg):
    rows, width = q.shape
    T, L = rows // 2, k.shape[0]
    pairs = width // 128
    col = lambda n: pl.BlockSpec((n, 128), lambda i: (0, i))
    full = lambda a: pl.BlockSpec(a.shape, lambda i: (0, 0))
    return pl.pallas_call(
        functools.partial(bwd_attention_kernel, T),
        grid=(pairs,),
        in_specs=[col(rows), col(L), col(L), col(rows), col(rows), pl.BlockSpec((1, rows, 128), lambda i: (i, 0, 0)),
                  full(qpos), full(qseg), full(kseg)],
        out_specs=[col(rows), col(L), col(L)],
        out_shape=[jax.ShapeDtypeStruct((rows, width), BF16), jax.ShapeDtypeStruct((L, width), F32),
                   jax.ShapeDtypeStruct((L, width), F32)],
        scratch_shapes=[pltpu.VMEM((rows, L), F32)],
        compiler_params=pltpu.CompilerParams(vmem_limit_bytes=VMEM_LIMIT),
        name="attention_backward",
    )(q, k, v, go, o, lse, qpos, qseg, kseg)


def xor_route(size, bit):
    return [(i, i ^ (1 << bit)) for i in range(size)]


def halve(grad, axis_name, bit, at):
    mine = (lax.axis_index(axis_name) >> bit) & 1
    keep = lax.dynamic_index_in_dim(grad, mine, at, keepdims=False)
    send = lax.dynamic_index_in_dim(grad, 1 - mine, at, keepdims=False)
    got = lax.ppermute(send, axis_name, xor_route(lax.axis_size(axis_name), bit))
    return (keep.astype(F32) + got.astype(F32)).astype(grad.dtype)


def bits_of(axis_name):
    return lax.axis_size(axis_name).bit_length() - 1


def scatter_sum(grad, order, skip_first=False):
    dims = [("dp", b) for b in reversed(range(bits_of("dp")))] + [("ctx", b) for b in reversed(range(bits_of("ctx")))]
    if skip_first:
        dims = dims[1:]
    parts = len(dims)
    rows, cols = grad.shape
    grad = grad.reshape((2,) * parts + (rows >> parts, cols))
    for item in order:
        at = dims.index(item)
        grad = halve(grad, item[0], item[1], at)
        dims.pop(at)
    return grad


def shards(ends, segment_ids, ln1_gain, ln1_bias, qkv_weight, out_weight, ln2_gain, ln2_bias, fc_weight, fc_bias,
           proj_weight, shared_weight):
    core = lax.axis_index("section")
    place = lax.axis_index("ctx")
    C = lax.axis_size("ctx")
    N = C // 2
    micros, T, D = ends.shape[1:]
    L = T * C
    half = D // 2
    F = fc_weight.shape[2]
    FH = F // 2
    upper = place >= N
    row = upper.astype(jnp.int32)
    reverse = [(i, C - 1 - i) for i in range(C)]
    first = core == 0

    mine = lax.dynamic_index_in_dim(ends[0], row, 0, keepdims=False)
    other = lax.dynamic_index_in_dim(ends[0], 1 - row, 0, keepdims=False)
    got = lax.ppermute(other, "ctx", reverse)
    both = jnp.where(upper, jnp.concatenate([got, mine], 0), jnp.concatenate([mine, got], 0))
    both_other = swap(both)
    x_in = jnp.where(first, both, both_other)
    g_out = jnp.where(first, both_other, both)

    lo = jnp.minimum(place, C - 1 - place)
    hi = C - 1 - lo
    seg_pieces = [(place, segment_ids)]
    for k in range(1, C):
        seg_pieces.append((lax.rem(place + C - k, C), lax.ppermute(segment_ids, "ctx", [(i, (i + k) % C) for i in range(C)])))
    seg_row = jnp.zeros((C, T), jnp.int32)
    for at, piece in seg_pieces:
        seg_row = lax.dynamic_update_slice(seg_row, lax.dynamic_index_in_dim(piece, row, 0, keepdims=True), (at, 0))
    kseg = seg_row.reshape(1, L)
    qseg = jnp.concatenate([lax.dynamic_index_in_dim(seg_row, lo, 0, keepdims=False),
                            lax.dynamic_index_in_dim(seg_row, hi, 0, keepdims=False)]).reshape(2 * T, 1)
    qpos = jnp.concatenate([lo * T + jnp.arange(T), hi * T + jnp.arange(T)]).astype(jnp.int32).reshape(2 * T, 1)

    def qkv_half(c):
        wq = lax.dynamic_slice_in_dim(qkv_weight[0], c * half, half, 1)
        wk = lax.dynamic_slice_in_dim(qkv_weight[0], D + c * half, half, 1)
        wv = jnp.where(c == 0, shared_weight, qkv_weight[0][:, 2 * D :])
        return jnp.concatenate([wq, wk, wv], axis=1)

    def halves(c):
        return (qkv_half(c), lax.dynamic_slice_in_dim(out_weight[0], c * half, half, 0),
                lax.dynamic_slice_in_dim(fc_weight[0], c * FH, FH, 1), lax.dynamic_slice_in_dim(proj_weight[0], c * FH, FH, 0))

    own_half = halves(core)
    got_half = tuple(swap(w) for w in halves(1 - core))
    small = jnp.concatenate([ln1_gain[0], ln1_bias[0], ln2_gain[0], ln2_bias[0], fc_bias[0]])
    small_other = swap(small)

    def layer_weights(l):
        is_own = core == l
        ws = tuple(jnp.where(is_own, a, b) for a, b in zip(own_half, got_half))
        sm = jnp.where(is_own, small, small_other)
        norms = tuple(sm[i * D : (i + 1) * D] for i in range(4))
        return ws + (norms, lax.dynamic_slice_in_dim(sm, 4 * D + core * FH, FH, 0))

    weights = [layer_weights(0), layer_weights(1)]

    def to_group(blocks):
        send = jnp.where(first, blocks[:T], blocks[T:])
        out = jnp.zeros((C, T, D), blocks.dtype)
        out = lax.dynamic_update_slice(out, blocks[:T][None], (lo, 0, 0))
        out = lax.dynamic_update_slice(out, blocks[T:][None], (hi, 0, 0))
        base = jnp.where(upper, N, 0)
        for k in range(1, N):
            route = [(g * N + i, g * N + (i + k) % N) for g in range(2) for i in range(N)]
            piece = lax.ppermute(send, "ctx", route)
            other_piece = swap(piece)
            src = base + lax.rem(place - base + N - k, N)
            slo = jnp.minimum(src, C - 1 - src)
            a = jnp.where(first, piece, other_piece)
            b = jnp.where(first, other_piece, piece)
            out = lax.dynamic_update_slice(out, a[None], (slo, 0, 0))
            out = lax.dynamic_update_slice(out, b[None], (C - 1 - slo, 0, 0))
        return out.reshape(L, D)

    def from_group(parts):
        parts = parts.reshape(C, T, D)
        base = jnp.where(upper, N, 0)
        own = jnp.concatenate([lax.dynamic_index_in_dim(parts, lo, 0, keepdims=False),
                               lax.dynamic_index_in_dim(parts, hi, 0, keepdims=False)], 0)
        sums = None
        for k in range(1, N):
            dst = base + lax.rem(place - base + k, N)
            dlo = jnp.minimum(dst, C - 1 - dst)
            plo = lax.dynamic_index_in_dim(parts, dlo, 0, keepdims=False)
            phi = lax.dynamic_index_in_dim(parts, C - 1 - dlo, 0, keepdims=False)
            keep = jnp.where(first, plo, phi)
            give = jnp.where(first, phi, plo).astype(BF16)
            pair = (keep + swap(give).astype(F32)).astype(BF16)
            route = [(g * N + i, g * N + (i + k) % N) for g in range(2) for i in range(N)]
            come = lax.ppermute(pair, "ctx", route).astype(F32)
            sums = come if sums is None else sums + come
        zero = jnp.zeros_like(own[:T])
        extra = jnp.where(first, jnp.concatenate([sums, zero], 0), jnp.concatenate([zero, sums], 0))
        own = own + extra
        return own + swap(own.astype(BF16)).astype(F32)

    def pair_sum(x):
        return x + swap(x.astype(BF16)).astype(F32)

    def forward(l, resid, first_all):
        wqkv, wout, wfc, wproj, (g1, b1, g2, b2), fcb = weights[l]
        normed = layer_norm(resid, g1, b1).astype(BF16)
        normed_all = to_group(normed)
        source_all = normed_all if l == 0 else first_all
        value_in = jnp.where(first, source_all, normed_all)
        q = mm(normed, wqkv[:, :half]).astype(BF16)
        k = mm(normed_all, wqkv[:, half : 2 * half]).astype(BF16)
        v = mm(value_in, wqkv[:, 2 * half :]).astype(BF16)
        o, lse = fwd_attention(q, k, v, qpos, qseg, kseg)
        hidden = resid + pair_sum(mm(o, wout))
        normed2 = layer_norm(hidden, g2, b2).astype(BF16)
        up = mm(normed2, wfc) + fcb
        act = gelu(up).astype(BF16)
        out = hidden + pair_sum(mm(act, wproj))
        return out, dict(resid=resid, normed=normed, normed_all=normed_all, value_in=value_in, q=q, k=k, v=v, o=o,
                         lse=lse, hidden=hidden, normed2=normed2, up=up, act=act)

    def backward(l, st, grad_out, source_part):
        wqkv, wout, wfc, wproj, (g1, b1, g2, b2), fcb = weights[l]
        gm = grad_out.astype(BF16)
        gu = (gelu_grad(st["up"]) * mm_nt(gm, wproj)).astype(BF16)
        proj_g = mm_tn(st["act"], gm).astype(BF16)
        fc_g = mm_tn(st["normed2"], gu).astype(BF16)
        fcb_g = jnp.sum(gu.astype(F32), axis=0)
        gn2 = pair_sum(mm_nt(gu, wfc))
        gh, g2_g, b2_g = norm_back(st["hidden"], g2, gn2)
        gh = gh + grad_out
        gb = gh.astype(BF16)
        go = mm_nt(gb, wout).astype(BF16)
        out_g = mm_tn(st["o"], gb).astype(BF16)
        dq, dk, dv = bwd_attention(st["q"], st["k"], st["v"], go, st["o"], st["lse"], qpos, qseg, kseg)
        dk = dk.astype(BF16)
        dv = dv.astype(BF16)
        wq, wk, wv = wqkv[:, :half], wqkv[:, half : 2 * half], wqkv[:, 2 * half :]
        from_v = mm_nt(dv, wv)
        parts = mm_nt(dk, wk)
        if l == 0:
            parts = parts + from_v + source_part
            next_source = None
        else:
            parts = parts + jnp.where(first, 0.0, from_v)
            next_source = jnp.where(first, from_v, 0.0)
        own_q = mm_nt(dq, wq)
        parts = parts.reshape(C, T, D)
        parts = lax.dynamic_update_slice(parts, (lax.dynamic_index_in_dim(parts, lo, 0) + own_q[:T][None]), (lo, 0, 0))
        parts = lax.dynamic_update_slice(parts, (lax.dynamic_index_in_dim(parts, hi, 0) + own_q[T:][None]), (hi, 0, 0))
        gn = from_group(parts.reshape(L, D))
        gr, g1_g, b1_g = norm_back(st["resid"], g1, gn)
        gr = gr + gh
        q_g = mm_tn(st["normed"], dq).astype(BF16)
        k_g = mm_tn(st["normed_all"], dk).astype(BF16)
        v_g = mm_tn(st["value_in"], dv)
        return gr, next_source, (q_g, k_g, v_g, out_g, fc_g, proj_g), (fcb_g, g1_g, b1_g, g2_g, b2_g)

    sent, st0 = forward(0, x_in.astype(F32), None)
    sent = sent.astype(BF16).astype(F32)
    y, st1 = forward(1, sent, st0["normed_all"])
    gr1, src, big1, small1 = backward(1, st1, g_out.astype(F32), None)
    gx, _, big0, small0 = backward(0, st0, gr1, src)

    dpb, cb = bits_of("dp"), bits_of("ctx")
    dp_bits = [("dp", b) for b in range(dpb)]
    ctx_bits = [("ctx", b) for b in range(cb)]
    x_first = dp_bits + ctx_bits
    z_first = ctx_bits + dp_bits
    y_first = [("dp", b) for b in reversed(range(dpb))] + ctx_bits

    def sided(grad):
        dp = lax.axis_index("dp")
        size = lax.axis_size("dp")
        top = size // 2
        route = [(c * size + d, c * size + (d ^ top)) for c in range(2) for d in range(size) if (d >= top) != (c == 1)]
        got = lax.ppermute(grad, ("section", "dp"), route)
        total = (grad.astype(F32) + got.astype(F32)).astype(BF16)
        return scatter_sum(total, y_first[1:], skip_first=True)

    shared_half = big0[2] + big1[2]
    zero = jnp.zeros_like(shared_half)
    res = []
    for l, (q_g, k_g, v_g, out_g, fc_g, proj_g) in ((1, big1), (0, big0)):
        fc_s = scatter_sum(fc_g, x_first)
        proj_s = sided(proj_g)
        out_s = sided(out_g)
        if l == 1:
            v_use = jnp.where(first, zero, v_g)
        else:
            v_use = jnp.where(first, shared_half, v_g)
        qkv_s = scatter_sum(jnp.concatenate([q_g, k_g, v_use.astype(BF16)], axis=1), z_first)
        res.append((qkv_s, out_s, fc_s, proj_s))
    res = res[::-1]

    dp_top = lax.axis_index("dp") >= lax.axis_size("dp") // 2
    holder = jnp.where(dp_top, 1, 0) == core
    mine_l = tuple(jnp.where(first, a, b) for a, b in zip(res[0], res[1]))
    other_l = tuple(jnp.where(first, b, a) for a, b in zip(res[0], res[1]))
    got_l = tuple(swap(a) for a in other_l)

    def columns(a, b):
        left = jnp.where(first, a, b).astype(F32)
        right = jnp.where(first, b, a).astype(F32)
        return left, right

    ql, qr = columns(mine_l[0], got_l[0])
    qkv_out = jnp.concatenate([ql[:, :half], qr[:, :half], ql[:, half : 2 * half], qr[:, half : 2 * half], qr[:, 2 * half :]], axis=1)
    fc_out = jnp.concatenate(columns(mine_l[2], got_l[2]), axis=1)
    out_out = jnp.where(holder, mine_l[1], got_l[1]).astype(F32)
    proj_out = jnp.where(holder, mine_l[3], got_l[3]).astype(F32)
    shared_own = mine_l[0][:, 2 * half :]
    shared_out = jnp.where(first, shared_own, swap(shared_own)).astype(F32)

    def small_vector(parts, own):
        fcb_g, g1_g, b1_g, g2_g, b2_g = parts
        spread = lax.dynamic_update_slice(jnp.zeros((F,), F32), fcb_g, (core * FH,))
        keep = jnp.where(own, 1.0, 0.0)
        J = lax.axis_size("dp") * C
        return jnp.concatenate([spread.reshape(J, F // J)] + [(keep * v).reshape(J, D // J) for v in (g1_g, b1_g, g2_g, b2_g)], axis=1)

    vec0 = small_vector(small0, core == 0)
    vec1 = small_vector(small1, core == 1)
    vec = jnp.where(first, vec0, vec1) + swap(jnp.where(first, vec1, vec0))
    J = lax.axis_size("dp") * C
    vec = scatter_sum(vec, x_first)[0]
    fj, dj = F // J, D // J
    fcb_out = vec[:fj]
    ln = [vec[fj + i * dj : fj + (i + 1) * dj] for i in range(4)]

    end = jnp.where(first, gx, y)
    stay = jnp.where(upper, end[T:], end[:T])
    go_away = jnp.where(upper, end[:T], end[T:])
    come = lax.ppermute(go_away.astype(BF16), "ctx", reverse).astype(F32)
    block = jnp.where(upper, jnp.stack([come, stay]), jnp.stack([stay, come]))
    return (block[None], qkv_out[None], out_out[None], fc_out[None], fcb_out[None], proj_out[None], shared_out,
            ln[0][None], ln[1][None], ln[2][None], ln[3][None])


def solution(mesh):
    placed = (
        P("section", "dp", "ctx", None), P("dp", "ctx"), P("section", None), P("section", None),
        P("section", None, None), P("section", None, None), P("section", None), P("section", None),
        P("section", None, None), P("section", None), P("section", None, None), P(),
    )
    both = ("dp", "ctx")
    return jax.shard_map(
        shards, mesh=mesh, in_specs=placed,
        out_specs=(P("section", "dp", "ctx", None), P("section", both, None), P("section", both, None),
                   P("section", both, None), P("section", both), P("section", both, None), P(both, None),
                   P("section", both), P("section", both), P("section", both), P("section", both)),
        check_vma=False,
    )
```

```python
import functools

import jax
import jax.numpy as jnp
from jax import lax
from jax.experimental import pallas as pl
from jax.experimental.pallas import tpu as pltpu
from jax.sharding import PartitionSpec as P

HEAD = 64
EPSILON = 1e-05
MASKED = -1000000000.0
F32 = jnp.float32
BF16 = jnp.bfloat16
VMEM_LIMIT = 56 * 2**20


def mm(left, right):
    return jnp.dot(left, right, preferred_element_type=F32)


def mm_nt(left, right):
    return lax.dot_general(left, right, (((1,), (1,)), ((), ())), preferred_element_type=F32)


def mm_tn(left, right):
    return lax.dot_general(left, right, (((0,), (0,)), ((), ())), preferred_element_type=F32)


def norm_parts(values):
    mean = jnp.mean(values, axis=-1, keepdims=True)
    centred = values - mean
    spread = jnp.mean(centred * centred, axis=-1, keepdims=True)
    rstd = lax.rsqrt(spread + EPSILON)
    return centred * rstd, rstd


def layer_norm(values, gain, bias):
    return norm_parts(values)[0] * gain + bias


def norm_back(values, gain, grad):
    unit, rstd = norm_parts(values)
    scaled = grad * gain
    m1 = jnp.mean(scaled, axis=-1, keepdims=True)
    m2 = jnp.mean(scaled * unit, axis=-1, keepdims=True)
    return rstd * (scaled - m1 - unit * m2), jnp.sum(grad * unit, axis=0), jnp.sum(grad, axis=0)


def gelu(u):
    return 0.5 * u * (1.0 + jnp.tanh(0.7978845608028654 * (u + 0.044715 * u * u * u)))


def gelu_grad(u):
    t = jnp.tanh(0.7978845608028654 * (u + 0.044715 * u * u * u))
    return 0.5 * (1.0 + t) + 0.5 * u * (1.0 - t * t) * 0.7978845608028654 * (1.0 + 3 * 0.044715 * u * u)


def swap(x):
    return lax.ppermute(x, "section", [(0, 1), (1, 0)])


MESH = pl.DeviceIdType.MESH
HBM = pl.BlockSpec(memory_space=pl.ANY)
VM = pl.BlockSpec(memory_space=pltpu.VMEM)


class Sems:
    def __init__(self, ref):
        self.ref, self.used = ref, 0

    def one(self):
        self.used += 1
        return self.ref.at[self.used - 1]


def push(src, dst, send, recv, to):
    return pltpu.make_async_remote_copy(src_ref=src, dst_ref=dst, send_sem=send, recv_sem=recv, device_id=to,
                                        device_id_type=MESH)


def greet(peers):
    barrier = pltpu.get_barrier_semaphore()
    for peer in peers:
        pl.semaphore_signal(barrier, inc=1, device_id=peer, device_id_type=MESH)
    pl.semaphore_wait(barrier, len(peers))


def attention_block(l, blk, T, keys, pairs, q, k, v, o, lse, bias):
    rows = slice(blk * T, (blk + 1) * T)
    lane = lax.broadcasted_iota(jnp.int32, (T, 128), 1)

    def body(i, carry):
        cols = pl.ds(pl.multiple_of(i * 128, 128), 128)
        q2 = q[l, rows, cols] * jnp.asarray(HEAD**-0.5, BF16)
        k2 = k[l, :keys, cols]
        v2 = jnp.concatenate([v[l, :keys, cols], jnp.ones((keys, 128), BF16)], axis=1)
        outs, lses = [], []
        for h in range(2):
            qh = jnp.where((lane >= 64) == (h == 1), q2, jnp.zeros_like(q2))
            s = mm_nt(qh, k2) + bias[rows, :keys]
            top = jnp.max(s, axis=-1, keepdims=True)
            e = jnp.exp(s - top).astype(BF16)
            both = mm(e, v2)
            total = both[:, 128:]
            outs.append(both[:, :128] / total)
            lses.append(top + jnp.log(total))
        o[l, rows, cols] = jnp.where(lane < 64, outs[0], outs[1]).astype(BF16)
        lse[l, i, rows, :] = jnp.where(lane < 64, lses[0], lses[1])
        return carry

    lax.fori_loop(0, pairs, body, 0)


def column(row_values):
    T = row_values.shape[1]
    at = lax.broadcasted_iota(jnp.int32, (T, T), 0) == lax.broadcasted_iota(jnp.int32, (T, T), 1)
    spread = jnp.where(at, jnp.broadcast_to(row_values, (T, T)), 0).astype(F32)
    return jnp.sum(spread, axis=1, keepdims=True).astype(jnp.int32)


def forward_kernel(C, T, D, F, ends, segs, g1, b1, g2, b2, qkv, wo, fc, fcb, proj, shared,
                   xall_o, q_o, k_o, v_o, o_o, lse_o, r_o, hr_o, hh_o, up_o, act_o, y_o, gy_o, sm_o, wqk_o, wv_o, wout_o,
                   wfc_o, wproj_o, kseg_o,
                   e, seg, sm, wqk, wv, wout, wfc, wproj, xall, q, k, v, o, lse, r, hr, hh, up, act, y, bias,
                   br_s, br_r, ml_s, ml_r, dma):
    core, dp, z = lax.axis_index("section"), lax.axis_index("dp"), lax.axis_index("ctx")
    N, L, H, FH = C // 2, C * T, D // 2, F // 2
    T2 = T // 2
    row = z // N
    lo = z + row * (C - 1 - 2 * z)
    hi = C - 1 - lo
    base = row * N
    pairs = H // 128
    sems = Sems(dma)
    sib = (1 - core, dp, z)
    mirror = (core, dp, C - 1 - z)
    ahead = [(core, dp, base + lax.rem(z - base + n, N)) for n in range(1, N)]
    behind = [base + lax.rem(z - base + N - n, N) for n in range(1, N)]
    line = [(core, dp, lax.rem(z + n, C)) for n in range(1, C)]
    pos = lambda blk: lo + blk * (hi - lo)
    rows_at = lambda p: pl.ds(pl.multiple_of(p * T, T), T)
    saves = []

    def save(src, dst):
        cp = pltpu.make_async_copy(src, dst, sems.one())
        cp.start()
        saves.append(cp)

    e_load = pltpu.make_async_copy(ends.at[0, row], e.at[core, row], sems.one())
    e_load.start()
    qc = pl.ds(pl.multiple_of(core * H, 128), H)
    kc = pl.ds(pl.multiple_of(D + core * H, 128), H)
    qo = pl.ds(pl.multiple_of((1 - core) * H, 128), H)
    ko = pl.ds(pl.multiple_of(D + (1 - core) * H, 128), H)
    loads = [
        pltpu.make_async_copy(qkv.at[0, :, qc], wqk.at[core, :, pl.ds(0, H)], sems.one()),
        pltpu.make_async_copy(qkv.at[0, :, kc], wqk.at[core, :, pl.ds(H, H)], sems.one()),
        pltpu.make_async_copy(wo.at[0, pl.ds(pl.multiple_of(core * H, H), H), :], wout.at[core], sems.one()),
        pltpu.make_async_copy(fc.at[0, :, pl.ds(pl.multiple_of(core * FH, 128), FH)], wfc.at[core], sems.one()),
        pltpu.make_async_copy(proj.at[0, pl.ds(pl.multiple_of(core * FH, FH), FH), :], wproj.at[core], sems.one()),
    ]
    for cp in loads:
        cp.start()
    v_sem = sems.one()
    v_shared = pltpu.make_async_copy(shared, wv.at[0], v_sem)
    v_fresh = pltpu.make_async_copy(qkv.at[0, :, pl.ds(2 * D, H)], wv.at[1], v_sem)

    @pl.when(core == 0)
    def _():
        v_shared.start()

    @pl.when(core == 1)
    def _():
        v_fresh.start()

    seg_load = pltpu.make_async_copy(segs.at[row], seg.at[z], sems.one())
    seg_load.start()
    sm[core] = jnp.zeros_like(sm[core])
    sm[core, 0:1, :D] = g1[...]
    sm[core, 1:2, :D] = b1[...]
    sm[core, 2:3, :D] = g2[...]
    sm[core, 3:4, :D] = b2[...]
    sm[core, 4:5, :] = fcb[...]

    greet([sib] + line)

    own_s, own_r = sems.one(), sems.one()
    own_push = push(ends.at[0, row], e.at[core, row], own_s, own_r, sib)
    own_come = push(ends.at[0, row], e.at[1 - core, row], own_s, own_r, sib)
    far_s, far_r = sems.one(), sems.one()
    far_push = push(ends.at[0, 1 - row], e.at[core, row], far_s, far_r, mirror)
    far_come = push(ends.at[0, 1 - row], e.at[core, 1 - row], far_s, far_r, mirror)
    fwd_s, fwd_r = sems.one(), sems.one()
    fwd_push = push(e.at[core, 1 - row], e.at[core, 1 - row], fwd_s, fwd_r, sib)
    fwd_come = push(e.at[1 - core, 1 - row], e.at[1 - core, 1 - row], fwd_s, fwd_r, sib)

    @pl.when(core == 0)
    def _():
        far_push.start()

    own_push.start()
    sm_push = push(sm.at[core], sm.at[core], sems.one(), sems.one(), sib)
    sm_push.start()
    seg_push = []
    for n in range(1, C):
        to = lax.rem(z + n, C)
        cp = push(segs.at[to // N], seg.at[z], sems.one(), sems.one(), line[n - 1])
        cp.start()
        seg_push.append(cp)
    qk_push = [
        push(qkv.at[0, :, qo], wqk.at[core, :, pl.ds(0, H)], sems.one(), sems.one(), sib),
        push(qkv.at[0, :, ko], wqk.at[core, :, pl.ds(H, H)], sems.one(), sems.one(), sib),
    ]
    for cp in qk_push:
        cp.start()
    v_push = push(qkv.at[0, :, pl.ds(2 * D, H)], wv.at[0], sems.one(), sems.one(), sib)

    @pl.when(core == 0)
    def _():
        v_push.start()

    rest_push = [
        push(wo.at[0, pl.ds(pl.multiple_of((1 - core) * H, H), H), :], wout.at[core], sems.one(), sems.one(), sib),
        push(fc.at[0, :, pl.ds(pl.multiple_of((1 - core) * FH, 128), FH)], wfc.at[core], sems.one(), sems.one(), sib),
        push(proj.at[0, pl.ds(pl.multiple_of((1 - core) * FH, FH), FH), :], wproj.at[core], sems.one(), sems.one(), sib),
    ]

    seg_load.wait()
    for n, cp in enumerate(seg_push):
        cp.wait()
    kseg = jnp.concatenate([seg[n] for n in range(C)], axis=1)
    kseg_o[...] = kseg
    for blk in range(2):
        rows = slice(blk * T, (blk + 1) * T)
        qpos = pos(blk) * T + lax.broadcasted_iota(jnp.int32, (T, L), 0)
        kpos = lax.broadcasted_iota(jnp.int32, (T, L), 1)
        allowed = (kpos <= qpos) & (kseg == column(seg[pos(blk)]))
        bias[rows, :] = jnp.where(allowed, 0.0, MASKED)

    xh_sends = {}

    def normed_block(l, turn, blk, values):
        p = pos(blk)
        xall[l, rows_at(p), :] = layer_norm(values, sm[l, 0:1, :D], sm[l, 1:2, :D]).astype(BF16)
        for n in range(N - 1):
            part = xall.at[l, pl.ds(pl.multiple_of(p * T + core * T2, T2), T2), :]
            s, rsem = sems.one(), sems.one()
            cp = push(part, part, s, rsem, ahead[n])
            cp.start()
            src = behind[n]
            slo = src + row * (C - 1 - 2 * src)
            sp = slo + blk * (C - 1 - 2 * slo)
            got = xall.at[l, pl.ds(pl.multiple_of(sp * T + core * T2, T2), T2), :]
            other = xall.at[l, pl.ds(pl.multiple_of(sp * T + (1 - core) * T2, T2), T2), :]
            come = push(got, got, s, rsem, ahead[n])
            fs, fr = sems.one(), sems.one()
            onward = push(got, got, fs, fr, sib)
            arrive = push(other, other, fs, fr, sib)
            xh_sends[(l, turn, n)] = (cp, come, onward, arrive, sp)

    def own_products(l, blk):
        p = pos(blk)
        xh = xall[l, rows_at(p), :]
        both = mm(xh, wqk[l])
        q[l, blk * T : (blk + 1) * T, :] = both[:, :H].astype(BF16)
        k[l, rows_at(p), :] = both[:, H:].astype(BF16)

    def value_products(l, p):
        src = l * core
        v[l, rows_at(p), :] = mm(xall[src, rows_at(p), :], wv[src]).astype(BF16)

    def key_products(l, p):
        k[l, rows_at(p), :] = mm(xall[l, rows_at(p), :], wqk[l, :, H:]).astype(BF16)

    @pl.when(core == 0)
    def _():
        e_load.wait()

    @pl.when(core == 1)
    def _():
        own_come.wait_recv()

    sm_push.wait()
    blk = row
    r[0, pl.ds(pl.multiple_of(blk * T, T), T), :] = e[0, blk]
    normed_block(0, 0, blk, e[0, blk].astype(F32))

    @pl.when(core == 0)
    def _():
        loads[0].wait()
        loads[1].wait()
        v_shared.wait()

    @pl.when(core == 1)
    def _():
        for cp in qk_push:
            cp.wait_recv()
        v_push.wait_recv()

    def own_products_dynamic(l, blk):
        p = pos(blk)
        both = mm(xall[l, rows_at(p), :], wqk[l])
        q[l, pl.ds(pl.multiple_of(blk * T, T), T), :] = both[:, :H].astype(BF16)
        k[l, rows_at(p), :] = both[:, H:].astype(BF16)
        value_products(l, p)

    own_products_dynamic(0, blk)
    blk = 1 - row

    @pl.when(core == 0)
    def _():
        far_come.wait_recv()
        fwd_push.start()

    @pl.when(core == 1)
    def _():
        fwd_come.wait_recv()

    r[0, pl.ds(pl.multiple_of(blk * T, T), T), :] = e[0, blk]
    normed_block(0, 1, blk, e[0, blk].astype(F32))
    own_products_dynamic(0, blk)

    def finish_layer_inputs(l):
        for turn in range(2):
            for n in range(N - 1):
                cp, come, onward, arrive, sp = xh_sends[(l, turn, n)]
                come.wait_recv()
                onward.start()
        for turn in range(2):
            for n in range(N - 1):
                cp, come, onward, arrive, sp = xh_sends[(l, turn, n)]
                arrive.wait_recv()
                key_products(l, sp)
                value_products(l, sp)

    def middle(l):
        sends = []
        for blk in range(2):
            rows = slice(blk * T, (blk + 1) * T)
            attention_block(l, blk, T, L // 2 if blk == 0 else L, pairs, q, k, v, o, lse, bias)
            if l == 0 and blk == 0:
                @pl.when(core == 0)
                def _():
                    loads[2].wait()

                @pl.when(core == 1)
                def _():
                    rest_push[0].wait_recv()
            if l == 1 and blk == 0:
                @pl.when(core == 1)
                def _():
                    loads[2].wait()

                @pl.when(core == 0)
                def _():
                    rest_push[0].wait_recv()
            part = mm(o[l, rows, :], wout[l])
            hr[l, rows, :] = part
            br_s[l, rows, :] = part.astype(BF16)
            cp = push(br_s.at[l, rows, :], br_r.at[l, rows, :], sems.one(), sems.one(), sib)
            cp.start()
            sends.append(cp)
        save(q.at[l], q_o.at[l])
        save(k.at[l], k_o.at[l])
        save(v.at[l], v_o.at[l])
        save(o.at[l], o_o.at[l])
        save(lse.at[l], lse_o.at[l])
        save(xall.at[l], xall_o.at[l])
        mlps = []
        for blk in range(2):
            rows = slice(blk * T, (blk + 1) * T)
            sends[blk].wait_recv()
            hidden = r[l, rows, :].astype(F32) + hr[l, rows, :] + br_r[l, rows, :].astype(F32)
            hr[l, rows, :] = hidden
            normed2 = layer_norm(hidden, sm[l, 2:3, :D], sm[l, 3:4, :D]).astype(BF16)
            hh[l, rows, :] = normed2
            if blk == 0:
                local = core == l

                @pl.when(local)
                def _():
                    loads[3].wait()
                    loads[4].wait()

                @pl.when(jnp.logical_not(local))
                def _():
                    rest_push[1].wait_recv()
                    rest_push[2].wait_recv()
            mine = pl.ds(pl.multiple_of(core * FH, 128), FH)
            u = mm(normed2, wfc[l]) + sm[l, 4:5, mine]
            up[l, rows, :] = u
            a = gelu(u).astype(BF16)
            act[l, rows, :] = a
            part = mm(a, wproj[l])
            y[rows, :] = part
            ml_s[l, rows, :] = part.astype(BF16)
            cp = push(ml_s.at[l, rows, :], ml_r.at[l, rows, :], sems.one(), sems.one(), sib)
            cp.start()
            mlps.append(cp)
        save(hr.at[l], hr_o.at[l])
        save(hh.at[l], hh_o.at[l])
        save(up.at[l], up_o.at[l])
        save(act.at[l], act_o.at[l])
        for blk in range(2):
            rows = slice(blk * T, (blk + 1) * T)
            mlps[blk].wait_recv()
            out = hr[l, rows, :] + y[rows, :] + ml_r[l, rows, :].astype(F32)
            if l == 0:
                sent = out.astype(BF16)
                r[1, rows, :] = sent
                normed_block(1, blk, blk, sent.astype(F32))
                if blk == 0:
                    @pl.when(core == 1)
                    def _():
                        loads[0].wait()
                        loads[1].wait()
                        v_fresh.wait()

                    @pl.when(core == 0)
                    def _():
                        for cp in qk_push:
                            cp.wait_recv()
                own_products(1, blk)
                value_products(1, pos(blk))
            else:
                y[rows, :] = out
        return sends + mlps

    finish_layer_inputs(0)
    for cp in rest_push:
        cp.start()
    pair_sends = middle(0)

    @pl.when(core == 1)
    def _():
        far_push.start()

    finish_layer_inputs(1)
    save(r, r_o)
    pair_sends += middle(1)
    save(y, y_o)

    @pl.when(core == 1)
    def _():
        far_come.wait_recv()
        fwd_push.start()
        e_load.wait()

    @pl.when(core == 0)
    def _():
        fwd_come.wait_recv()
        own_come.wait_recv()

    save(e.at[1], gy_o)
    save(sm, sm_o)
    save(wqk, wqk_o)
    save(wv, wv_o)
    save(wout, wout_o)
    save(wfc, wfc_o)
    save(wproj, wproj_o)
    far_push.wait_send()
    fwd_push.wait_send()
    own_push.wait_send()
    for cp in qk_push + rest_push + pair_sends:
        cp.wait_send()

    @pl.when(core == 0)
    def _():
        v_push.wait_send()

    for cp, come, onward, arrive, sp in xh_sends.values():
        cp.wait_send()
        onward.wait_send()
    for cp in saves:
        cp.wait()


def forward_pass(C, ends, segs, g1, b1, g2, b2, qkv, wo, fc, fcb, proj, shared):
    T, D, F = ends.shape[2], ends.shape[3], fc.shape[2]
    N, L, H, FH = C // 2, C * T, D // 2, F // 2
    R, pairs = 2 * T, D // 256
    S = jax.ShapeDtypeStruct
    outs = [S((2, L, D), BF16), S((2, R, H), BF16), S((2, L, H), BF16), S((2, L, H), BF16), S((2, R, H), BF16),
            S((2, pairs, R, 128), F32), S((2, R, D), BF16), S((2, R, D), F32), S((2, R, D), BF16), S((2, R, FH), F32),
            S((2, R, FH), BF16), S((R, D), F32), S((2, T, D), BF16), S((2, 8, F), F32), S((2, D, D), BF16),
            S((2, D, H), BF16), S((2, H, D), BF16), S((2, D, FH), BF16), S((2, FH, D), BF16), S((1, L), jnp.int32)]
    V = pltpu.VMEM
    scratch = [V((2, 2, T, D), BF16), V((C, 1, T), jnp.int32), V((2, 8, F), F32), V((2, D, D), BF16), V((2, D, H), BF16),
               V((2, H, D), BF16), V((2, D, FH), BF16), V((2, FH, D), BF16), V((2, L, D), BF16), V((2, R, H), BF16),
               V((2, L, H), BF16), V((2, L, H), BF16), V((2, R, H), BF16), V((2, pairs, R, 128), F32), V((2, R, D), BF16),
               V((2, R, D), F32), V((2, R, D), BF16), V((2, R, FH), F32), V((2, R, FH), BF16), V((R, D), F32),
               V((R, L), F32), V((2, R, D), BF16), V((2, R, D), BF16), V((2, R, D), BF16), V((2, R, D), BF16),
               pltpu.SemaphoreType.DMA((80 + 20 * N + 2 * C,))]
    return pl.pallas_call(
        functools.partial(forward_kernel, C, T, D, F),
        in_specs=[HBM, HBM, VM, VM, VM, VM, HBM, HBM, HBM, VM, HBM, HBM],
        out_specs=[HBM] * 19 + [VM],
        out_shape=outs,
        scratch_shapes=scratch,
        compiler_params=pltpu.CompilerParams(collective_id=0, has_side_effects=True, vmem_limit_bytes=VMEM_LIMIT),
        name="forward_pass",
    )(ends, segs, g1, b1, g2, b2, qkv, wo, fc, fcb, proj, shared)


def bwd_attention_kernel(T, q_ref, k_ref, v_ref, go_ref, o_ref, lse_ref, qpos_ref, qseg_ref, kseg_ref,
                         dq_ref, dk_ref, dv_ref, bias):
    L = k_ref.shape[0]

    @pl.when(pl.program_id(0) == 0)
    def _():
        kpos = lax.broadcasted_iota(jnp.int32, (2 * T, L), 1)
        allowed = (kpos <= qpos_ref[...]) & (kseg_ref[...] == qseg_ref[...])
        bias[...] = jnp.where(allowed, 0.0, MASKED)

    lane = lax.broadcasted_iota(jnp.int32, (T, 128), 1)
    lane_k = lax.broadcasted_iota(jnp.int32, (L, 128), 1)
    scale = jnp.asarray(HEAD**-0.5, BF16)
    for part in (1, 0):
        rows = slice(part * T, (part + 1) * T)
        keys = L // 2 if part == 0 else L
        q2 = q_ref[rows, :]
        go2 = go_ref[rows, :]
        prod = go2.astype(F32) * o_ref[rows, :].astype(F32)
        lse2 = lse_ref[0, rows, :]
        dqs, dks, dvs = [], [], []
        for h in range(2):
            sel = (lane >= 64) == (h == 1)
            qh = jnp.where(sel, q2, jnp.zeros_like(q2)) * scale
            goh = jnp.where(sel, go2, jnp.zeros_like(go2))
            delta = jnp.sum(jnp.where(sel, prod, 0.0), axis=-1, keepdims=True)
            s = mm_nt(qh, k_ref[:keys, :]) + bias[rows, :keys]
            prob = jnp.exp(s - lse2[:, 64 * h : 64 * h + 1])
            gp = mm_nt(goh, v_ref[:keys, :])
            gs = (prob * (gp - delta)).astype(BF16)
            dqs.append(mm(gs, k_ref[:keys, :]))
            dks.append(mm_tn(gs, qh))
            dvs.append(mm_tn(prob.astype(BF16), goh))
        dq_ref[rows, :] = (jnp.where(lane < 64, dqs[0], dqs[1]) * HEAD**-0.5).astype(BF16)
        dk = dks[0] + dks[1]
        dv = dvs[0] + dvs[1]
        if part == 1:
            dk_ref[...] = dk
            dv_ref[...] = dv
        else:
            dk_ref[:keys, :] += dk
            dv_ref[:keys, :] += dv


def bwd_attention(q, k, v, go, o, lse, qpos, qseg, kseg):
    rows, width = q.shape
    T, L = rows // 2, k.shape[0]
    pairs = width // 128
    col = lambda n: pl.BlockSpec((n, 128), lambda i: (0, i))
    full = lambda a: pl.BlockSpec(a.shape, lambda i: (0, 0))
    return pl.pallas_call(
        functools.partial(bwd_attention_kernel, T),
        grid=(pairs,),
        in_specs=[col(rows), col(L), col(L), col(rows), col(rows), pl.BlockSpec((1, rows, 128), lambda i: (i, 0, 0)),
                  full(qpos), full(qseg), full(kseg)],
        out_specs=[col(rows), col(L), col(L)],
        out_shape=[jax.ShapeDtypeStruct((rows, width), BF16), jax.ShapeDtypeStruct((L, width), F32),
                   jax.ShapeDtypeStruct((L, width), F32)],
        scratch_shapes=[pltpu.VMEM((rows, L), F32)],
        compiler_params=pltpu.CompilerParams(vmem_limit_bytes=VMEM_LIMIT),
        name="attention_backward",
    )(q, k, v, go, o, lse, qpos, qseg, kseg)


def xor_route(size, bit):
    return [(i, i ^ (1 << bit)) for i in range(size)]


def halve(grad, axis_name, bit, at):
    mine = (lax.axis_index(axis_name) >> bit) & 1
    keep = lax.dynamic_index_in_dim(grad, mine, at, keepdims=False)
    send = lax.dynamic_index_in_dim(grad, 1 - mine, at, keepdims=False)
    got = lax.ppermute(send, axis_name, xor_route(lax.axis_size(axis_name), bit))
    return (keep.astype(F32) + got.astype(F32)).astype(grad.dtype)


def bits_of(axis_name):
    return lax.axis_size(axis_name).bit_length() - 1


def scatter_sum(grad, order, skip_first=False):
    dims = [("dp", b) for b in reversed(range(bits_of("dp")))] + [("ctx", b) for b in reversed(range(bits_of("ctx")))]
    if skip_first:
        dims = dims[1:]
    parts = len(dims)
    rows, cols = grad.shape
    grad = grad.reshape((2,) * parts + (rows >> parts, cols))
    for item in order:
        at = dims.index(item)
        grad = halve(grad, item[0], item[1], at)
        dims.pop(at)
    return grad


def shards(ends, segment_ids, ln1_gain, ln1_bias, qkv_weight, out_weight, ln2_gain, ln2_bias, fc_weight, fc_bias,
           proj_weight, shared_weight):
    core = lax.axis_index("section")
    place = lax.axis_index("ctx")
    C = lax.axis_size("ctx")
    N = C // 2
    micros, T, D = ends.shape[1:]
    L = T * C
    half = D // 2
    F = fc_weight.shape[2]
    FH = F // 2
    upper = place >= N
    row = upper.astype(jnp.int32)
    reverse = [(i, C - 1 - i) for i in range(C)]
    first = core == 0

    lo = jnp.minimum(place, C - 1 - place)
    hi = C - 1 - lo
    (xall, q, k, v, o, lse, r, hr, hh, up, act, y, gy, sm, wqk, wv, wout, wfc, wproj, kseg) = forward_pass(
        C, ends, segment_ids.reshape(micros, 1, T), ln1_gain, ln1_bias, ln2_gain, ln2_bias, qkv_weight, out_weight,
        fc_weight, fc_bias, proj_weight, shared_weight)
    seg_row = kseg.reshape(C, T)
    qseg = jnp.concatenate([lax.dynamic_index_in_dim(seg_row, lo, 0, keepdims=False),
                            lax.dynamic_index_in_dim(seg_row, hi, 0, keepdims=False)]).reshape(2 * T, 1)
    qpos = jnp.concatenate([lo * T + jnp.arange(T), hi * T + jnp.arange(T)]).astype(jnp.int32).reshape(2 * T, 1)
    g_out = gy.reshape(2 * T, D)
    reverse = [(i, C - 1 - i) for i in range(C)]

    def layer_weights(l):
        wv_l = wv[0] if l == 0 else jnp.where(first, wv[0], wv[1])
        norms = tuple(sm[l, i, :D] for i in range(4))
        return (jnp.concatenate([wqk[l], wv_l], axis=1), wout[l], wfc[l], wproj[l], norms,
                lax.dynamic_slice_in_dim(sm[l, 4], core * FH, FH, 0))

    def saved(l):
        own = jnp.concatenate([lax.dynamic_slice_in_dim(xall[l], lo * T, T, 0), lax.dynamic_slice_in_dim(xall[l], hi * T, T, 0)], 0)
        return dict(resid=r[l].astype(F32), normed=own, normed_all=xall[l], value_in=xall[0] if l == 0 else jnp.where(first, xall[0], xall[1]),
                    q=q[l], k=k[l], v=v[l], o=o[l], lse=lse[l], hidden=hr[l], normed2=hh[l], up=up[l], act=act[l])

    weights = [layer_weights(0), layer_weights(1)]
    st0, st1 = saved(0), saved(1)

    def from_group(parts):
        parts = parts.reshape(C, T, D)
        base = jnp.where(upper, N, 0)
        own = jnp.concatenate([lax.dynamic_index_in_dim(parts, lo, 0, keepdims=False),
                               lax.dynamic_index_in_dim(parts, hi, 0, keepdims=False)], 0)
        sums = None
        for k in range(1, N):
            dst = base + lax.rem(place - base + k, N)
            dlo = jnp.minimum(dst, C - 1 - dst)
            plo = lax.dynamic_index_in_dim(parts, dlo, 0, keepdims=False)
            phi = lax.dynamic_index_in_dim(parts, C - 1 - dlo, 0, keepdims=False)
            keep = jnp.where(first, plo, phi)
            give = jnp.where(first, phi, plo).astype(BF16)
            pair = (keep + swap(give).astype(F32)).astype(BF16)
            route = [(g * N + i, g * N + (i + k) % N) for g in range(2) for i in range(N)]
            come = lax.ppermute(pair, "ctx", route).astype(F32)
            sums = come if sums is None else sums + come
        zero = jnp.zeros_like(own[:T])
        extra = jnp.where(first, jnp.concatenate([sums, zero], 0), jnp.concatenate([zero, sums], 0))
        own = own + extra
        return own + swap(own.astype(BF16)).astype(F32)

    def pair_sum(x):
        return x + swap(x.astype(BF16)).astype(F32)

    def backward(l, st, grad_out, source_part):
        wqkv, wout, wfc, wproj, (g1, b1, g2, b2), fcb = weights[l]
        gm = grad_out.astype(BF16)
        gu = (gelu_grad(st["up"]) * mm_nt(gm, wproj)).astype(BF16)
        proj_g = mm_tn(st["act"], gm).astype(BF16)
        fc_g = mm_tn(st["normed2"], gu).astype(BF16)
        fcb_g = jnp.sum(gu.astype(F32), axis=0)
        gn2 = pair_sum(mm_nt(gu, wfc))
        gh, g2_g, b2_g = norm_back(st["hidden"], g2, gn2)
        gh = gh + grad_out
        gb = gh.astype(BF16)
        go = mm_nt(gb, wout).astype(BF16)
        out_g = mm_tn(st["o"], gb).astype(BF16)
        dq, dk, dv = bwd_attention(st["q"], st["k"], st["v"], go, st["o"], st["lse"], qpos, qseg, kseg)
        dk = dk.astype(BF16)
        dv = dv.astype(BF16)
        wq, wk, wv = wqkv[:, :half], wqkv[:, half : 2 * half], wqkv[:, 2 * half :]
        from_v = mm_nt(dv, wv)
        parts = mm_nt(dk, wk)
        if l == 0:
            parts = parts + from_v + source_part
            next_source = None
        else:
            parts = parts + jnp.where(first, 0.0, from_v)
            next_source = jnp.where(first, from_v, 0.0)
        own_q = mm_nt(dq, wq)
        parts = parts.reshape(C, T, D)
        parts = lax.dynamic_update_slice(parts, (lax.dynamic_index_in_dim(parts, lo, 0) + own_q[:T][None]), (lo, 0, 0))
        parts = lax.dynamic_update_slice(parts, (lax.dynamic_index_in_dim(parts, hi, 0) + own_q[T:][None]), (hi, 0, 0))
        gn = from_group(parts.reshape(L, D))
        gr, g1_g, b1_g = norm_back(st["resid"], g1, gn)
        gr = gr + gh
        q_g = mm_tn(st["normed"], dq).astype(BF16)
        k_g = mm_tn(st["normed_all"], dk).astype(BF16)
        v_g = mm_tn(st["value_in"], dv)
        return gr, next_source, (q_g, k_g, v_g, out_g, fc_g, proj_g), (fcb_g, g1_g, b1_g, g2_g, b2_g)

    gr1, src, big1, small1 = backward(1, st1, g_out.astype(F32), None)
    gx, _, big0, small0 = backward(0, st0, gr1, src)

    dpb, cb = bits_of("dp"), bits_of("ctx")
    dp_bits = [("dp", b) for b in range(dpb)]
    ctx_bits = [("ctx", b) for b in range(cb)]
    x_first = dp_bits + ctx_bits
    z_first = ctx_bits + dp_bits
    y_first = [("dp", b) for b in reversed(range(dpb))] + ctx_bits

    def sided(grad):
        dp = lax.axis_index("dp")
        size = lax.axis_size("dp")
        top = size // 2
        route = [(c * size + d, c * size + (d ^ top)) for c in range(2) for d in range(size) if (d >= top) != (c == 1)]
        got = lax.ppermute(grad, ("section", "dp"), route)
        total = (grad.astype(F32) + got.astype(F32)).astype(BF16)
        return scatter_sum(total, y_first[1:], skip_first=True)

    shared_half = big0[2] + big1[2]
    zero = jnp.zeros_like(shared_half)
    res = []
    for l, (q_g, k_g, v_g, out_g, fc_g, proj_g) in ((1, big1), (0, big0)):
        fc_s = scatter_sum(fc_g, x_first)
        proj_s = sided(proj_g)
        out_s = sided(out_g)
        if l == 1:
            v_use = jnp.where(first, zero, v_g)
        else:
            v_use = jnp.where(first, shared_half, v_g)
        qkv_s = scatter_sum(jnp.concatenate([q_g, k_g, v_use.astype(BF16)], axis=1), z_first)
        res.append((qkv_s, out_s, fc_s, proj_s))
    res = res[::-1]

    dp_top = lax.axis_index("dp") >= lax.axis_size("dp") // 2
    holder = jnp.where(dp_top, 1, 0) == core
    mine_l = tuple(jnp.where(first, a, b) for a, b in zip(res[0], res[1]))
    other_l = tuple(jnp.where(first, b, a) for a, b in zip(res[0], res[1]))
    got_l = tuple(swap(a) for a in other_l)

    def columns(a, b):
        left = jnp.where(first, a, b).astype(F32)
        right = jnp.where(first, b, a).astype(F32)
        return left, right

    ql, qr = columns(mine_l[0], got_l[0])
    qkv_out = jnp.concatenate([ql[:, :half], qr[:, :half], ql[:, half : 2 * half], qr[:, half : 2 * half], qr[:, 2 * half :]], axis=1)
    fc_out = jnp.concatenate(columns(mine_l[2], got_l[2]), axis=1)
    out_out = jnp.where(holder, mine_l[1], got_l[1]).astype(F32)
    proj_out = jnp.where(holder, mine_l[3], got_l[3]).astype(F32)
    shared_own = mine_l[0][:, 2 * half :]
    shared_out = jnp.where(first, shared_own, swap(shared_own)).astype(F32)

    def small_vector(parts, own):
        fcb_g, g1_g, b1_g, g2_g, b2_g = parts
        spread = lax.dynamic_update_slice(jnp.zeros((F,), F32), fcb_g, (core * FH,))
        keep = jnp.where(own, 1.0, 0.0)
        J = lax.axis_size("dp") * C
        return jnp.concatenate([spread.reshape(J, F // J)] + [(keep * v).reshape(J, D // J) for v in (g1_g, b1_g, g2_g, b2_g)], axis=1)

    vec0 = small_vector(small0, core == 0)
    vec1 = small_vector(small1, core == 1)
    vec = jnp.where(first, vec0, vec1) + swap(jnp.where(first, vec1, vec0))
    J = lax.axis_size("dp") * C
    vec = scatter_sum(vec, x_first)[0]
    fj, dj = F // J, D // J
    fcb_out = vec[:fj]
    ln = [vec[fj + i * dj : fj + (i + 1) * dj] for i in range(4)]

    end = jnp.where(first, gx, y)
    stay = jnp.where(upper, end[T:], end[:T])
    go_away = jnp.where(upper, end[:T], end[T:])
    come = lax.ppermute(go_away.astype(BF16), "ctx", reverse).astype(F32)
    block = jnp.where(upper, jnp.stack([come, stay]), jnp.stack([stay, come]))
    return (block[None], qkv_out[None], out_out[None], fc_out[None], fcb_out[None], proj_out[None], shared_out,
            ln[0][None], ln[1][None], ln[2][None], ln[3][None])


def solution(mesh):
    placed = (
        P("section", "dp", "ctx", None), P("dp", "ctx"), P("section", None), P("section", None),
        P("section", None, None), P("section", None, None), P("section", None), P("section", None),
        P("section", None, None), P("section", None), P("section", None, None), P(),
    )
    both = ("dp", "ctx")
    return jax.shard_map(
        shards, mesh=mesh, in_specs=placed,
        out_specs=(P("section", "dp", "ctx", None), P("section", both, None), P("section", both, None),
                   P("section", both, None), P("section", both), P("section", both, None), P(both, None),
                   P("section", both), P("section", both), P("section", both), P("section", both)),
        check_vma=False,
    )
```

```python
import functools

import jax
import jax.numpy as jnp
from jax import lax
from jax.experimental import pallas as pl
from jax.experimental.pallas import tpu as pltpu
from jax.sharding import PartitionSpec as P

HEAD = 64
SECTION, DP, CTX = "section", "dp", "ctx"
EPSILON = 1e-05
MASKED = -1000000000.0
F32 = jnp.float32
BF16 = jnp.bfloat16
VMEM_LIMIT = 63 * 2**20


def mm(left, right):
    return jnp.dot(left, right, preferred_element_type=F32)


def mm_nt(left, right):
    return lax.dot_general(left, right, (((1,), (1,)), ((), ())), preferred_element_type=F32)


def mm_tn(left, right):
    return lax.dot_general(left, right, (((0,), (0,)), ((), ())), preferred_element_type=F32)


def unit_norm(values):
    mean = jnp.mean(values, axis=-1, keepdims=True)
    centred = values - mean
    rstd = lax.rsqrt(jnp.mean(centred * centred, axis=-1, keepdims=True) + EPSILON)
    return centred * rstd, rstd


def layer_norm(values, gain, bias):
    return unit_norm(values)[0] * gain + bias


def gelu_both(u):
    t = jnp.tanh(0.7978845608028654 * (u + 0.044715 * u * u * u))
    half = 0.5 * (1.0 + t)
    return u * half, half + 0.5 * u * (1.0 - t * t) * (0.7978845608028654 + 3 * 0.044715 * 0.7978845608028654 * u * u)


def swap(x):
    return lax.ppermute(x, SECTION, [(0, 1), (1, 0)])


MESH = pl.DeviceIdType.MESH
HBM = pl.BlockSpec(memory_space=pl.ANY)
VM = pl.BlockSpec(memory_space=pltpu.VMEM)


class Sems:
    def __init__(self, ref):
        self.ref, self.used = ref, 0

    def one(self):
        self.used += 1
        return self.ref.at[self.used - 1]


def push(src, dst, send, recv, to):
    return pltpu.make_async_remote_copy(src_ref=src, dst_ref=dst, send_sem=send, recv_sem=recv, device_id=to,
                                        device_id_type=MESH)


def greet(peers):
    barrier = pltpu.get_barrier_semaphore()
    for peer in peers:
        pl.semaphore_signal(barrier, inc=1, device_id=peer, device_id_type=MESH)
    pl.semaphore_wait(barrier, len(peers))


def attention_block(l, blk, T, keys, pairs, q, k, v, o, lse, bias):
    rows = slice(blk * T, (blk + 1) * T)
    lane = lax.broadcasted_iota(jnp.int32, (T, 128), 1)

    def body(i, carry):
        cols = pl.ds(pl.multiple_of(i * 128, 128), 128)
        q2 = q[l, rows, cols] * jnp.asarray(HEAD**-0.5, BF16)
        k2 = k[l, :keys, cols]
        v2 = jnp.concatenate([v[l, :keys, cols], jnp.ones((keys, 128), BF16)], axis=1)
        outs, lses = [], []
        for h in range(2):
            qh = jnp.where((lane >= 64) == (h == 1), q2, jnp.zeros_like(q2))
            s = mm_nt(qh, k2) + bias[rows, :keys]
            top = jnp.max(s, axis=-1, keepdims=True)
            e = jnp.exp(s - top).astype(BF16)
            both = mm(e, v2)
            total = both[:, 128:]
            outs.append(both[:, :128] / total)
            lses.append(top + jnp.log(total))
        o[l, rows, cols] = jnp.where(lane < 64, outs[0], outs[1]).astype(BF16)
        lse[l, i, rows, :] = jnp.where(lane < 64, lses[0], lses[1])
        return carry

    lax.fori_loop(0, pairs, body, 0)


def column(row_values):
    T = row_values.shape[1]
    at = lax.broadcasted_iota(jnp.int32, (T, T), 0) == lax.broadcasted_iota(jnp.int32, (T, T), 1)
    spread = jnp.where(at, jnp.broadcast_to(row_values, (T, T)), 0).astype(F32)
    return jnp.sum(spread, axis=1, keepdims=True).astype(jnp.int32)


def forward_kernel(C, T, D, F, ends, segs, g1, b1, g2, b2, qkv, wo, fc, fcb, proj, shared,
                   xall_o, q_o, k_o, v_o, o_o, lse_o, r_o, hr_o, hh_o, gp_o, act_o, y_o, yb_o, gy_o, sm_o, watt_o, wfc_o, wproj_o,
                   kseg_o,
                   e, seg, sm, wqk, wv, wout, wfc, wproj, xall, q, k, v, o, lse, r, hr, hh, gp, act, y, yb, wvt, bias,
                   br_s, br_r, ml_s, ml_r, dma):
    core, dp, z = lax.axis_index(SECTION), lax.axis_index(DP), lax.axis_index(CTX)
    N, L, H, FH = C // 2, C * T, D // 2, F // 2
    T2 = T // 2
    row = z // N
    lo = z + row * (C - 1 - 2 * z)
    hi = C - 1 - lo
    base = row * N
    pairs = H // 128
    sems = Sems(dma)
    sib = (1 - core, dp, z)
    mirror = (core, dp, C - 1 - z)
    ahead = [(core, dp, base + lax.rem(z - base + n, N)) for n in range(1, N)]
    behind = [base + lax.rem(z - base + N - n, N) for n in range(1, N)]
    line = [(core, dp, lax.rem(z + n, C)) for n in range(1, C)]
    pos = lambda blk: lo + blk * (hi - lo)
    rows_at = lambda p: pl.ds(pl.multiple_of(p * T, T), T)
    saves = []

    def save(src, dst):
        cp = pltpu.make_async_copy(src, dst, sems.one())
        cp.start()
        saves.append(cp)

    e_load = pltpu.make_async_copy(ends.at[0, row], e.at[core, row], sems.one())
    e_load.start()
    qc = pl.ds(pl.multiple_of(core * H, 128), H)
    kc = pl.ds(pl.multiple_of(D + core * H, 128), H)
    qo = pl.ds(pl.multiple_of((1 - core) * H, 128), H)
    ko = pl.ds(pl.multiple_of(D + (1 - core) * H, 128), H)
    loads = [
        pltpu.make_async_copy(qkv.at[0, :, qc], wqk.at[core, :, pl.ds(0, H)], sems.one()),
        pltpu.make_async_copy(qkv.at[0, :, kc], wqk.at[core, :, pl.ds(H, H)], sems.one()),
        pltpu.make_async_copy(wo.at[0, pl.ds(pl.multiple_of(core * H, H), H), :], wout.at[core], sems.one()),
        pltpu.make_async_copy(fc.at[0, :, pl.ds(pl.multiple_of(core * FH, 128), FH)], wfc.at[core], sems.one()),
        pltpu.make_async_copy(proj.at[0, pl.ds(pl.multiple_of(core * FH, FH), FH), :], wproj.at[core], sems.one()),
    ]
    for cp in loads:
        cp.start()
    v_sem = sems.one()
    v_shared = pltpu.make_async_copy(shared, wv.at[0], v_sem)
    v_fresh = pltpu.make_async_copy(qkv.at[0, :, pl.ds(2 * D, H)], wv.at[1], v_sem)

    @pl.when(core == 0)
    def _():
        v_shared.start()

    @pl.when(core == 1)
    def _():
        v_fresh.start()

    seg_load = pltpu.make_async_copy(segs.at[row], seg.at[z], sems.one())
    seg_load.start()
    sm[core] = jnp.zeros_like(sm[core])
    sm[core, 0:1, :D] = g1[...]
    sm[core, 1:2, :D] = b1[...]
    sm[core, 2:3, :D] = g2[...]
    sm[core, 3:4, :D] = b2[...]
    sm[core, 4:5, :] = fcb[...]

    greet([sib] + line)

    own_s, own_r = sems.one(), sems.one()
    own_push = push(ends.at[0, row], e.at[core, row], own_s, own_r, sib)
    own_come = push(ends.at[0, row], e.at[1 - core, row], own_s, own_r, sib)
    far_s, far_r = sems.one(), sems.one()
    far_push = push(ends.at[0, 1 - row], e.at[core, row], far_s, far_r, mirror)
    far_come = push(ends.at[0, 1 - row], e.at[core, 1 - row], far_s, far_r, mirror)
    fwd_s, fwd_r = sems.one(), sems.one()
    fwd_push = push(e.at[core, 1 - row], e.at[core, 1 - row], fwd_s, fwd_r, sib)
    fwd_come = push(e.at[1 - core, 1 - row], e.at[1 - core, 1 - row], fwd_s, fwd_r, sib)

    @pl.when(core == 0)
    def _():
        far_push.start()

    own_push.start()
    sm_push = push(sm.at[core], sm.at[core], sems.one(), sems.one(), sib)
    sm_push.start()
    seg_push = []
    for n in range(1, C):
        to = lax.rem(z + n, C)
        cp = push(segs.at[to // N], seg.at[z], sems.one(), sems.one(), line[n - 1])
        cp.start()
        seg_push.append(cp)
    qk_push = [
        push(qkv.at[0, :, qo], wqk.at[core, :, pl.ds(0, H)], sems.one(), sems.one(), sib),
        push(qkv.at[0, :, ko], wqk.at[core, :, pl.ds(H, H)], sems.one(), sems.one(), sib),
    ]
    for cp in qk_push:
        cp.start()
    v_push = push(qkv.at[0, :, pl.ds(2 * D, H)], wv.at[0], sems.one(), sems.one(), sib)

    @pl.when(core == 0)
    def _():
        v_push.start()

    rest_push = [
        push(wo.at[0, pl.ds(pl.multiple_of((1 - core) * H, H), H), :], wout.at[core], sems.one(), sems.one(), sib),
        push(fc.at[0, :, pl.ds(pl.multiple_of((1 - core) * FH, 128), FH)], wfc.at[core], sems.one(), sems.one(), sib),
        push(proj.at[0, pl.ds(pl.multiple_of((1 - core) * FH, FH), FH), :], wproj.at[core], sems.one(), sems.one(), sib),
    ]

    seg_load.wait()
    for n, cp in enumerate(seg_push):
        cp.wait()
    kseg = jnp.concatenate([seg[n] for n in range(C)], axis=1)
    kseg_o[...] = kseg
    for blk in range(2):
        rows = slice(blk * T, (blk + 1) * T)
        qpos = pos(blk) * T + lax.broadcasted_iota(jnp.int32, (T, L), 0)
        kpos = lax.broadcasted_iota(jnp.int32, (T, L), 1)
        allowed = (kpos <= qpos) & (kseg == column(seg[pos(blk)]))
        bias[rows, :] = jnp.where(allowed, 0.0, MASKED)

    xh_sends = {}

    def normed_block(l, turn, blk, values):
        p = pos(blk)
        xall[l, rows_at(p), :] = layer_norm(values, sm[l, 0:1, :D], sm[l, 1:2, :D]).astype(BF16)
        for n in range(N - 1):
            part = xall.at[l, pl.ds(pl.multiple_of(p * T + core * T2, T2), T2), :]
            s, rsem = sems.one(), sems.one()
            cp = push(part, part, s, rsem, ahead[n])
            cp.start()
            src = behind[n]
            slo = src + row * (C - 1 - 2 * src)
            sp = slo + blk * (C - 1 - 2 * slo)
            got = xall.at[l, pl.ds(pl.multiple_of(sp * T + core * T2, T2), T2), :]
            other = xall.at[l, pl.ds(pl.multiple_of(sp * T + (1 - core) * T2, T2), T2), :]
            come = push(got, got, s, rsem, ahead[n])
            fs, fr = sems.one(), sems.one()
            onward = push(got, got, fs, fr, sib)
            arrive = push(other, other, fs, fr, sib)
            xh_sends[(l, turn, n)] = (cp, come, onward, arrive, sp)

    def own_products(l, blk):
        p = pos(blk)
        xh = xall[l, rows_at(p), :]
        both = mm(xh, wqk[l])
        q[l, blk * T : (blk + 1) * T, :] = both[:, :H].astype(BF16)
        k[l, rows_at(p), :] = both[:, H:].astype(BF16)

    def value_products(l, p):
        src = l * core
        v[l, rows_at(p), :] = mm(xall[src, rows_at(p), :], wv[src]).astype(BF16)

    def key_products(l, p):
        k[l, rows_at(p), :] = mm(xall[l, rows_at(p), :], wqk[l, :, H:]).astype(BF16)

    @pl.when(core == 0)
    def _():
        e_load.wait()

    @pl.when(core == 1)
    def _():
        own_come.wait_recv()

    sm_push.wait()
    blk = row
    r[0, pl.ds(pl.multiple_of(blk * T, T), T), :] = e[0, blk]
    normed_block(0, 0, blk, e[0, blk].astype(F32))

    @pl.when(core == 0)
    def _():
        loads[0].wait()
        loads[1].wait()
        v_shared.wait()

    @pl.when(core == 1)
    def _():
        for cp in qk_push:
            cp.wait_recv()
        v_push.wait_recv()

    def own_products_dynamic(l, blk):
        p = pos(blk)
        both = mm(xall[l, rows_at(p), :], wqk[l])
        q[l, pl.ds(pl.multiple_of(blk * T, T), T), :] = both[:, :H].astype(BF16)
        k[l, rows_at(p), :] = both[:, H:].astype(BF16)
        value_products(l, p)

    own_products_dynamic(0, blk)
    blk = 1 - row

    @pl.when(core == 0)
    def _():
        far_come.wait_recv()
        fwd_push.start()

    @pl.when(core == 1)
    def _():
        fwd_come.wait_recv()

    r[0, pl.ds(pl.multiple_of(blk * T, T), T), :] = e[0, blk]
    normed_block(0, 1, blk, e[0, blk].astype(F32))
    own_products_dynamic(0, blk)

    def finish_layer_inputs(l):
        for turn in range(2):
            for n in range(N - 1):
                cp, come, onward, arrive, sp = xh_sends[(l, turn, n)]
                come.wait_recv()
                onward.start()
        for turn in range(2):
            for n in range(N - 1):
                cp, come, onward, arrive, sp = xh_sends[(l, turn, n)]
                arrive.wait_recv()
                key_products(l, sp)
                value_products(l, sp)

    def middle(l):
        sends = []
        for blk in range(2):
            rows = slice(blk * T, (blk + 1) * T)
            attention_block(l, blk, T, L // 2 if blk == 0 else L, pairs, q, k, v, o, lse, bias)
            if l == 0 and blk == 0:
                @pl.when(core == 0)
                def _():
                    loads[2].wait()

                @pl.when(core == 1)
                def _():
                    rest_push[0].wait_recv()
            if l == 1 and blk == 0:
                @pl.when(core == 1)
                def _():
                    loads[2].wait()

                @pl.when(core == 0)
                def _():
                    rest_push[0].wait_recv()
            part = mm(o[l, rows, :], wout[l])
            hr[l, rows, :] = part
            br_s[l, rows, :] = part.astype(BF16)
            cp = push(br_s.at[l, rows, :], br_r.at[l, rows, :], sems.one(), sems.one(), sib)
            cp.start()
            sends.append(cp)
        save(q.at[l], q_o.at[l])
        save(k.at[l], k_o.at[l])
        save(v.at[l], v_o.at[l])
        save(o.at[l], o_o.at[l])
        save(lse.at[l], lse_o.at[l])
        save(xall.at[l], xall_o.at[l])
        mlps = []
        for blk in range(2):
            rows = slice(blk * T, (blk + 1) * T)
            sends[blk].wait_recv()
            hidden = r[l, rows, :].astype(F32) + hr[l, rows, :] + br_r[l, rows, :].astype(F32)
            hr[l, rows, :] = hidden
            normed2 = layer_norm(hidden, sm[l, 2:3, :D], sm[l, 3:4, :D]).astype(BF16)
            hh[l, rows, :] = normed2
            if blk == 0:
                local = core == l

                @pl.when(local)
                def _():
                    loads[3].wait()
                    loads[4].wait()

                @pl.when(jnp.logical_not(local))
                def _():
                    rest_push[1].wait_recv()
                    rest_push[2].wait_recv()
            mine = pl.ds(pl.multiple_of(core * FH, 128), FH)
            u = mm(normed2, wfc[l]) + sm[l, 4:5, mine]
            a, slope = gelu_both(u)
            a = a.astype(BF16)
            gp[l, rows, :] = slope.astype(BF16)
            act[l, rows, :] = a
            part = mm(a, wproj[l])
            y[rows, :] = part
            ml_s[l, rows, :] = part.astype(BF16)
            cp = push(ml_s.at[l, rows, :], ml_r.at[l, rows, :], sems.one(), sems.one(), sib)
            cp.start()
            mlps.append(cp)
        save(hr.at[l], hr_o.at[l])
        save(hh.at[l], hh_o.at[l])
        save(gp.at[l], gp_o.at[l])
        save(act.at[l], act_o.at[l])
        for blk in range(2):
            rows = slice(blk * T, (blk + 1) * T)
            mlps[blk].wait_recv()
            out = hr[l, rows, :] + y[rows, :] + ml_r[l, rows, :].astype(F32)
            if l == 0:
                sent = out.astype(BF16)
                r[1, rows, :] = sent
                normed_block(1, blk, blk, sent.astype(F32))
                if blk == 0:
                    @pl.when(core == 1)
                    def _():
                        loads[0].wait()
                        loads[1].wait()
                        v_fresh.wait()

                    @pl.when(core == 0)
                    def _():
                        for cp in qk_push:
                            cp.wait_recv()
                own_products(1, blk)
                value_products(1, pos(blk))
            else:
                y[rows, :] = out
                yb[rows, :] = out.astype(BF16)
        return sends + mlps

    finish_layer_inputs(0)
    for cp in rest_push:
        cp.start()
    pair_sends = middle(0)

    @pl.when(core == 1)
    def _():
        far_push.start()

    finish_layer_inputs(1)
    save(r, r_o)
    pair_sends += middle(1)
    save(y, y_o)
    save(yb, yb_o)

    @pl.when(core == 1)
    def _():
        far_come.wait_recv()
        fwd_push.start()
        e_load.wait()

    @pl.when(core == 0)
    def _():
        fwd_come.wait_recv()
        own_come.wait_recv()

    save(e.at[1], gy_o)
    save(sm, sm_o)
    for l in range(2):
        wvt[l] = jnp.transpose(wv[l * core])
        save(wqk.at[l], watt_o.at[l, pl.ds(0, D)])
        save(wout.at[l], watt_o.at[l, pl.ds(D, H)])
        save(wvt.at[l], watt_o.at[l, pl.ds(D + H, H)])
    save(wfc, wfc_o)
    save(wproj, wproj_o)
    far_push.wait_send()
    fwd_push.wait_send()
    own_push.wait_send()
    for cp in qk_push + rest_push + pair_sends:
        cp.wait_send()

    @pl.when(core == 0)
    def _():
        v_push.wait_send()

    for cp, come, onward, arrive, sp in xh_sends.values():
        cp.wait_send()
        onward.wait_send()
    for cp in saves:
        cp.wait()


def forward_pass(C, ends, segs, g1, b1, g2, b2, qkv, wo, fc, fcb, proj, shared):
    T, D, F = ends.shape[2], ends.shape[3], fc.shape[2]
    N, L, H, FH = C // 2, C * T, D // 2, F // 2
    R, pairs = 2 * T, D // 256
    S = jax.ShapeDtypeStruct
    outs = [S((2, L, D), BF16), S((2, R, H), BF16), S((2, L, H), BF16), S((2, L, H), BF16), S((2, R, H), BF16),
            S((2, pairs, R, 128), F32), S((2, R, D), BF16), S((2, R, D), F32), S((2, R, D), BF16), S((2, R, FH), BF16),
            S((2, R, FH), BF16), S((R, D), F32), S((R, D), BF16), S((2, T, D), BF16), S((2, 8, F), F32), S((2, 2 * D, D), BF16),
            S((2, D, FH), BF16), S((2, FH, D), BF16), S((1, L), jnp.int32)]
    V = pltpu.VMEM
    scratch = [V((2, 2, T, D), BF16), V((C, 1, T), jnp.int32), V((2, 8, F), F32), V((2, D, D), BF16), V((2, D, H), BF16),
               V((2, H, D), BF16), V((2, D, FH), BF16), V((2, FH, D), BF16), V((2, L, D), BF16), V((2, R, H), BF16),
               V((2, L, H), BF16), V((2, L, H), BF16), V((2, R, H), BF16), V((2, pairs, R, 128), F32), V((2, R, D), BF16),
               V((2, R, D), F32), V((2, R, D), BF16), V((2, R, FH), BF16), V((2, R, FH), BF16), V((R, D), F32),
               V((R, D), BF16), V((2, H, D), BF16), V((R, L), F32), V((2, R, D), BF16), V((2, R, D), BF16), V((2, R, D), BF16), V((2, R, D), BF16),
               pltpu.SemaphoreType.DMA((80 + 20 * N + 2 * C,))]
    return pl.pallas_call(
        functools.partial(forward_kernel, C, T, D, F),
        in_specs=[HBM, HBM, VM, VM, VM, VM, HBM, HBM, HBM, VM, HBM, HBM],
        out_specs=[HBM] * 18 + [VM],
        out_shape=outs,
        scratch_shapes=scratch,
        compiler_params=pltpu.CompilerParams(collective_id=0, has_side_effects=True, vmem_limit_bytes=VMEM_LIMIT),
        name="forward_pass",
    )(ends, segs, g1, b1, g2, b2, qkv, wo, fc, fcb, proj, shared)


class Job:
    def __init__(self, env, buf, lead, cols, order, sided, land, credits, first_layer, active, earlier):
        self.env, self.buf, self.lead, self.cols = env, buf, lead, cols
        self.sided, self.land, self.credits, self.first_layer, self.active = sided, land, credits, first_layer, active
        self.earlier = earlier
        self.bits = list(range(env.m - 2 if sided else env.m - 1, -1, -1))
        self.fixed, self.z_done, self.steps, self.at = {}, False, [], 0
        self.used = 0
        if sided:
            self.steps.append(("side", None, None))
        for item in order:
            if item == "z":
                for s in range(1, env.C):
                    self.steps.append(("z", s, dict(self.fixed)))
                self.z_done = True
            else:
                self.steps.append(("bit", item, (dict(self.fixed), self.z_done)))
                self.fixed[item] = env.bit(item)
        self.plans = [self.plan(i) for i in range(len(self.steps))]

    def view(self, fixed, zat):
        at = tuple(self.lead) + tuple(fixed.get(b, slice(None)) for b in self.bits)
        return at + (slice(None) if zat is None else zat, slice(None), self.cols)

    def plan(self, i):
        env = self.env
        kind, what, state = self.steps[i]
        moves = []
        if kind == "side":
            other = env.dp_xor(env.m - 1)
            moves.append((env.bit(env.m - 1) != env.core, self.view({}, None), other, env.bit(env.m - 1) == env.core,
                          self.view({}, None), other))
            return [self.bind(move, self.land[i]) for move in moves]
        active = self.active if not self.sided else (env.bit(env.m - 1) == env.core)
        if kind == "bit":
            fixed, z_done = state
            zat = env.z if z_done else None
            other = env.dp_xor(what)
            mine = env.bit(what)
            moves.append((active, self.view({**fixed, what: 1 - mine}, zat), other, active,
                          self.view({**fixed, what: mine}, zat), other))
            return [self.bind(move, self.land[i]) for move in moves]
        s, C, z = what, env.C, env.z
        zm = C - 1 - z
        for side, (p, sign) in enumerate(((z, 1), (zm, -1))):
            out_at = z + sign * (C - s)
            in_at = z + sign * (C - s - 1)
            moves.append((both(active, p < s), self.view(state, out_at), env.line(z + sign),
                          both(active, both(p >= 1, p <= s)), self.view(state, in_at), env.line(z - sign)))
        return [self.bind(move, self.land[i].at[side]) for side, move in enumerate(moves)]

    def bind(self, move, slot):
        send_if, src, to, recv_if, dst, source = move
        env = self.env
        sem_s, sem_r = env.sems.one(), env.sems.one()
        credit = self.credits.at[self.used]
        self.used += 1
        return send_if, src, to, recv_if, dst, source, slot, sem_s, sem_r, credit

    def send(self, i):
        for send_if, src, to, recv_if, dst, source, slot, sem_s, sem_r, credit in self.plans[i]:
            cp = push(self.buf.at[src], slot, sem_s, sem_r, to)

            def go(cp=cp, credit=credit):
                if not self.first_layer:
                    when(self.earlier, lambda: pl.semaphore_wait(credit, 1))
                cp.start()

            when(send_if, go)
            self.env.sent.append((send_if, cp))

    def take(self, i):
        for send_if, src, to, recv_if, dst, source, slot, sem_s, sem_r, credit in self.plans[i]:
            cp = push(slot, slot, sem_s, sem_r, to)

            def got(cp=cp, dst=dst, slot=slot, credit=credit, source=source):
                cp.wait_recv()
                self.buf[dst] = self.buf[dst] + slot[...]
                if self.first_layer:
                    pl.semaphore_signal(credit, inc=1, device_id=source, device_id_type=MESH)

            when(recv_if, got)

    def start(self):
        self.send(0)

    def advance(self):
        if self.at >= len(self.steps):
            return
        self.take(self.at)
        self.at += 1
        if self.at < len(self.steps):
            self.send(self.at)

    def own(self):
        return self.view(self.fixed, self.env.z)


def both(a, b):
    if a is True:
        return b
    if b is True:
        return a
    return jnp.logical_and(a, b)


def when(condition, fn):
    if condition is True:
        fn()
    else:
        pl.when(condition)(fn)


class Env:
    def __init__(self, C, m, core, dp, z, sems):
        self.C, self.m, self.core, self.dp, self.z, self.sems, self.sent = C, m, core, dp, z, sems, []

    def bit(self, b):
        return lax.rem(lax.div(self.dp, 1 << b), 2)

    def dp_xor(self, b):
        return (self.core, self.dp + (1 << b) * (1 - 2 * self.bit(b)), self.z)

    def line(self, z):
        return (self.core, self.dp, z)


def job_table(m):
    xs, ys = list(range(m)), list(range(m - 1, -1, -1))
    rest = list(range(m - 1))
    return {
        "P0": ("gproj", (0, 3), rest + ["z"], True), "P1": ("gproj", (1, 3), rest + ["z"], True),
        "P2": ("gproj", (2, 3), rest + ["z"], True),
        "F0": ("gfc", (0, 3), xs + ["z"], False), "F1": ("gfc", (1, 3), xs + ["z"], False),
        "F2": ("gfc", (2, 3), ["z"] + xs, False),
        "O": ("gout", (0, 1), rest + ["z"], True),
        "Q": ("gq", (0, 1), xs + ["z"], False), "K": ("gk", (0, 1), ["z"] + xs, False),
        "V": ("gv", (0, 1), ys + ["z"], False),
    }


def grad_shapes(C, m, D, F):
    H, FH, J = D // 2, F // 2, C << m
    full, side = (2,) * m + (C,), (2,) * (m - 1) + (C,)
    return {"gproj": side + (F // J, D), "gfc": full + (D // J, FH), "gout": side + (D // J, D),
            "gq": full + (D // J, H), "gk": full + (D // J, H), "gv": full + (D // J, H)}


def landing_shapes(C, m, D, F):
    shapes = grad_shapes(C, m, D, F)
    result = {}
    for name, (buf, (at, parts), order, sided) in job_table(m).items():
        shape = list(shapes[buf])
        shape[-1] //= parts
        n = m - 1 if sided else m
        lead = {b: 2 for b in range(n)}
        tail = [shape[-2], shape[-1]]
        zdim = [C]
        steps = []
        if sided:
            steps.append(tuple([2] * n + zdim + tail))
        for item in order:
            if item == "z":
                zdim = []
                for s in range(1, C):
                    steps.append(tuple([2] + [2] * len(lead) + tail))
            else:
                lead.pop(item)
                steps.append(tuple([2] * len(lead) + zdim + tail))
        result[name] = steps
    return result


def norm_grad(values, gain, grad):
    unit, rstd = unit_norm(values)
    scaled = grad * gain
    m1 = jnp.mean(scaled, axis=-1, keepdims=True)
    m2 = jnp.mean(scaled * unit, axis=-1, keepdims=True)
    back = rstd * (scaled - m1 - unit * m2)
    return back, jnp.sum(grad * unit, axis=0, keepdims=True), jnp.sum(grad, axis=0, keepdims=True)


def attention_back_pair(i, T, L, q, k, v, o, lse, goa, bias, dq, dk, dv, dv_at):
    cols = slice(i * 128, (i + 1) * 128)
    lane = lax.broadcasted_iota(jnp.int32, (T, 128), 1)
    scale = jnp.asarray(HEAD**-0.5, BF16)
    totals = None
    for blk in (1, 0):
        rows = slice(blk * T, (blk + 1) * T)
        keys = L if blk else L // 2
        q2, go2 = q[rows, cols] * scale, goa[rows, cols]
        prod = go2.astype(F32) * o[rows, cols].astype(F32)
        k2, v2 = k[:keys, cols], v[:keys, cols]
        dqs, dks, dvs = [], None, None
        for h in range(2):
            sel = (lane >= 64) == (h == 1)
            qh = jnp.where(sel, q2, jnp.zeros_like(q2))
            goh = jnp.where(sel, go2, jnp.zeros_like(go2))
            delta = jnp.sum(jnp.where(sel, prod, 0.0), axis=-1, keepdims=True)
            s = mm_nt(qh, k2) + bias[rows, :keys]
            prob = jnp.exp(s - lse[i, rows, 64 * h : 64 * h + 1])
            gp = mm_nt(goh, v2)
            gs = (prob * (gp - delta)).astype(BF16)
            dqs.append(mm(gs, k2))
            one_k = mm_tn(gs, qh)
            one_v = mm_tn(prob.astype(BF16), goh)
            dks = one_k if dks is None else dks + one_k
            dvs = one_v if dvs is None else dvs + one_v
        dq[rows, cols] = (jnp.where(lane < 64, dqs[0], dqs[1]) * HEAD**-0.5).astype(BF16)
        if blk:
            totals = (dks, dvs)
        else:
            dk[:keys, cols] = (totals[0][:keys] + dks).astype(BF16)
            dk[keys:, cols] = totals[0][keys:].astype(BF16)
            dv[dv_at, :keys, cols] = (totals[1][:keys] + dvs).astype(BF16)
            dv[dv_at, keys:, cols] = totals[1][keys:].astype(BF16)


LOADED = ("gp", "act", "hh", "hr", "o", "q", "k", "v", "lse", "xall", "r")


def backward_kernel(C, m, T, D, F, fused, names_in, *refs):
    n_in = len(names_in)
    hbm = dict(zip(names_in, refs[:n_in]))
    outs, (vm, dma, credits) = refs[n_in:-3], refs[-3:]
    ends_o, small_o = outs[:2]
    core, dp, z = lax.axis_index(SECTION), lax.axis_index(DP), lax.axis_index(CTX)
    N, L, H, FH = C // 2, C * T, D // 2, F // 2
    row = lax.div(z, N)
    lo = z + row * (C - 1 - 2 * z)
    hi = C - 1 - lo
    base = row * N
    pairs = H // 128
    sems = Sems(dma)
    env = Env(C, m, core, dp, z, sems)
    sib = (1 - core, dp, z)
    mirror = (core, dp, C - 1 - z)
    pos = lambda blk: lo + blk * (hi - lo)
    block = lambda at: pl.ds(pl.multiple_of(at * T, T), T)
    other_nodes = [base + lax.rem(z - base + n, N) for n in range(1, N)]
    sent = env.sent
    loads = {}

    def load(name, l, src=None, dst=None):
        cp = pltpu.make_async_copy(hbm[name].at[l] if src is None else src, vm[name] if dst is None else dst, sems.one())
        cp.start()
        loads[(name, l)] = cp

    def need(*names):
        for name in names:
            loads[name].wait()

    def pushed(src, dst, to, condition=True, until=sent):
        cp = push(src, dst, sems.one(), sems.one(), to)
        when(condition, cp.start)
        until.append((condition, cp))
        return cp

    load("gy", 1, hbm["gy"].at[0], vm["gm"].at[slice(0, T)])
    load("gy", 0, hbm["gy"].at[1], vm["gm"].at[slice(T, 2 * T)])
    load("wproj", 1, dst=vm["wa"])
    load("gp", 1)
    load("wfc", 1)
    load("act", 1)
    load("hh", 1)
    load("hr", 1)
    load("sm", 0, hbm["sm"], vm["sm"])
    for name in ("o", "q", "k", "v", "lse", "xall", "r"):
        load(name, 1)
    y_keep = pltpu.make_async_copy(hbm["y"].at[block(row)], ends_o.at[0, row], sems.one())
    when(core == 1, y_keep.start)

    kseg = hbm["kseg"]
    for blk in range(2):
        rows = slice(blk * T, (blk + 1) * T)
        qpos = pos(blk) * T + lax.broadcasted_iota(jnp.int32, (T, L), 0)
        kpos = lax.broadcasted_iota(jnp.int32, (T, L), 1)
        mine = kseg[0:1, 0:T]
        for n in range(1, C):
            mine = jnp.where(pos(blk) == n, kseg[0:1, n * T : (n + 1) * T], mine)
        allowed = (kpos <= qpos) & (kseg[...] == column(mine))
        vm["bias"][rows, :] = jnp.where(allowed, 0.0, MASKED)

    greet([sib] + [env.line(lax.rem(z + n, C)) for n in range(1, C)] + [env.dp_xor(b) for b in range(m)])

    y_push = pushed(hbm["yb"].at[block(1 - row)], vm["far"], mirror, core == 1)

    table = job_table(m)
    jobs = {}

    def start(name, l):
        if not fused:
            return
        buf, (at, parts), order, sided = table[name]
        width = vm[buf].shape[-1] // parts
        earlier = True if name != "V" else core == 1
        active = True if l == 0 else earlier
        jobs[(name, l)] = Job(env, vm[buf], (l,), slice(at * width, (at + 1) * width), order, sided, vm["land"][name],
                              credits[name], l == 1, active, earlier)
        jobs[(name, l)].start()

    def adv(l, *names):
        if not fused:
            return
        for name in names:
            jobs[(name, l)].advance()

    gm, gp, go, ghh, wa, wfc = vm["gm"], vm["gp"], vm["go"], vm["ghh"], vm["wa"], vm["wfc"]
    sm, sg = vm["sm"], vm["sg"]

    def put(buf, l, cols, value):
        shape = vm[buf].shape[1:-1] + (value.shape[-1],)
        vm[buf][(l,) + (slice(None),) * (len(shape) - 1) + (cols,)] = value.astype(BF16).reshape(shape)

    def layer_back(l, poll):
        again = []
        need(("wproj", l), ("gp", l))
        bias_sum = None
        for blk in range(2):
            rows = slice(blk * T, (blk + 1) * T)
            if l == 1:
                need(("gy", 1 - blk))
                go[rows, :] = gm[rows, :].astype(F32)
            gu = (gp[rows, :].astype(F32) * mm_nt(gm[rows, :], wa[...])).astype(BF16)
            gp[rows, :] = gu
            part = jnp.sum(gu.astype(F32), axis=0, keepdims=True)
            bias_sum = part if bias_sum is None else bias_sum + part
        sg[l, 4:5, :] = bias_sum
        load("watt", l, dst=wa)
        need(("wfc", l))
        shares = []
        for blk in range(2):
            rows = slice(blk * T, (blk + 1) * T)
            part = mm_nt(gp[rows, :], wfc[...])
            ghh[rows, :] = part
            vm["a_s"][rows, :] = part.astype(BF16)
            shares.append(pushed(vm["a_s"].at[rows, :], vm["a_r"].at[rows, :], sib, until=again))
        if l == 1:
            load("wfc", 0)
        poll("up")
        need(("act", l))
        third = D // 3
        for i in range(3):
            cols = slice(i * third, (i + 1) * third)
            put("gproj", l, cols, mm_tn(vm["act"][...], gm[:, cols]))
            start("P%d" % i, l)
        poll("proj")
        if l == 1:
            load("act", 0)
        need(("hh", l))
        third = FH // 3
        for i in (2, 0, 1):
            cols = slice(i * third, (i + 1) * third)
            put("gfc", l, cols, mm_tn(vm["hh"][...], gp[:, cols]))
            start("F%d" % i, l)
        poll("fc")
        if l == 1:
            load("hh", 0)
            load("gp", 0)
        need(("hr", l), ("watt", l))
        if l == 1:
            need(("sm", 0))
        sums = None
        for blk in range(2):
            rows = slice(blk * T, (blk + 1) * T)
            shares[blk].wait_recv()
            grad = ghh[rows, :] + vm["a_r"][rows, :].astype(F32)
            back, gain_sum, bias_sum = norm_grad(vm["hr"][rows, :], sm[l, 2:3, :D], grad)
            total = go[rows, :] + back
            go[rows, :] = total
            low = total.astype(BF16)
            gm[rows, :] = low
            vm["goa"][rows, :] = mm_nt(low, wa[D : D + H, :]).astype(BF16)
            sums = (gain_sum, bias_sum) if sums is None else (sums[0] + gain_sum, sums[1] + bias_sum)
        sg[l, 2:3, :D] = sums[0]
        sg[l, 3:4, :D] = sums[1]
        if l == 1:
            load("hr", 0)
        need(("o", l))
        put("gout", l, slice(0, D), mm_tn(vm["o"][...], gm[...]))
        start("O", l)
        poll("norm")
        need(("q", l), ("k", l), ("v", l), ("lse", l))
        for i in range(pairs):
            attention_back_pair(i, T, L, vm["q"], vm["k"], vm["v"], vm["o"], vm["lse"], vm["goa"], vm["bias"], vm["dq"],
                                vm["dk"], vm["dv"], l)
            poll("pair%d" % i)
        if l == 1:
            for name in ("o", "q", "k", "v", "lse"):
                load(name, 0)
        else:
            def merge():
                vm["dv"][0] = (vm["dv"][0].astype(F32) + vm["dv"][1].astype(F32)).astype(BF16)

            when(core == 0, merge)
        dk, dv, dq = vm["dk"], vm["dv"], vm["dq"]

        def key_part(at):
            part_v = dv[l, block(at), :]
            if l == 1:
                part_v = jnp.where(core == 1, part_v, jnp.zeros_like(part_v))
            return mm_nt(dk[block(at), :], wa[:D, H:]) + mm(part_v, wa[D + H :, :])

        crossing, gives = [], []
        for n, node in enumerate(other_nodes):
            dlo = node + row * (C - 1 - 2 * node)
            dhi = C - 1 - dlo
            vm["fs_s"][n] = key_part(dlo + (1 - core) * (dhi - dlo)).astype(BF16)
            gives.append(pushed(vm["fs_s"].at[n], vm["fs_r"].at[n], sib, until=again))
        for n, node in enumerate(other_nodes):
            dlo = node + row * (C - 1 - 2 * node)
            keep = key_part(dlo + core * (C - 1 - 2 * dlo))
            gives[n].wait_recv()
            vm["fx_s"][l, n] = (keep + vm["fs_r"][n].astype(F32)).astype(BF16)
            crossing.append(pushed(vm["fx_s"].at[l, n], vm["fx_r"].at[l, n], (core, dp, node)))
        poll("cross")
        for blk in range(2):
            rows = slice(blk * T, (blk + 1) * T)
            ghh[rows, :] = key_part(pos(blk)) + mm_nt(dq[rows, :], wa[:D, :H])
        early = pl.ds(pl.multiple_of((1 - core) * T, T), T)
        late = pl.ds(pl.multiple_of(core * T, T), T)
        vm["b_s"][early, :] = ghh[early, :].astype(BF16)
        shares = [pushed(vm["b_s"].at[early, :], vm["b_r"].at[early, :], sib, until=again)]
        if l == 1:
            load("wproj", 0, dst=wa)
        need(("xall", l))
        xall = vm["xall"]
        put("gk", l, slice(0, H), mm_tn(xall[...], dk[...]))
        start("K", l)
        put("gq", l, slice(0, H), mm_tn(xall[block(lo), :], dq[:T, :]) + mm_tn(xall[block(hi), :], dq[T:, :]))
        start("Q", l)
        put("gv", l, slice(0, H), mm_tn(xall[...], dv[l]))
        start("V", l)
        poll("qkv")
        if l == 1:
            load("xall", 0)
        need(("r", l))
        for n in range(N - 1):
            crossing[n].wait_recv()
            ghh[late, :] += vm["fx_r"][l, n].astype(F32)
        vm["b_s"][late, :] = ghh[late, :].astype(BF16)
        shares.append(pushed(vm["b_s"].at[late, :], vm["b_r"].at[late, :], sib, until=again))
        for cp in shares:
            cp.wait_recv()
        sums = None
        for blk in range(2):
            rows = slice(blk * T, (blk + 1) * T)
            grad = ghh[rows, :] + vm["b_r"][rows, :].astype(F32)
            back, gain_sum, bias_sum = norm_grad(vm["r"][rows, :].astype(F32), sm[l, 0:1, :D], grad)
            total = go[rows, :] + back
            go[rows, :] = total
            if l == 1:
                gm[rows, :] = total.astype(BF16)
            sums = (gain_sum, bias_sum) if sums is None else (sums[0] + gain_sum, sums[1] + bias_sum)
        sg[l, 0:1, :D] = sums[0]
        sg[l, 1:2, :D] = sums[1]
        if l == 1:
            load("r", 0)
        for condition, cp in again:
            when(condition, cp.wait_send)

    def poll_first(where):
        plan = {
            "norm": ["F2"], "pair0": ["F2"], "pair2": ["F2"], "cross": ["F0", "F1", "F2"], "qkv": ["F2"],
        }
        adv(1, *plan.get(where, []))

    def poll_second(where):
        plan = {
            "up": ["P0", "P1", "P2", "K", "F0", "F1"],
            "proj": ["F0", "F1", "K", "O"],
            "fc": ["F0", "F1", "K", "Q", "V", "P0", "P1", "P2"],
            "norm": ["F0", "F1", "K", "Q", "V", "O"],
            "pair0": ["P0", "P1", "P2", "K", "Q", "V", "O"],
            "pair1": ["P0", "P1", "P2", "Q", "V", "O"],
            "pair2": ["P0", "P1", "P2", "Q", "V", "O"],
        }
        adv(1, *plan.get(where, []))
        if where in ("pair0", "pair1", "pair2"):
            adv(0, "F2")
        if where == "cross":
            adv(0, "F0", "F1", "F2")
        if where == "qkv":
            adv(0, "F2", "F0", "F1")

    layer_back(1, poll_first)
    layer_back(0, poll_second)

    keep = pl.ds(pl.multiple_of(row * T, T), T)
    away = pl.ds(pl.multiple_of((1 - row) * T, T), T)
    vm["far_s"][...] = go[away, :].astype(BF16)
    x_push = pushed(vm["far_s"], vm["far"], mirror, core == 0)
    x_keep = pltpu.make_async_copy(go.at[keep, :], ends_o.at[0, row], sems.one())
    when(core == 0, x_keep.start)

    sv, sv_r = vm["sv"], vm["sv_r"]
    sv[0] = jnp.zeros_like(sv[0])
    sv[0, 0:4, :] = sg[core, 0:4, :]
    sv[0, 4:5, :] = sg[0, 4:5, :]
    sv[0, 5:6, :] = sg[1, 4:5, :]
    around = [env.dp_xor(b) for b in range(m)]
    b = 1
    while b < C:
        around.append(env.line(z + b * (1 - 2 * lax.rem(lax.div(z, b), 2))))
        b *= 2
    small_at = [0]
    small_cp = [pushed(sv.at[0], sv_r.at[0], around[0])]

    def small_step():
        i = small_at[0]
        small_cp[0].wait_recv()
        sv[i + 1] = sv[i] + sv_r[i]
        small_at[0] += 1
        if i + 1 < len(around):
            small_cp[0] = pushed(sv.at[i + 1], sv_r.at[i + 1], around[i + 1])

    def finish_ends():
        when(core == 0, x_push.wait_recv)
        when(core == 1, y_push.wait_recv)
        vm["far_f"][...] = vm["far"][...].astype(F32)
        far_keep = pltpu.make_async_copy(vm["far_f"], ends_o.at[0, 1 - row], sems.one())
        far_keep.start()
        far_keep.wait()
        when(core == 0, x_keep.wait)
        when(core == 1, y_keep.wait)

    if fused:
        for name in ("P0", "F0", "P1", "F1", "P2", "F2", "K", "O", "Q", "V"):
            for _ in range(len(jobs[(name, 1)].steps)):
                adv(1, name)
        order = ["F0", "F1", "F2", "K", "P0", "P1", "P2", "Q", "O", "V"]
        while any(jobs[(name, 0)].at < len(jobs[(name, 0)].steps) for name in order):
            adv(0, *order)
            if small_at[0] < len(around):
                small_step()
    while small_at[0] < len(around):
        small_step()
    last = len(around)
    small_o[...] = sv[last]

    if fused:
        hand_over(core, sib, env, vm, jobs, m, D, H, FH, pushed, sv, last, outs)
    else:
        leave = []
        for name, out in zip(("gproj", "gfc", "gout", "gq", "gk", "gv"), outs[2:]):
            leave.append(pltpu.make_async_copy(vm[name], out, sems.one()))
            leave[-1].start()
        for cp in leave:
            cp.wait()
    finish_ends()
    for condition, cp in sent:
        when(condition, cp.wait_send)


def hand_over(core, sib, env, vm, jobs, m, D, H, FH, pushed, sv, last, outs):
    small_o, qkv_o, out_o, fc_o, proj_o, shared_o = outs[1:]
    vm["fb_s"][...] = jnp.where(core == 0, sv[last, 5:6, :], sv[last, 4:5, :])
    fin = vm["fin"]
    top = env.bit(m - 1) == core
    own = lambda name, l: (l,) + jobs[(name, 0)].own()[1:]
    arrive = [
        pushed(vm["gfc"].at[own("F0", 1 - core)[:-1]], fin["fc"], sib),
        pushed(vm["gq"].at[own("Q", 1 - core)], fin["q"], sib),
        pushed(vm["gk"].at[own("K", 1 - core)], fin["k"], sib),
        pushed(vm["gv"].at[own("V", 0)], fin["v"], sib),
        pushed(vm["fb_s"], fin["fb"], sib),
    ]
    out_push = pushed(vm["gout"].at[own("O", 1 - core)], fin["out"], sib, top)
    proj_push = pushed(vm["gproj"].at[own("P0", 1 - core)[:-1]], fin["proj"], sib, top)

    here = pl.ds(pl.multiple_of(core * H, 128), H)
    there = pl.ds(pl.multiple_of((1 - core) * H, 128), H)
    here_k = pl.ds(pl.multiple_of(D + core * H, 128), H)
    there_k = pl.ds(pl.multiple_of(D + (1 - core) * H, 128), H)
    qkv_o[0, :, here] = vm["gq"][own("Q", core)].astype(F32)
    qkv_o[0, :, here_k] = vm["gk"][own("K", core)].astype(F32)
    fc_o[0, :, pl.ds(pl.multiple_of(core * FH, 128), FH)] = vm["gfc"][own("F0", core)[:-1]].astype(F32)

    def top_out():
        out_o[0] = vm["gout"][own("O", core)].astype(F32)
        proj_o[0] = vm["gproj"][own("P0", core)[:-1]].astype(F32)

    when(top, top_out)
    for cp in arrive:
        cp.wait_recv()

    def other_out():
        out_push.wait_recv()
        proj_push.wait_recv()
        out_o[0] = fin["out"][...].astype(F32)
        proj_o[0] = fin["proj"][...].astype(F32)

    when(jnp.logical_not(top), other_out)
    qkv_o[0, :, there] = fin["q"][...].astype(F32)
    qkv_o[0, :, there_k] = fin["k"][...].astype(F32)
    fc_o[0, :, pl.ds(pl.multiple_of((1 - core) * FH, 128), FH)] = fin["fc"][...].astype(F32)
    fresh = pl.ds(2 * D, H)

    def fresh_first():
        qkv_o[0, :, fresh] = fin["v"][...].astype(F32)
        shared_o[...] = vm["gv"][own("V", 0)].astype(F32)

    def fresh_second():
        qkv_o[0, :, fresh] = vm["gv"][own("V", 1)].astype(F32)
        shared_o[...] = fin["v"][...].astype(F32)

    when(core == 0, fresh_first)
    when(core == 1, fresh_second)
    small_o[6:7, :] = fin["fb"][...]


def backward_pass(C, m, T, D, F, inputs):
    N, L, H, FH, R, J = C // 2, C * T, D // 2, F // 2, 2 * T, C << m
    fused = (D // J) % 16 == 0 and (F // J) % 16 == 0 and m > 0
    pairs = H // 128
    S, V = jax.ShapeDtypeStruct, pltpu.VMEM
    names = tuple(inputs)
    outs = [S((1, 2, T, D), F32), S((8, FH), F32)]
    flat = {"gproj": (FH, D), "gfc": (D, FH), "gout": (H, D), "gq": (D, H), "gk": (D, H), "gv": (D, H)}
    if fused:
        outs += [S((1, D // J, 5 * H), F32), S((1, D // J, D), F32), S((1, D // J, F), F32), S((1, F // J, D), F32),
                 S((D // J, H), F32)]
        grads = grad_shapes(C, m, D, F)
        land = {name: [V(shape, BF16) for shape in steps] for name, steps in landing_shapes(C, m, D, F).items()}
    else:
        outs += [S((2,) + shape, BF16) for shape in flat.values()]
        grads, land = flat, {}
    stages = m + C.bit_length() - 1
    vm = dict(
        gm=V((R, D), BF16), gp=V((R, FH), BF16), act=V((R, FH), BF16), hh=V((R, D), BF16), hr=V((R, D), F32),
        o=V((R, H), BF16), q=V((R, H), BF16), k=V((L, H), BF16), v=V((L, H), BF16), lse=V((pairs, R, 128), F32),
        xall=V((L, D), BF16), r=V((R, D), BF16), sm=V((2, 8, F), F32), sg=V((2, 8, FH), F32), bias=V((R, L), F32),
        wa=V((2 * D, D), BF16), wfc=V((D, FH), BF16), go=V((R, D), F32), ghh=V((R, D), F32), a_s=V((R, D), BF16),
        a_r=V((R, D), BF16), b_s=V((R, D), BF16), b_r=V((R, D), BF16), goa=V((R, H), BF16), dq=V((R, H), BF16),
        dk=V((L, H), BF16), dv=V((2, L, H), BF16), fs_s=V((N - 1, T, D), BF16), fs_r=V((N - 1, T, D), BF16),
        fx_s=V((2, N - 1, T, D), BF16), fx_r=V((2, N - 1, T, D), BF16), far=V((T, D), BF16), far_s=V((T, D), BF16),
        far_f=V((T, D), F32), sv=V((stages + 1, 8, FH), F32), sv_r=V((stages, 8, FH), F32), fb_s=V((1, FH), F32),
        fin=dict(fc=V((D // J, FH), BF16), q=V((D // J, H), BF16), k=V((D // J, H), BF16), v=V((D // J, H), BF16),
                 out=V((D // J, D), BF16), proj=V((F // J, D), BF16), fb=V((1, FH), F32)),
        land=land, **{name: V((2,) + shape, BF16) for name, shape in grads.items()})
    moves = 1 + m + 2 * (C - 1)
    credits = {name: pltpu.SemaphoreType.REGULAR((moves,)) for name in job_table(m)} if fused else {}
    in_specs = [VM if name == "kseg" else HBM for name in names]
    return pl.pallas_call(
        functools.partial(backward_kernel, C, m, T, D, F, fused, names),
        in_specs=in_specs,
        out_specs=[HBM, VM] + [VM if fused else HBM] * (len(outs) - 2),
        out_shape=outs,
        scratch_shapes=[vm, pltpu.SemaphoreType.DMA((120 + 40 * moves,)), credits],
        compiler_params=pltpu.CompilerParams(collective_id=1, has_side_effects=True, vmem_limit_bytes=VMEM_LIMIT),
        name="backward_pass",
    )(*inputs.values())


def xor_route(size, bit):
    return [(i, i ^ (1 << bit)) for i in range(size)]


def halve(grad, axis_name, bit, at):
    mine = (lax.axis_index(axis_name) >> bit) & 1
    keep = lax.dynamic_index_in_dim(grad, mine, at, keepdims=False)
    send = lax.dynamic_index_in_dim(grad, 1 - mine, at, keepdims=False)
    got = lax.ppermute(send, axis_name, xor_route(lax.axis_size(axis_name), bit))
    return (keep.astype(F32) + got.astype(F32)).astype(grad.dtype)


def bits_of(axis_name):
    return lax.axis_size(axis_name).bit_length() - 1


def scatter_sum(grad, order, skip_first=False):
    dims = [(DP, b) for b in reversed(range(bits_of(DP)))] + [(CTX, b) for b in reversed(range(bits_of(CTX)))]
    if skip_first:
        dims = dims[1:]
    parts = len(dims)
    rows, cols = grad.shape
    grad = grad.reshape((2,) * parts + (rows >> parts, cols))
    for item in order:
        at = dims.index(item)
        grad = halve(grad, item[0], item[1], at)
        dims.pop(at)
    return grad


def shards(ends, segment_ids, ln1_gain, ln1_bias, qkv_weight, out_weight, ln2_gain, ln2_bias, fc_weight, fc_bias,
           proj_weight, shared_weight):
    core = lax.axis_index(SECTION)
    first = core == 0
    C, m = lax.axis_size(CTX), bits_of(DP)
    J = C << m
    micros, T, D = ends.shape[1:]
    F = fc_weight.shape[2]
    half, FH = D // 2, F // 2
    names = ("xall", "q", "k", "v", "o", "lse", "r", "hr", "hh", "gp", "act", "y", "yb", "gy", "sm", "watt", "wfc", "wproj", "kseg")
    kept = dict(zip(names, forward_pass(
        C, ends, segment_ids.reshape(micros, 1, T), ln1_gain, ln1_bias, ln2_gain, ln2_bias, qkv_weight, out_weight,
        fc_weight, fc_bias, proj_weight, shared_weight)))
    block, small, *grads = backward_pass(C, m, T, D, F, kept)
    if len(grads) == 5:
        qkv_out, out_out, fc_out, proj_out, shared_out = grads
        other_bias = small[6]
    else:
        qkv_out, out_out, fc_out, proj_out, shared_out = scattered(grads, core, m, half)
        other_bias = swap(jnp.where(first, small[5], small[4]))
    own_bias = jnp.where(first, small[4], small[5])
    bias_grad = jnp.concatenate([jnp.where(first, own_bias, other_bias), jnp.where(first, other_bias, own_bias)])
    j = lax.axis_index(DP) * C + lax.axis_index(CTX)
    fcb_out = lax.dynamic_slice_in_dim(bias_grad, j * (F // J), F // J, 0)
    ln = lax.dynamic_slice_in_dim(small[:4], j * (D // J), D // J, 1)
    return (block, qkv_out, out_out, fc_out, fcb_out[None], proj_out, shared_out, ln[0:1], ln[1:2], ln[2:3], ln[3:4])


def scattered(grads, core, m, half):
    gproj, gfc, gout, gq, gk, gv = grads
    first = core == 0
    x_first = [(DP, b) for b in range(m)] + [(CTX, b) for b in range(bits_of(CTX))]
    y_first = [(DP, b) for b in reversed(range(m))] + x_first[m:]

    def sided(grad):
        dp, size = lax.axis_index(DP), lax.axis_size(DP)
        top = size // 2
        route = [(c * size + d, c * size + (d ^ top)) for c in range(2) for d in range(size) if (d >= top) != (c == 1)]
        got = lax.ppermute(grad, (SECTION, DP), route)
        return scatter_sum((grad.astype(F32) + got.astype(F32)).astype(BF16), y_first[1:], skip_first=True)

    res = []
    for l in range(2):
        qkv = jnp.concatenate([gq[l], gk[l], gv[l]], axis=1)
        res.append((scatter_sum(qkv, x_first), sided(gout[l]), scatter_sum(gfc[l], x_first), sided(gproj[l])))
    holder = jnp.where(lax.axis_index(DP) >= lax.axis_size(DP) // 2, 1, 0) == core
    mine = tuple(jnp.where(first, a, b) for a, b in zip(res[0], res[1]))
    got = tuple(swap(jnp.where(first, b, a)) for a, b in zip(res[0], res[1]))
    left, right = [jnp.where(first, a, b).astype(F32) for a, b in zip(mine, got)], [jnp.where(first, b, a).astype(F32) for a, b in zip(mine, got)]
    fresh0 = res[0][0][:, 2 * half :]
    fresh0_other = swap(fresh0)
    fresh = jnp.where(first, fresh0_other, res[1][0][:, 2 * half :]).astype(F32)
    qkv_out = jnp.concatenate([left[0][:, :half], right[0][:, :half], left[0][:, half : 2 * half], right[0][:, half : 2 * half], fresh], axis=1)
    fc_out = jnp.concatenate([left[2], right[2]], axis=1)
    out_out = jnp.where(holder, mine[1], got[1]).astype(F32)
    proj_out = jnp.where(holder, mine[3], got[3]).astype(F32)
    shared_out = jnp.where(first, fresh0, fresh0_other).astype(F32)
    return qkv_out[None], out_out[None], fc_out[None], proj_out[None], shared_out


def solution(mesh):
    placed = (
        P(SECTION, DP, CTX, None), P(DP, CTX), P(SECTION, None), P(SECTION, None),
        P(SECTION, None, None), P(SECTION, None, None), P(SECTION, None), P(SECTION, None),
        P(SECTION, None, None), P(SECTION, None), P(SECTION, None, None), P(),
    )
    both = (DP, CTX)
    return jax.shard_map(
        shards, mesh=mesh, in_specs=placed,
        out_specs=(P(SECTION, DP, CTX, None), P(SECTION, both, None), P(SECTION, both, None),
                   P(SECTION, both, None), P(SECTION, both), P(SECTION, both, None), P(both, None),
                   P(SECTION, both), P(SECTION, both), P(SECTION, both), P(SECTION, both)),
        check_vma=False,
    )
```

```python
import functools

import jax
import jax.numpy as jnp
from jax import lax
from jax.experimental import pallas as pl
from jax.experimental.pallas import tpu as pltpu
from jax.sharding import PartitionSpec as P

HEAD = 64
SECTION, DP, CTX = "section", "dp", "ctx"
EPSILON = 1e-05
MASKED = -1000000000.0
F32 = jnp.float32
BF16 = jnp.bfloat16
VMEM_LIMIT = 127 * 2**19


def mm(left, right):
    return jnp.dot(left, right, preferred_element_type=F32)


def mm_nt(left, right):
    return lax.dot_general(left, right, (((1,), (1,)), ((), ())), preferred_element_type=F32)


def mm_tn(left, right):
    return lax.dot_general(left, right, (((0,), (0,)), ((), ())), preferred_element_type=F32)


def unit_norm(values):
    mean = jnp.mean(values, axis=-1, keepdims=True)
    centred = values - mean
    rstd = lax.rsqrt(jnp.mean(centred * centred, axis=-1, keepdims=True) + EPSILON)
    return centred * rstd, rstd


def layer_norm(values, gain, bias):
    return unit_norm(values)[0] * gain + bias


def gelu_both(u):
    t = jnp.tanh(0.7978845608028654 * (u + 0.044715 * u * u * u))
    half = 0.5 * (1.0 + t)
    return u * half, half + 0.5 * u * (1.0 - t * t) * (0.7978845608028654 + 3 * 0.044715 * 0.7978845608028654 * u * u)


def swap(x):
    return lax.ppermute(x, SECTION, [(0, 1), (1, 0)])


MESH = pl.DeviceIdType.MESH
HBM = pl.BlockSpec(memory_space=pl.ANY)
VM = pl.BlockSpec(memory_space=pltpu.VMEM)


class Sems:
    def __init__(self, ref):
        self.ref, self.used = ref, 0

    def one(self):
        self.used += 1
        return self.ref.at[self.used - 1]


def push(src, dst, send, recv, to):
    return pltpu.make_async_remote_copy(src_ref=src, dst_ref=dst, send_sem=send, recv_sem=recv, device_id=to,
                                        device_id_type=MESH)


def greet(peers):
    barrier = pltpu.get_barrier_semaphore()
    for peer in peers:
        pl.semaphore_signal(barrier, inc=1, device_id=peer, device_id_type=MESH)
    pl.semaphore_wait(barrier, len(peers))


def attention_block(l, blk, T, keys, pairs, q, k, v, o, lse, bias):
    rows = slice(blk * T, (blk + 1) * T)
    lane = lax.broadcasted_iota(jnp.int32, (T, 128), 1)

    def body(i, carry):
        cols = pl.ds(pl.multiple_of(i * 128, 128), 128)
        q2 = q[l, rows, cols] * jnp.asarray(HEAD**-0.5, BF16)
        k2 = k[l, :keys, cols]
        v2 = jnp.concatenate([v[l, :keys, cols], jnp.ones((keys, 128), BF16)], axis=1)
        outs, lses = [], []
        for h in range(2):
            qh = jnp.where((lane >= 64) == (h == 1), q2, jnp.zeros_like(q2))
            s = mm_nt(qh, k2) + bias[rows, :keys]
            top = jnp.max(s, axis=-1, keepdims=True)
            e = jnp.exp(s - top).astype(BF16)
            both = mm(e, v2)
            total = both[:, 128:]
            outs.append(both[:, :128] / total)
            lses.append(top + jnp.log(total))
        o[l, rows, cols] = jnp.where(lane < 64, outs[0], outs[1]).astype(BF16)
        old = jnp.where(lane == 2 * i, lses[0], lse[l, rows, :])
        lse[l, rows, :] = jnp.where(lane == 2 * i + 1, lses[1], old)
        return carry

    lax.fori_loop(0, pairs, body, 0)


def column(row_values):
    T = row_values.shape[1]
    at = lax.broadcasted_iota(jnp.int32, (T, T), 0) == lax.broadcasted_iota(jnp.int32, (T, T), 1)
    spread = jnp.where(at, jnp.broadcast_to(row_values, (T, T)), 0).astype(F32)
    return jnp.sum(spread, axis=1, keepdims=True).astype(jnp.int32)


def forward_kernel(C, m, T, D, F, ends, segs, g1, b1, g2, b2, qkv, wo, fc, fcb, proj, shared,
                   xall_o, q_o, k_o, v_o, o_o, lse_o, r_o, hr_o, hh_o, gp_o, act_o, y_o, yb_o, gy_o, sm_o, watt_o, wfc_o, wproj_o,
                   act_in_o, gm_in_o, kseg_o,
                   e, seg, sm, wqk, wv, wout, wfc, wproj, xall, q, k, v, o, lse, r, hr, hh, gp, act, y, yb, wvt, bias,
                   br_s, br_r, ml_s, ml_r, dma):
    core, dp, z = lax.axis_index(SECTION), lax.axis_index(DP), lax.axis_index(CTX)
    N, L, H, FH = C // 2, C * T, D // 2, F // 2
    T2 = T // 2
    row = z // N
    lo = z + row * (C - 1 - 2 * z)
    hi = C - 1 - lo
    base = row * N
    pairs = H // 128
    sems = Sems(dma)
    sib = (1 - core, dp, z)
    mirror = (core, dp, C - 1 - z)
    top_bit = lax.div(dp, 1 << (m - 1))
    across = (core, dp + (1 - 2 * top_bit) * (1 << (m - 1)), z)
    owner = top_bit == core
    ahead = [(core, dp, base + lax.rem(z - base + n, N)) for n in range(1, N)]
    behind = [base + lax.rem(z - base + N - n, N) for n in range(1, N)]
    line = [(core, dp, lax.rem(z + n, C)) for n in range(1, C)]
    pos = lambda blk: lo + blk * (hi - lo)
    rows_at = lambda p: pl.ds(pl.multiple_of(p * T, T), T)
    saves = []

    def save(src, dst):
        cp = pltpu.make_async_copy(src, dst, sems.one())
        cp.start()
        saves.append(cp)

    e_load = pltpu.make_async_copy(ends.at[0, row], e.at[core, row], sems.one())
    e_load.start()
    qc = pl.ds(pl.multiple_of(core * H, 128), H)
    kc = pl.ds(pl.multiple_of(D + core * H, 128), H)
    qo = pl.ds(pl.multiple_of((1 - core) * H, 128), H)
    ko = pl.ds(pl.multiple_of(D + (1 - core) * H, 128), H)
    loads = [
        pltpu.make_async_copy(qkv.at[0, :, qc], wqk.at[core, :, pl.ds(0, H)], sems.one()),
        pltpu.make_async_copy(qkv.at[0, :, kc], wqk.at[core, :, pl.ds(H, H)], sems.one()),
        pltpu.make_async_copy(wo.at[0, pl.ds(pl.multiple_of(core * H, H), H), :], wout.at[core], sems.one()),
        pltpu.make_async_copy(fc.at[0, :, pl.ds(pl.multiple_of(core * FH, 128), FH)], wfc.at[core], sems.one()),
        pltpu.make_async_copy(proj.at[0, pl.ds(pl.multiple_of(core * FH, FH), FH), :], wproj.at[core], sems.one()),
    ]
    for cp in loads:
        cp.start()
    v_sem = sems.one()
    v_shared = pltpu.make_async_copy(shared, wv.at[0], v_sem)
    v_fresh = pltpu.make_async_copy(qkv.at[0, :, pl.ds(2 * D, H)], wv.at[1], v_sem)

    @pl.when(core == 0)
    def _():
        v_shared.start()

    @pl.when(core == 1)
    def _():
        v_fresh.start()

    seg_load = pltpu.make_async_copy(segs.at[row], seg.at[z], sems.one())
    seg_load.start()
    sm[core] = jnp.zeros_like(sm[core])
    sm[core, 0:1, :D] = g1[...]
    sm[core, 1:2, :D] = b1[...]
    sm[core, 2:3, :D] = g2[...]
    sm[core, 3:4, :D] = b2[...]
    sm[core, 4:5, :] = fcb[...]

    greet([sib, across] + line)

    own_s, own_r = sems.one(), sems.one()
    own_push = push(ends.at[0, row], e.at[core, row], own_s, own_r, sib)
    own_come = push(ends.at[0, row], e.at[1 - core, row], own_s, own_r, sib)
    far_s, far_r = sems.one(), sems.one()
    far_push = push(ends.at[0, 1 - row], e.at[core, row], far_s, far_r, mirror)
    far_come = push(ends.at[0, 1 - row], e.at[core, 1 - row], far_s, far_r, mirror)
    fwd_s, fwd_r = sems.one(), sems.one()
    fwd_push = push(e.at[core, 1 - row], e.at[core, 1 - row], fwd_s, fwd_r, sib)
    fwd_come = push(e.at[1 - core, 1 - row], e.at[1 - core, 1 - row], fwd_s, fwd_r, sib)

    @pl.when(core == 0)
    def _():
        far_push.start()

    own_push.start()
    sm_push = push(sm.at[core], sm.at[core], sems.one(), sems.one(), sib)
    sm_push.start()
    seg_push = []
    for n in range(1, C):
        to = lax.rem(z + n, C)
        cp = push(segs.at[to // N], seg.at[z], sems.one(), sems.one(), line[n - 1])
        cp.start()
        seg_push.append(cp)
    qk_push = [
        push(qkv.at[0, :, qo], wqk.at[core, :, pl.ds(0, H)], sems.one(), sems.one(), sib),
        push(qkv.at[0, :, ko], wqk.at[core, :, pl.ds(H, H)], sems.one(), sems.one(), sib),
    ]
    for cp in qk_push:
        cp.start()
    v_push = push(qkv.at[0, :, pl.ds(2 * D, H)], wv.at[0], sems.one(), sems.one(), sib)

    @pl.when(core == 0)
    def _():
        v_push.start()

    rest_push = [
        push(wo.at[0, pl.ds(pl.multiple_of((1 - core) * H, H), H), :], wout.at[core], sems.one(), sems.one(), sib),
        push(fc.at[0, :, pl.ds(pl.multiple_of((1 - core) * FH, 128), FH)], wfc.at[core], sems.one(), sems.one(), sib),
        push(proj.at[0, pl.ds(pl.multiple_of((1 - core) * FH, FH), FH), :], wproj.at[core], sems.one(), sems.one(), sib),
    ]

    seg_load.wait()
    for n, cp in enumerate(seg_push):
        cp.wait()
    kseg = jnp.concatenate([seg[n] for n in range(C)], axis=1)
    kseg_o[...] = kseg
    for blk in range(2):
        rows = slice(blk * T, (blk + 1) * T)
        qpos = pos(blk) * T + lax.broadcasted_iota(jnp.int32, (T, L), 0)
        kpos = lax.broadcasted_iota(jnp.int32, (T, L), 1)
        allowed = (kpos <= qpos) & (kseg == column(seg[pos(blk)]))
        bias[rows, :] = jnp.where(allowed, 0.0, MASKED)

    xh_sends = {}

    def normed_block(l, turn, blk, values):
        p = pos(blk)
        xall[l, rows_at(p), :] = layer_norm(values, sm[l, 0:1, :D], sm[l, 1:2, :D]).astype(BF16)
        for n in range(N - 1):
            part = xall.at[l, pl.ds(pl.multiple_of(p * T + core * T2, T2), T2), :]
            s, rsem = sems.one(), sems.one()
            cp = push(part, part, s, rsem, ahead[n])
            cp.start()
            src = behind[n]
            slo = src + row * (C - 1 - 2 * src)
            sp = slo + blk * (C - 1 - 2 * slo)
            got = xall.at[l, pl.ds(pl.multiple_of(sp * T + core * T2, T2), T2), :]
            other = xall.at[l, pl.ds(pl.multiple_of(sp * T + (1 - core) * T2, T2), T2), :]
            come = push(got, got, s, rsem, ahead[n])
            fs, fr = sems.one(), sems.one()
            onward = push(got, got, fs, fr, sib)
            arrive = push(other, other, fs, fr, sib)
            xh_sends[(l, turn, n)] = (cp, come, onward, arrive, sp)

    def own_products(l, blk):
        p = pos(blk)
        xh = xall[l, rows_at(p), :]
        both = mm(xh, wqk[l])
        q[l, blk * T : (blk + 1) * T, :] = both[:, :H].astype(BF16)
        k[l, rows_at(p), :] = both[:, H:].astype(BF16)

    def value_products(l, p):
        src = l * core
        v[l, rows_at(p), :] = mm(xall[src, rows_at(p), :], wv[src]).astype(BF16)

    def key_products(l, p):
        k[l, rows_at(p), :] = mm(xall[l, rows_at(p), :], wqk[l, :, H:]).astype(BF16)

    @pl.when(core == 0)
    def _():
        e_load.wait()

    @pl.when(core == 1)
    def _():
        own_come.wait_recv()

    sm_push.wait()
    blk = row
    r[0, pl.ds(pl.multiple_of(blk * T, T), T), :] = e[0, blk]
    normed_block(0, 0, blk, e[0, blk].astype(F32))

    @pl.when(core == 0)
    def _():
        loads[0].wait()
        loads[1].wait()
        v_shared.wait()

    @pl.when(core == 1)
    def _():
        for cp in qk_push:
            cp.wait_recv()
        v_push.wait_recv()

    def own_products_dynamic(l, blk):
        p = pos(blk)
        both = mm(xall[l, rows_at(p), :], wqk[l])
        q[l, pl.ds(pl.multiple_of(blk * T, T), T), :] = both[:, :H].astype(BF16)
        k[l, rows_at(p), :] = both[:, H:].astype(BF16)
        value_products(l, p)

    own_products_dynamic(0, blk)
    blk = 1 - row

    @pl.when(core == 0)
    def _():
        far_come.wait_recv()
        fwd_push.start()

    @pl.when(core == 1)
    def _():
        fwd_come.wait_recv()

    r[0, pl.ds(pl.multiple_of(blk * T, T), T), :] = e[0, blk]
    normed_block(0, 1, blk, e[0, blk].astype(F32))
    own_products_dynamic(0, blk)

    def finish_layer_inputs(l):
        for turn in range(2):
            for n in range(N - 1):
                cp, come, onward, arrive, sp = xh_sends[(l, turn, n)]
                come.wait_recv()
                onward.start()
        for turn in range(2):
            for n in range(N - 1):
                cp, come, onward, arrive, sp = xh_sends[(l, turn, n)]
                arrive.wait_recv()
                key_products(l, sp)
                value_products(l, sp)

    def middle(l):
        sends = []
        for blk in range(2):
            rows = slice(blk * T, (blk + 1) * T)
            attention_block(l, blk, T, L // 2 if blk == 0 else L, pairs, q, k, v, o, lse, bias)
            if l == 0 and blk == 0:
                @pl.when(core == 0)
                def _():
                    loads[2].wait()

                @pl.when(core == 1)
                def _():
                    rest_push[0].wait_recv()
            if l == 1 and blk == 0:
                @pl.when(core == 1)
                def _():
                    loads[2].wait()

                @pl.when(core == 0)
                def _():
                    rest_push[0].wait_recv()
            part = mm(o[l, rows, :], wout[l])
            hr[l, rows, :] = part
            br_s[l, rows, :] = part.astype(BF16)
            cp = push(br_s.at[l, rows, :], br_r.at[l, rows, :], sems.one(), sems.one(), sib)
            cp.start()
            sends.append(cp)
        save(q.at[l], q_o.at[l])
        save(k.at[l], k_o.at[l])
        save(v.at[l], v_o.at[l])
        save(o.at[l], o_o.at[l])
        save(lse.at[l], lse_o.at[l])
        save(xall.at[l], xall_o.at[l])
        mlps = []
        for blk in range(2):
            rows = slice(blk * T, (blk + 1) * T)
            sends[blk].wait_recv()
            hidden = r[l, rows, :].astype(F32) + hr[l, rows, :] + br_r[l, rows, :].astype(F32)
            hr[l, rows, :] = hidden
            normed2 = layer_norm(hidden, sm[l, 2:3, :D], sm[l, 3:4, :D]).astype(BF16)
            hh[l, rows, :] = normed2
            if blk == 0:
                local = core == l

                @pl.when(local)
                def _():
                    loads[3].wait()
                    loads[4].wait()

                @pl.when(jnp.logical_not(local))
                def _():
                    rest_push[1].wait_recv()
                    rest_push[2].wait_recv()
            mine = pl.ds(pl.multiple_of(core * FH, 128), FH)
            u = mm(normed2, wfc[l]) + sm[l, 4:5, mine]
            a, slope = gelu_both(u)
            a = a.astype(BF16)
            gp[l, rows, :] = slope.astype(BF16)
            act[l, rows, :] = a
            part = mm(a, wproj[l])
            y[rows, :] = part
            ml_s[l, rows, :] = part.astype(BF16)
            cp = push(ml_s.at[l, rows, :], ml_r.at[l, rows, :], sems.one(), sems.one(), sib)
            cp.start()
            mlps.append(cp)
        save(hr.at[l], hr_o.at[l])
        save(hh.at[l], hh_o.at[l])
        save(gp.at[l], gp_o.at[l])
        save(act.at[l], act_o.at[l])
        if l == 0:
            when(jnp.logical_not(owner), act_push.start)
        for blk in range(2):
            rows = slice(blk * T, (blk + 1) * T)
            mlps[blk].wait_recv()
            out = hr[l, rows, :] + y[rows, :] + ml_r[l, rows, :].astype(F32)
            if l == 0:
                sent = out.astype(BF16)
                r[1, rows, :] = sent
                normed_block(1, blk, blk, sent.astype(F32))
                if blk == 0:
                    @pl.when(core == 1)
                    def _():
                        loads[0].wait()
                        loads[1].wait()
                        v_fresh.wait()

                    @pl.when(core == 0)
                    def _():
                        for cp in qk_push:
                            cp.wait_recv()
                own_products(1, blk)
                value_products(1, pos(blk))
            else:
                y[rows, :] = out
                yb[rows, :] = out.astype(BF16)
        return sends + mlps

    act_push = push(act.at[0], act_in_o, sems.one(), sems.one(), across)
    gm_push = push(e.at[1], gm_in_o, sems.one(), sems.one(), across)
    finish_layer_inputs(0)

    @pl.when(core == 1)
    def _():
        far_push.start()

    for cp in rest_push:
        cp.start()
    pair_sends = middle(0)

    @pl.when(core == 1)
    def _():
        far_come.wait_recv()
        fwd_push.start()
        e_load.wait()

    finish_layer_inputs(1)

    @pl.when(core == 0)
    def _():
        fwd_come.wait_recv()
        own_come.wait_recv()

    when(jnp.logical_not(owner), gm_push.start)
    save(r, r_o)
    pair_sends += middle(1)
    save(y, y_o)
    save(yb, yb_o)
    save(e.at[1], gy_o)
    save(sm, sm_o)
    for l in range(2):
        wvt[l] = jnp.transpose(wv[l * core])
        save(wqk.at[l], watt_o.at[l, pl.ds(0, D)])
        save(wout.at[l], watt_o.at[l, pl.ds(D, H)])
        save(wvt.at[l], watt_o.at[l, pl.ds(D + H, H)])
    save(wfc, wfc_o)
    save(wproj, wproj_o)
    def crossed():
        act_push.wait_recv()
        gm_push.wait_recv()

    def crossing():
        act_push.wait_send()
        gm_push.wait_send()

    when(owner, crossed)
    when(jnp.logical_not(owner), crossing)
    far_push.wait_send()
    fwd_push.wait_send()
    own_push.wait_send()
    for cp in qk_push + rest_push + pair_sends:
        cp.wait_send()

    @pl.when(core == 0)
    def _():
        v_push.wait_send()

    for cp, come, onward, arrive, sp in xh_sends.values():
        cp.wait_send()
        onward.wait_send()
    for cp in saves:
        cp.wait()


def forward_pass(C, m, ends, segs, g1, b1, g2, b2, qkv, wo, fc, fcb, proj, shared):
    T, D, F = ends.shape[2], ends.shape[3], fc.shape[2]
    N, L, H, FH = C // 2, C * T, D // 2, F // 2
    R, pairs = 2 * T, D // 256
    S = jax.ShapeDtypeStruct
    outs = [S((2, L, D), BF16), S((2, R, H), BF16), S((2, L, H), BF16), S((2, L, H), BF16), S((2, R, H), BF16),
            S((2, R, 128), F32), S((2, R, D), BF16), S((2, R, D), F32), S((2, R, D), BF16), S((2, R, FH), BF16),
            S((2, R, FH), BF16), S((R, D), F32), S((R, D), BF16), S((2, T, D), BF16), S((2, 8, F), F32), S((2, 2 * D, D), BF16),
            S((2, D, FH), BF16), S((2, FH, D), BF16), S((R, FH), BF16), S((2, T, D), BF16), S((1, L), jnp.int32)]
    V = pltpu.VMEM
    scratch = [V((2, 2, T, D), BF16), V((C, 1, T), jnp.int32), V((2, 8, F), F32), V((2, D, D), BF16), V((2, D, H), BF16),
               V((2, H, D), BF16), V((2, D, FH), BF16), V((2, FH, D), BF16), V((2, L, D), BF16), V((2, R, H), BF16),
               V((2, L, H), BF16), V((2, L, H), BF16), V((2, R, H), BF16), V((2, R, 128), F32), V((2, R, D), BF16),
               V((2, R, D), F32), V((2, R, D), BF16), V((2, R, FH), BF16), V((2, R, FH), BF16), V((R, D), F32),
               V((R, D), BF16), V((2, H, D), BF16), V((R, L), F32), V((2, R, D), BF16), V((2, R, D), BF16), V((2, R, D), BF16), V((2, R, D), BF16),
               pltpu.SemaphoreType.DMA((80 + 20 * N + 2 * C,))]
    return pl.pallas_call(
        functools.partial(forward_kernel, C, m, T, D, F),
        in_specs=[HBM, HBM, VM, VM, VM, VM, HBM, HBM, HBM, VM, HBM, HBM],
        out_specs=[HBM] * 20 + [VM],
        out_shape=outs,
        scratch_shapes=scratch,
        compiler_params=pltpu.CompilerParams(collective_id=0, has_side_effects=True, vmem_limit_bytes=VMEM_LIMIT),
        name="forward_pass",
    )(ends, segs, g1, b1, g2, b2, qkv, wo, fc, fcb, proj, shared)


WHOLE, SIDED, SIDE_STEP = 0, 1, 2
JOBS = ("P0", "P1", "P2", "F0", "F1", "F2", "O", "Q", "K", "V")
POLLS = (
    (),
    (),
    (),
    (13,),
    (),
    (14, 13),
    (15, 16),
    (10, 11, 13, 14),
    (12,),
    (10, 15, 13, 11),
    (16, 14),
    (13,),
    (),
    (18, 17, 12, 10, 15, 19, 11),
    (16, 14, 12, 15),
    (18, 11, 10, 16),
    (14, 12),
    (15, 18, 16),
    (19, 17, 3),
    (18, 19, 17, 4, 3, 6),
    (5,),
    (0, 4, 18, 19, 17, 1),
    (3, 5),
    (2, 0),
    (4, 19, 17, 3),
    (6,),
    (1, 3),
    (8, 7, 5, 2, 0, 4, 6),
)
TAIL = (9, 1, 5, 2, 7, 8, 4, 0, 6, 9, 1, 5, 2, 7, 8, 6, 9, 7, 8, 9, 7, 8, 9)


class Job:
    def __init__(self, env, buf, lead, cols, order, sided, land, credits, first_layer, active, earlier):
        self.env, self.buf, self.lead, self.cols = env, buf, lead, cols
        self.sided, self.land, self.credits, self.first_layer, self.active = sided, land, credits, first_layer, active
        self.earlier = earlier
        self.bits = list(range(env.m - 2 if sided else env.m - 1, -1, -1))
        self.fixed, self.z_done, self.steps, self.at = {}, False, [], 0
        self.used = 0
        if sided == SIDE_STEP:
            self.steps.append(("side", None, None))
        for item in order:
            if item == "z":
                for s in range(1, env.C):
                    self.steps.append(("z", s, dict(self.fixed)))
                self.z_done = True
            else:
                self.steps.append(("bit", item, (dict(self.fixed), self.z_done)))
                self.fixed[item] = env.bit(item)
        self.plans = [self.plan(i) for i in range(len(self.steps))]

    def view(self, fixed, zat):
        at = tuple(self.lead) + tuple(fixed.get(b, slice(None)) for b in self.bits)
        return at + (slice(None) if zat is None else zat, slice(None), self.cols)

    def plan(self, i):
        env = self.env
        kind, what, state = self.steps[i]
        moves = []
        if kind == "side":
            other = env.dp_xor(env.m - 1)
            moves.append((env.bit(env.m - 1) != env.core, self.view({}, None), other, env.bit(env.m - 1) == env.core,
                          self.view({}, None), other))
            return [self.bind(move, self.land[i]) for move in moves]
        active = self.active if not self.sided else (env.bit(env.m - 1) == env.core)
        if kind == "bit":
            fixed, z_done = state
            zat = env.z if z_done else None
            other = env.dp_xor(what)
            mine = env.bit(what)
            moves.append((active, self.view({**fixed, what: 1 - mine}, zat), other, active,
                          self.view({**fixed, what: mine}, zat), other))
            return [self.bind(move, self.land[i]) for move in moves]
        s, C, z = what, env.C, env.z
        zm = C - 1 - z
        for side, (p, sign) in enumerate(((z, 1), (zm, -1))):
            out_at = z + sign * (C - s)
            in_at = z + sign * (C - s - 1)
            moves.append((both(active, p < s), self.view(state, out_at), env.line(z + sign),
                          both(active, both(p >= 1, p <= s)), self.view(state, in_at), env.line(z - sign)))
        return [self.bind(move, self.land[i].at[side]) for side, move in enumerate(moves)]

    def bind(self, move, slot):
        send_if, src, to, recv_if, dst, source = move
        env = self.env
        sem_s, sem_r = env.sems.one(), env.sems.one()
        credit = self.credits.at[self.used]
        self.used += 1
        return send_if, src, to, recv_if, dst, source, slot, sem_s, sem_r, credit

    def send(self, i):
        for send_if, src, to, recv_if, dst, source, slot, sem_s, sem_r, credit in self.plans[i]:
            cp = push(self.buf.at[src], slot, sem_s, sem_r, to)

            def go(cp=cp, credit=credit):
                if not self.first_layer:
                    when(self.earlier, lambda: pl.semaphore_wait(credit, 1))
                cp.start()

            when(send_if, go)
            self.env.sent.append((send_if, cp))

    def take(self, i):
        for send_if, src, to, recv_if, dst, source, slot, sem_s, sem_r, credit in self.plans[i]:
            cp = push(slot, slot, sem_s, sem_r, to)

            def got(cp=cp, dst=dst, slot=slot, credit=credit, source=source):
                cp.wait_recv()
                self.buf[dst] = self.buf[dst] + slot[...]
                if self.first_layer:
                    pl.semaphore_signal(credit, inc=1, device_id=source, device_id_type=MESH)

            when(recv_if, got)

    def start(self):
        self.send(0)

    def advance(self):
        if self.at >= len(self.steps):
            return
        self.take(self.at)
        self.at += 1
        if self.at < len(self.steps):
            self.send(self.at)

    def own(self):
        return self.view(self.fixed, self.env.z)


def both(a, b):
    if a is True:
        return b
    if b is True:
        return a
    return jnp.logical_and(a, b)


def when(condition, fn):
    if condition is True:
        fn()
    else:
        pl.when(condition)(fn)


class Env:
    def __init__(self, C, m, core, dp, z, sems):
        self.C, self.m, self.core, self.dp, self.z, self.sems, self.sent = C, m, core, dp, z, sems, []

    def bit(self, b):
        return lax.rem(lax.div(self.dp, 1 << b), 2)

    def dp_xor(self, b):
        return (self.core, self.dp + (1 << b) * (1 - 2 * self.bit(b)), self.z)

    def line(self, z):
        return (self.core, self.dp, z)


def job_table(m):
    xs, ys = list(range(m)), list(range(m - 1, -1, -1))
    rest = list(range(m - 1))
    xz, yz = xs + ["z"], ys + ["z"]
    return {
        "P0": ("gproj", (0, 3), ["z"] + rest, SIDED), "P1": ("gproj", (1, 3), rest + ["z"], SIDED),
        "P2": ("gproj", (2, 3), rest + ["z"], SIDED),
        "F0": ("gfc", (0, 3), ["z"] + ys, WHOLE), "F1": ("gfc", (1, 3), xz, WHOLE), "F2": ("gfc", (2, 3), xz, WHOLE),
        "O": ("gout", (0, 1), rest + ["z"], SIDE_STEP),
        "Q": ("gq", (0, 1), xz, WHOLE), "K": ("gk", (0, 1), yz, WHOLE), "V": ("gv", (0, 1), xz, WHOLE),
    }


def grad_shapes(C, m, D, F):
    H, FH, J = D // 2, F // 2, C << m
    full, side = (2,) * m + (C,), (2,) * (m - 1) + (C,)
    return {"gproj": side + (F // J, D), "gfc": full + (D // J, FH), "gout": side + (D // J, D),
            "gq": full + (D // J, H), "gk": full + (D // J, H), "gv": full + (D // J, H)}


def landing_shapes(C, m, D, F):
    shapes = grad_shapes(C, m, D, F)
    result = {}
    for name, (buf, (at, parts), order, sided) in job_table(m).items():
        shape = list(shapes[buf])
        shape[-1] //= parts
        n = m - 1 if sided else m
        lead = {b: 2 for b in range(n)}
        tail = [shape[-2], shape[-1]]
        zdim = [C]
        steps = []
        if sided == SIDE_STEP:
            steps.append(tuple([2] * n + zdim + tail))
        for item in order:
            if item == "z":
                zdim = []
                for s in range(1, C):
                    steps.append(tuple([2] + [2] * len(lead) + tail))
            else:
                lead.pop(item)
                steps.append(tuple([2] * len(lead) + zdim + tail))
        result[name] = steps
    return result


def norm_grad(values, gain, grad):
    unit, rstd = unit_norm(values)
    scaled = grad * gain
    m1 = jnp.mean(scaled, axis=-1, keepdims=True)
    m2 = jnp.mean(scaled * unit, axis=-1, keepdims=True)
    back = rstd * (scaled - m1 - unit * m2)
    return back, jnp.sum(grad * unit, axis=0, keepdims=True), jnp.sum(grad, axis=0, keepdims=True)


def attention_back_pair(i, T, L, q, k, v, o, lse, goa, bias, dq, dk, dv, dv_at):
    cols = slice(i * 128, (i + 1) * 128)
    lane = lax.broadcasted_iota(jnp.int32, (T, 128), 1)
    scale = jnp.asarray(HEAD**-0.5, BF16)
    totals = None
    for blk in (1, 0):
        rows = slice(blk * T, (blk + 1) * T)
        keys = L if blk else L // 2
        q2, go2 = q[rows, cols] * scale, goa[rows, cols]
        prod = go2.astype(F32) * o[rows, cols].astype(F32)
        k2, v2 = k[:keys, cols], v[:keys, cols]
        dqs, dks, dvs = [], None, None
        for h in range(2):
            sel = (lane >= 64) == (h == 1)
            qh = jnp.where(sel, q2, jnp.zeros_like(q2))
            goh = jnp.where(sel, go2, jnp.zeros_like(go2))
            delta = jnp.sum(jnp.where(sel, prod, 0.0), axis=-1, keepdims=True)
            s = mm_nt(qh, k2) + bias[rows, :keys].astype(F32)
            prob = jnp.exp(s - lse[rows, 2 * i + h : 2 * i + h + 1])
            gp = mm_nt(goh, v2)
            gs = (prob * (gp - delta)).astype(BF16)
            dqs.append(mm(gs, k2))
            one_k = mm_tn(gs, qh)
            one_v = mm_tn(prob.astype(BF16), goh)
            dks = one_k if dks is None else dks + one_k
            dvs = one_v if dvs is None else dvs + one_v
        dq[rows, cols] = (jnp.where(lane < 64, dqs[0], dqs[1]) * HEAD**-0.5).astype(BF16)
        if blk:
            totals = (dks, dvs)
        else:
            dk[:keys, cols] = (totals[0][:keys] + dks).astype(BF16)
            dk[keys:, cols] = totals[0][keys:].astype(BF16)
            dv[dv_at, :keys, cols] = (totals[1][:keys] + dvs).astype(BF16)
            dv[dv_at, keys:, cols] = totals[1][keys:].astype(BF16)


LOADED = ("gp", "act", "hh", "hr", "o", "q", "k", "v", "lse", "xall", "r")


def backward_kernel(C, m, T, D, F, fused, names_in, *refs):
    n_in = len(names_in)
    hbm = dict(zip(names_in, refs[:n_in]))
    outs, (vm, dma, credits) = refs[n_in:-3], refs[-3:]
    ends_o, small_o = outs[:2]
    core, dp, z = lax.axis_index(SECTION), lax.axis_index(DP), lax.axis_index(CTX)
    N, L, H, FH = C // 2, C * T, D // 2, F // 2
    row = lax.div(z, N)
    lo = z + row * (C - 1 - 2 * z)
    hi = C - 1 - lo
    base = row * N
    pairs = H // 128
    sems = Sems(dma)
    env = Env(C, m, core, dp, z, sems)
    sib = (1 - core, dp, z)
    mirror = (core, dp, C - 1 - z)
    pos = lambda blk: lo + blk * (hi - lo)
    block = lambda at: pl.ds(pl.multiple_of(at * T, T), T)
    other_nodes = [base + lax.rem(z - base + n, N) for n in range(1, N)]
    sent = env.sent
    loads = {}

    def load(name, l, src=None, dst=None):
        cp = pltpu.make_async_copy(hbm[name].at[l] if src is None else src, vm[name] if dst is None else dst, sems.one())
        cp.start()
        loads[(name, l)] = cp

    def need(*names):
        for name in names:
            loads[name].wait()

    def pushed(src, dst, to, condition=True, until=sent):
        cp = push(src, dst, sems.one(), sems.one(), to)
        when(condition, cp.start)
        until.append((condition, cp))
        return cp

    load("gy", 1, hbm["gy"].at[0], vm["gm"].at[0])
    load("gy", 0, hbm["gy"].at[1], vm["gm"].at[1])
    load("wproj", 1, dst=vm["wa"])
    load("gp", 1)
    load("wfc", 1)
    load("act", 1)
    load("hh", 1)
    load("hr", 1)
    load("sm", 0, hbm["sm"], vm["sm"])
    for name in ("o", "q", "k", "v", "lse", "xall", "r"):
        load(name, 1)
    y_keep = pltpu.make_async_copy(hbm["y"].at[block(row)], ends_o.at[0, row], sems.one())
    when(core == 1, y_keep.start)

    kseg = hbm["kseg"]
    for blk in range(2):
        rows = slice(blk * T, (blk + 1) * T)
        qpos = pos(blk) * T + lax.broadcasted_iota(jnp.int32, (T, L), 0)
        kpos = lax.broadcasted_iota(jnp.int32, (T, L), 1)
        mine = kseg[0:1, 0:T]
        for n in range(1, C):
            mine = jnp.where(pos(blk) == n, kseg[0:1, n * T : (n + 1) * T], mine)
        allowed = (kpos <= qpos) & (kseg[...] == column(mine))
        vm["bias"][rows, :] = jnp.where(allowed, 0.0, MASKED).astype(BF16)

    greet([sib] + [env.line(lax.rem(z + n, C)) for n in range(1, C)] + [env.dp_xor(b) for b in range(m)])

    y_push = pushed(hbm["yb"].at[block(1 - row)], vm["far"], mirror, core == 1)
    top = env.bit(m - 1) == core
    aside = jnp.logical_not(top)
    across = env.dp_xor(m - 1)
    act_push = pushed(hbm["act"].at[1], vm["act_in"], across, aside)
    gm_in_load = pltpu.make_async_copy(hbm["gm_in"], vm["gm_in"].at[1], sems.one())
    act_in_load = pltpu.make_async_copy(hbm["act_in"], vm["act_in"], sems.one())
    when(top, gm_in_load.start)
    gm_push = push(vm["gm"], vm["gm_in"].at[0], sems.one(), sems.one(), across)

    table = job_table(m)
    jobs = {}

    def start(name, l):
        if not fused:
            return
        buf, (at, parts), order, sided = table[name]
        width = vm[buf].shape[-1] // parts
        earlier = True if name != "V" else core == 1
        active = True if l == 0 else earlier
        jobs[(name, l)] = Job(env, vm[buf], (l,), slice(at * width, (at + 1) * width), order, sided, vm["land"][name],
                              credits[name], l == 1, active, earlier)
        jobs[(name, l)].start()

    def adv(l, *names):
        if not fused:
            return
        for name in names:
            jobs[(name, l)].advance()

    gm, gp, go, ghh, wa, wfc = vm["gm"], vm["gp"], vm["go"], vm["ghh"], vm["wa"], vm["wfc"]
    sm, sg = vm["sm"], vm["sg"]

    def put(buf, l, cols, value):
        shape = vm[buf].shape[1:-1] + (value.shape[-1],)
        vm[buf][(l,) + (slice(None),) * (len(shape) - 1) + (cols,)] = value.astype(BF16).reshape(shape)

    polls = iter(POLLS)

    def poll():
        for code in next(polls):
            adv(code // 10, JOBS[code % 10])

    def layer_back(l):
        again = []
        need(("wproj", l), ("gp", l))
        bias_sum = None
        for blk in range(2):
            rows = slice(blk * T, (blk + 1) * T)
            if l == 1:
                need(("gy", 1 - blk))
                go[rows, :] = gm[blk].astype(F32)
            gu = (gp[rows, :].astype(F32) * mm_nt(gm[blk], wa[...])).astype(BF16)
            gp[rows, :] = gu
            part = jnp.sum(gu.astype(F32), axis=0, keepdims=True)
            bias_sum = part if bias_sum is None else bias_sum + part
        sg[l, 4:5, :] = bias_sum
        load("watt", l, dst=wa)
        poll()
        need(("wfc", l))
        shares = []
        for blk in range(2):
            rows = slice(blk * T, (blk + 1) * T)
            part = mm_nt(gp[rows, :], wfc[...])
            ghh[rows, :] = part
            vm["a_s"][rows, :] = part.astype(BF16)
            shares.append(pushed(vm["a_s"].at[rows, :], vm["a_r"].at[rows, :], sib, until=[]))
        if l == 1:
            load("wfc", 0)
        poll()
        need(("hh", l))
        third = FH // 3
        for i in (0, 1, 2):
            cols = slice(i * third, (i + 1) * third)
            put("gfc", l, cols, mm_tn(vm["hh"][...], gp[:, cols]))
            start("F%d" % i, l)
        poll()
        if l == 1:
            load("hh", 0)
            load("gp", 0)
        need(("hr", l), ("watt", l))
        if l == 1:
            need(("sm", 0))
        sums = None
        for blk in range(2):
            rows = slice(blk * T, (blk + 1) * T)
            shares[blk].wait_recv()
            grad = ghh[rows, :] + vm["a_r"][rows, :].astype(F32)
            back, gain_sum, bias_sum = norm_grad(vm["hr"][rows, :], sm[l, 2:3, :D], grad)
            total = go[rows, :] + back
            go[rows, :] = total
            low = total.astype(BF16)
            vm["gb"][rows, :] = low
            vm["goa"][rows, :] = mm_nt(low, wa[D : D + H, :]).astype(BF16)
            sums = (gain_sum, bias_sum) if sums is None else (sums[0] + gain_sum, sums[1] + bias_sum)
        sg[l, 2:3, :D] = sums[0]
        sg[l, 3:4, :D] = sums[1]
        poll()
        if l == 1:
            load("hr", 0)
        need(("o", l))
        put("gout", l, slice(0, D), mm_tn(vm["o"][...], vm["gb"][...]))
        start("O", l)
        poll()
        need(("q", l), ("k", l), ("v", l), ("lse", l))
        for i in range(pairs):
            attention_back_pair(i, T, L, vm["q"], vm["k"], vm["v"], vm["o"], vm["lse"], vm["goa"], vm["bias"], vm["dq"],
                                vm["dk"], vm["dv"], l)
            if i == 0:
                def proj_grad():
                    if l == 1:
                        act_push.wait_recv()
                        gm_in_load.wait()
                    else:
                        act_in_load.wait()
                        gm_push.wait_recv()
                    third = D // 3
                    for n in range(3):
                        cols = slice(n * third, (n + 1) * third)
                        total = mm_tn(vm["act_in"][...], vm["gm_in"][l, :, :, cols].reshape(2 * T, third))
                        for blk in range(2):
                            total += mm_tn(vm["act"][blk * T : (blk + 1) * T, :], gm[blk, :, cols])
                        put("gproj", l, cols, total)

                need(("act", l))
                when(top, proj_grad)
                for n in range(3):
                    start("P%d" % n, l)
                if l == 1:
                    load("act", 0)
                    when(top, act_in_load.start)
            poll()
        if l == 1:
            for name in ("o", "q", "k", "v", "lse"):
                load(name, 0)
        else:
            def merge():
                vm["dv"][0] = (vm["dv"][0].astype(F32) + vm["dv"][1].astype(F32)).astype(BF16)

            when(core == 0, merge)
        dk, dv, dq = vm["dk"], vm["dv"], vm["dq"]

        def key_part(at):
            part_v = dv[l, block(at), :]
            if l == 1:
                part_v = jnp.where(core == 1, part_v, jnp.zeros_like(part_v))
            return mm_nt(dk[block(at), :], wa[:D, H:]) + mm(part_v, wa[D + H :, :])

        crossing, gives = [], []
        for n, node in enumerate(other_nodes):
            dlo = node + row * (C - 1 - 2 * node)
            dhi = C - 1 - dlo
            vm["fs_s"][n] = key_part(dlo + (1 - core) * (dhi - dlo)).astype(BF16)
            gives.append(pushed(vm["fs_s"].at[n], vm["fs_r"].at[n], sib, until=again))
        for n, node in enumerate(other_nodes):
            dlo = node + row * (C - 1 - 2 * node)
            keep = key_part(dlo + core * (C - 1 - 2 * dlo))
            gives[n].wait_recv()
            vm["fx_s"][n] = (keep + vm["fs_r"][n].astype(F32)).astype(BF16)
            crossing.append(pushed(vm["fx_s"].at[n], vm["fx_r"].at[l, n], (core, dp, node), until=again))
        poll()
        for blk in range(2):
            rows = slice(blk * T, (blk + 1) * T)
            ghh[rows, :] = key_part(pos(blk)) + mm_nt(dq[rows, :], wa[:D, :H])
        for cp in shares:
            cp.wait_send()
        early = pl.ds(pl.multiple_of((1 - core) * T, T), T)
        late = pl.ds(pl.multiple_of(core * T, T), T)
        vm["a_s"][early, :] = ghh[early, :].astype(BF16)
        shares = [pushed(vm["a_s"].at[early, :], vm["b_r"].at[early, :], sib, until=again)]
        if l == 1:
            load("wproj", 0, dst=wa)
        poll()
        need(("xall", l))
        xall = vm["xall"]
        put("gk", l, slice(0, H), mm_tn(xall[...], dk[...]))
        start("K", l)
        poll()
        put("gq", l, slice(0, H), mm_tn(xall[block(lo), :], dq[:T, :]) + mm_tn(xall[block(hi), :], dq[T:, :]))
        start("Q", l)
        poll()
        put("gv", l, slice(0, H), mm_tn(xall[...], dv[l]))
        start("V", l)
        poll()
        if l == 1:
            load("xall", 0)
        need(("r", l))
        for n in range(N - 1):
            crossing[n].wait_recv()
            ghh[late, :] += vm["fx_r"][l, n].astype(F32)
        vm["a_s"][late, :] = ghh[late, :].astype(BF16)
        shares.append(pushed(vm["a_s"].at[late, :], vm["b_r"].at[late, :], sib, until=again))
        for cp in shares:
            cp.wait_recv()
        sums = None
        for blk in range(2):
            rows = slice(blk * T, (blk + 1) * T)
            grad = ghh[rows, :] + vm["b_r"][rows, :].astype(F32)
            back, gain_sum, bias_sum = norm_grad(vm["r"][rows, :].astype(F32), sm[l, 0:1, :D], grad)
            total = go[rows, :] + back
            go[rows, :] = total
            if l == 1:
                gm[blk] = total.astype(BF16)
            sums = (gain_sum, bias_sum) if sums is None else (sums[0] + gain_sum, sums[1] + bias_sum)
        sg[l, 0:1, :D] = sums[0]
        sg[l, 1:2, :D] = sums[1]
        poll()
        if l == 1:
            load("r", 0)
            when(aside, gm_push.start)
            sent.append((aside, gm_push))
        for condition, cp in again:
            when(condition, cp.wait_send)

    layer_back(1)
    layer_back(0)

    keep = pl.ds(pl.multiple_of(row * T, T), T)
    away = pl.ds(pl.multiple_of((1 - row) * T, T), T)
    vm["gb"][:T, :] = go[away, :].astype(BF16)
    x_push = pushed(vm["gb"].at[pl.ds(0, T), :], vm["far"], mirror, core == 0)
    x_keep = pltpu.make_async_copy(go.at[keep, :], ends_o.at[0, row], sems.one())
    when(core == 0, x_keep.start)

    sv, sv_r = vm["sv"], vm["sv_r"]
    sv[0] = jnp.zeros_like(sv[0])
    sv[0, 0:4, :] = sg[core, 0:4, :]
    sv[0, 4:5, :] = sg[0, 4:5, :]
    sv[0, 5:6, :] = sg[1, 4:5, :]
    around = [env.dp_xor(b) for b in range(m)]
    b = 1
    while b < C:
        around.append(env.line(z + b * (1 - 2 * lax.rem(lax.div(z, b), 2))))
        b *= 2
    small_at = [0]
    small_cp = [pushed(sv.at[0], sv_r.at[0], around[0])]

    def small_step():
        i = small_at[0]
        small_cp[0].wait_recv()
        sv[i + 1] = sv[i] + sv_r[i]
        small_at[0] += 1
        if i + 1 < len(around):
            small_cp[0] = pushed(sv.at[i + 1], sv_r.at[i + 1], around[i + 1])

    def finish_ends():
        when(core == 0, x_push.wait_recv)
        when(core == 1, y_push.wait_recv)
        vm["ghh"][:T, :] = vm["far"][...].astype(F32)
        far_keep = pltpu.make_async_copy(vm["ghh"].at[pl.ds(0, T), :], ends_o.at[0, 1 - row], sems.one())
        far_keep.start()
        far_keep.wait()
        when(core == 0, x_keep.wait)
        when(core == 1, y_keep.wait)

    if fused:
        for at, code in enumerate(TAIL):
            adv(code // 10, JOBS[code % 10])
            if at % 4 == 3 and small_at[0] < len(around):
                small_step()
        for job in jobs.values():
            for _ in range(len(job.steps) - job.at):
                job.advance()
    while small_at[0] < len(around):
        small_step()
    last = len(around)
    small_o[...] = sv[last]

    if fused:
        hand_over(core, sib, env, vm, jobs, m, D, H, FH, pushed, sv, last, outs)
    else:
        leave = []
        for name, out in zip(("gproj", "gfc", "gout", "gq", "gk", "gv"), outs[2:]):
            leave.append(pltpu.make_async_copy(vm[name], out, sems.one()))
            leave[-1].start()
        for cp in leave:
            cp.wait()
    finish_ends()
    for condition, cp in sent:
        when(condition, cp.wait_send)


def hand_over(core, sib, env, vm, jobs, m, D, H, FH, pushed, sv, last, outs):
    small_o, qkv_o, out_o, fc_o, proj_o, shared_o = outs[1:]
    vm["fb_s"][...] = jnp.where(core == 0, sv[last, 5:6, :], sv[last, 4:5, :])
    fin = vm["fin"]
    top = env.bit(m - 1) == core
    own = lambda name, l: (l,) + jobs[(name, 0)].own()[1:]
    arrive = [
        pushed(vm["gfc"].at[own("F0", 1 - core)[:-1]], fin["fc"], sib),
        pushed(vm["gq"].at[own("Q", 1 - core)], fin["q"], sib),
        pushed(vm["gk"].at[own("K", 1 - core)], fin["k"], sib),
        pushed(vm["gv"].at[own("V", 0)], fin["v"], sib),
        pushed(vm["fb_s"], fin["fb"], sib),
    ]
    out_push = pushed(vm["gout"].at[own("O", 1 - core)], fin["out"], sib, top)
    proj_push = pushed(vm["gproj"].at[own("P0", 1 - core)[:-1]], fin["proj"], sib, top)

    here = pl.ds(pl.multiple_of(core * H, 128), H)
    there = pl.ds(pl.multiple_of((1 - core) * H, 128), H)
    here_k = pl.ds(pl.multiple_of(D + core * H, 128), H)
    there_k = pl.ds(pl.multiple_of(D + (1 - core) * H, 128), H)
    qkv_o[0, :, here] = vm["gq"][own("Q", core)].astype(F32)
    qkv_o[0, :, here_k] = vm["gk"][own("K", core)].astype(F32)
    fc_o[0, :, pl.ds(pl.multiple_of(core * FH, 128), FH)] = vm["gfc"][own("F0", core)[:-1]].astype(F32)

    def top_out():
        out_o[0] = vm["gout"][own("O", core)].astype(F32)
        proj_o[0] = vm["gproj"][own("P0", core)[:-1]].astype(F32)

    when(top, top_out)
    for cp in arrive:
        cp.wait_recv()

    def other_out():
        out_push.wait_recv()
        proj_push.wait_recv()
        out_o[0] = fin["out"][...].astype(F32)
        proj_o[0] = fin["proj"][...].astype(F32)

    when(jnp.logical_not(top), other_out)
    qkv_o[0, :, there] = fin["q"][...].astype(F32)
    qkv_o[0, :, there_k] = fin["k"][...].astype(F32)
    fc_o[0, :, pl.ds(pl.multiple_of((1 - core) * FH, 128), FH)] = fin["fc"][...].astype(F32)
    fresh = pl.ds(2 * D, H)

    def fresh_first():
        qkv_o[0, :, fresh] = fin["v"][...].astype(F32)
        shared_o[...] = vm["gv"][own("V", 0)].astype(F32)

    def fresh_second():
        qkv_o[0, :, fresh] = vm["gv"][own("V", 1)].astype(F32)
        shared_o[...] = fin["v"][...].astype(F32)

    when(core == 0, fresh_first)
    when(core == 1, fresh_second)
    small_o[6:7, :] = fin["fb"][...]


def backward_pass(C, m, T, D, F, inputs):
    N, L, H, FH, R, J = C // 2, C * T, D // 2, F // 2, 2 * T, C << m
    fused = (D // J) % 16 == 0 and (F // J) % 16 == 0 and m > 0
    pairs = H // 128
    S, V = jax.ShapeDtypeStruct, pltpu.VMEM
    names = tuple(inputs)
    outs = [S((1, 2, T, D), F32), S((8, FH), F32)]
    flat = {"gproj": (FH, D), "gfc": (D, FH), "gout": (H, D), "gq": (D, H), "gk": (D, H), "gv": (D, H)}
    if fused:
        outs += [S((1, D // J, 5 * H), F32), S((1, D // J, D), F32), S((1, D // J, F), F32), S((1, F // J, D), F32),
                 S((D // J, H), F32)]
        grads = grad_shapes(C, m, D, F)
        land = {name: [V(shape, BF16) for shape in steps] for name, steps in landing_shapes(C, m, D, F).items()}
    else:
        outs += [S((2,) + shape, BF16) for shape in flat.values()]
        grads, land = flat, {}
    stages = m + C.bit_length() - 1
    vm = dict(
        gm=V((2, T, D), BF16), gb=V((R, D), BF16), gm_in=V((2, 2, T, D), BF16), act_in=V((R, FH), BF16), gp=V((R, FH), BF16), act=V((R, FH), BF16), hh=V((R, D), BF16), hr=V((R, D), F32),
        o=V((R, H), BF16), q=V((R, H), BF16), k=V((L, H), BF16), v=V((L, H), BF16), lse=V((R, 128), F32),
        xall=V((L, D), BF16), r=V((R, D), BF16), sm=V((2, 8, F), F32), sg=V((2, 8, FH), F32), bias=V((R, L), BF16),
        wa=V((2 * D, D), BF16), wfc=V((D, FH), BF16), go=V((R, D), F32), ghh=V((R, D), F32), a_s=V((R, D), BF16),
        a_r=V((R, D), BF16), b_r=V((R, D), BF16), goa=V((R, H), BF16), dq=V((R, H), BF16),
        dk=V((L, H), BF16), dv=V((2, L, H), BF16), fs_s=V((N - 1, T, D), BF16), fs_r=V((N - 1, T, D), BF16),
        fx_s=V((N - 1, T, D), BF16), fx_r=V((2, N - 1, T, D), BF16), far=V((T, D), BF16),
        sv=V((stages + 1, 8, FH), F32), sv_r=V((stages, 8, FH), F32), fb_s=V((1, FH), F32),
        fin=dict(fc=V((D // J, FH), BF16), q=V((D // J, H), BF16), k=V((D // J, H), BF16), v=V((D // J, H), BF16),
                 out=V((D // J, D), BF16), proj=V((F // J, D), BF16), fb=V((1, FH), F32)),
        land=land, **{name: V((2,) + shape, BF16) for name, shape in grads.items()})
    moves = 1 + m + 2 * (C - 1)
    credits = {name: pltpu.SemaphoreType.REGULAR((moves,)) for name in job_table(m)} if fused else {}
    in_specs = [VM if name == "kseg" else HBM for name in names]
    return pl.pallas_call(
        functools.partial(backward_kernel, C, m, T, D, F, fused, names),
        in_specs=in_specs,
        out_specs=[HBM, VM] + [VM if fused else HBM] * (len(outs) - 2),
        out_shape=outs,
        scratch_shapes=[vm, pltpu.SemaphoreType.DMA((120 + 40 * moves,)), credits],
        compiler_params=pltpu.CompilerParams(collective_id=1, has_side_effects=True, vmem_limit_bytes=VMEM_LIMIT),
        name="backward_pass",
    )(*inputs.values())


def xor_route(size, bit):
    return [(i, i ^ (1 << bit)) for i in range(size)]


def halve(grad, axis_name, bit, at):
    mine = (lax.axis_index(axis_name) >> bit) & 1
    keep = lax.dynamic_index_in_dim(grad, mine, at, keepdims=False)
    send = lax.dynamic_index_in_dim(grad, 1 - mine, at, keepdims=False)
    got = lax.ppermute(send, axis_name, xor_route(lax.axis_size(axis_name), bit))
    return (keep.astype(F32) + got.astype(F32)).astype(grad.dtype)


def bits_of(axis_name):
    return lax.axis_size(axis_name).bit_length() - 1


def scatter_sum(grad, order, skip_first=False):
    dims = [(DP, b) for b in reversed(range(bits_of(DP)))] + [(CTX, b) for b in reversed(range(bits_of(CTX)))]
    if skip_first:
        dims = dims[1:]
    parts = len(dims)
    rows, cols = grad.shape
    grad = grad.reshape((2,) * parts + (rows >> parts, cols))
    for item in order:
        at = dims.index(item)
        grad = halve(grad, item[0], item[1], at)
        dims.pop(at)
    return grad


def shards(ends, segment_ids, ln1_gain, ln1_bias, qkv_weight, out_weight, ln2_gain, ln2_bias, fc_weight, fc_bias,
           proj_weight, shared_weight):
    core = lax.axis_index(SECTION)
    first = core == 0
    C, m = lax.axis_size(CTX), bits_of(DP)
    J = C << m
    micros, T, D = ends.shape[1:]
    F = fc_weight.shape[2]
    half, FH = D // 2, F // 2
    names = ("xall", "q", "k", "v", "o", "lse", "r", "hr", "hh", "gp", "act", "y", "yb", "gy", "sm", "watt", "wfc", "wproj", "act_in", "gm_in", "kseg")
    kept = dict(zip(names, forward_pass(
        C, m, ends, segment_ids.reshape(micros, 1, T), ln1_gain, ln1_bias, ln2_gain, ln2_bias, qkv_weight, out_weight,
        fc_weight, fc_bias, proj_weight, shared_weight)))
    block, small, *grads = backward_pass(C, m, T, D, F, kept)
    if len(grads) == 5:
        qkv_out, out_out, fc_out, proj_out, shared_out = grads
        other_bias = small[6]
    else:
        qkv_out, out_out, fc_out, proj_out, shared_out = scattered(grads, core, m, half)
        other_bias = swap(jnp.where(first, small[5], small[4]))
    own_bias = jnp.where(first, small[4], small[5])
    bias_grad = jnp.concatenate([jnp.where(first, own_bias, other_bias), jnp.where(first, other_bias, own_bias)])
    j = lax.axis_index(DP) * C + lax.axis_index(CTX)
    fcb_out = lax.dynamic_slice_in_dim(bias_grad, j * (F // J), F // J, 0)
    ln = lax.dynamic_slice_in_dim(small[:4], j * (D // J), D // J, 1)
    return (block, qkv_out, out_out, fc_out, fcb_out[None], proj_out, shared_out, ln[0:1], ln[1:2], ln[2:3], ln[3:4])


def scattered(grads, core, m, half):
    gproj, gfc, gout, gq, gk, gv = grads
    first = core == 0
    x_first = [(DP, b) for b in range(m)] + [(CTX, b) for b in range(bits_of(CTX))]
    y_first = [(DP, b) for b in reversed(range(m))] + x_first[m:]

    def sided(grad):
        dp, size = lax.axis_index(DP), lax.axis_size(DP)
        top = size // 2
        route = [(c * size + d, c * size + (d ^ top)) for c in range(2) for d in range(size) if (d >= top) != (c == 1)]
        got = lax.ppermute(grad, (SECTION, DP), route)
        return scatter_sum((grad.astype(F32) + got.astype(F32)).astype(BF16), y_first[1:], skip_first=True)

    res = []
    for l in range(2):
        qkv = jnp.concatenate([gq[l], gk[l], gv[l]], axis=1)
        res.append((scatter_sum(qkv, x_first), sided(gout[l]), scatter_sum(gfc[l], x_first),
                    scatter_sum(gproj[l], y_first[1:], skip_first=True)))
    holder = jnp.where(lax.axis_index(DP) >= lax.axis_size(DP) // 2, 1, 0) == core
    mine = tuple(jnp.where(first, a, b) for a, b in zip(res[0], res[1]))
    got = tuple(swap(jnp.where(first, b, a)) for a, b in zip(res[0], res[1]))
    left, right = [jnp.where(first, a, b).astype(F32) for a, b in zip(mine, got)], [jnp.where(first, b, a).astype(F32) for a, b in zip(mine, got)]
    fresh0 = res[0][0][:, 2 * half :]
    fresh0_other = swap(fresh0)
    fresh = jnp.where(first, fresh0_other, res[1][0][:, 2 * half :]).astype(F32)
    qkv_out = jnp.concatenate([left[0][:, :half], right[0][:, :half], left[0][:, half : 2 * half], right[0][:, half : 2 * half], fresh], axis=1)
    fc_out = jnp.concatenate([left[2], right[2]], axis=1)
    out_out = jnp.where(holder, mine[1], got[1]).astype(F32)
    proj_out = jnp.where(holder, mine[3], got[3]).astype(F32)
    shared_out = jnp.where(first, fresh0, fresh0_other).astype(F32)
    return qkv_out[None], out_out[None], fc_out[None], proj_out[None], shared_out


def solution(mesh):
    placed = (
        P(SECTION, DP, CTX, None), P(DP, CTX), P(SECTION, None), P(SECTION, None),
        P(SECTION, None, None), P(SECTION, None, None), P(SECTION, None), P(SECTION, None),
        P(SECTION, None, None), P(SECTION, None), P(SECTION, None, None), P(),
    )
    both = (DP, CTX)
    return jax.shard_map(
        shards, mesh=mesh, in_specs=placed,
        out_specs=(P(SECTION, DP, CTX, None), P(SECTION, both, None), P(SECTION, both, None),
                   P(SECTION, both, None), P(SECTION, both), P(SECTION, both, None), P(both, None),
                   P(SECTION, both), P(SECTION, both), P(SECTION, both), P(SECTION, both)),
        check_vma=False,
    )
```

```python
import functools

import jax
import jax.numpy as jnp
from jax import lax
from jax.experimental import pallas as pl
from jax.experimental.pallas import tpu as pltpu
from jax.sharding import PartitionSpec as P

HEAD = 64
SECTION, DP, CTX = "section", "dp", "ctx"
EPSILON = 1e-05
MASKED = -1000000000.0
F32 = jnp.float32
BF16 = jnp.bfloat16
VMEM_LIMIT = 127 * 2**19


def mm(left, right):
    return jnp.dot(left, right, preferred_element_type=F32)


def mm_nt(left, right):
    return lax.dot_general(left, right, (((1,), (1,)), ((), ())), preferred_element_type=F32)


def mm_tn(left, right):
    return lax.dot_general(left, right, (((0,), (0,)), ((), ())), preferred_element_type=F32)


def unit_norm(values):
    mean = jnp.mean(values, axis=-1, keepdims=True)
    centred = values - mean
    rstd = lax.rsqrt(jnp.mean(centred * centred, axis=-1, keepdims=True) + EPSILON)
    return centred * rstd, rstd


def layer_norm(values, gain, bias):
    return unit_norm(values)[0] * gain + bias


def gelu_both(u):
    t = jnp.tanh(0.7978845608028654 * (u + 0.044715 * u * u * u))
    half = 0.5 * (1.0 + t)
    return u * half, half + 0.5 * u * (1.0 - t * t) * (0.7978845608028654 + 3 * 0.044715 * 0.7978845608028654 * u * u)


def swap(x):
    return lax.ppermute(x, SECTION, [(0, 1), (1, 0)])


MESH = pl.DeviceIdType.MESH
HBM = pl.BlockSpec(memory_space=pl.ANY)
VM = pl.BlockSpec(memory_space=pltpu.VMEM)


class Sems:
    def __init__(self, ref):
        self.ref, self.used = ref, 0

    def one(self):
        self.used += 1
        return self.ref.at[self.used - 1]


def push(src, dst, send, recv, to):
    return pltpu.make_async_remote_copy(src_ref=src, dst_ref=dst, send_sem=send, recv_sem=recv, device_id=to,
                                        device_id_type=MESH)


def greet(peers):
    barrier = pltpu.get_barrier_semaphore()
    for peer in peers:
        pl.semaphore_signal(barrier, inc=1, device_id=peer, device_id_type=MESH)
    pl.semaphore_wait(barrier, len(peers))


def attention_block(l, blk, T, keys, pairs, q, k, v, o, lse, bias):
    rows = slice(blk * T, (blk + 1) * T)
    lane = lax.broadcasted_iota(jnp.int32, (T, 128), 1)

    def body(i, carry):
        cols = pl.ds(pl.multiple_of(i * 128, 128), 128)
        q2 = q[l, rows, cols] * jnp.asarray(HEAD**-0.5, BF16)
        k2 = k[l, :keys, cols]
        v2 = jnp.concatenate([v[l, :keys, cols], jnp.ones((keys, 128), BF16)], axis=1)
        outs, lses = [], []
        for h in range(2):
            qh = jnp.where((lane >= 64) == (h == 1), q2, jnp.zeros_like(q2))
            s = mm_nt(qh, k2) + bias[rows, :keys]
            top = jnp.max(s, axis=-1, keepdims=True)
            e = jnp.exp(s - top).astype(BF16)
            both = mm(e, v2)
            total = both[:, 128:]
            outs.append(both[:, :128] / total)
            lses.append(top + jnp.log(total))
        o[l, rows, cols] = jnp.where(lane < 64, outs[0], outs[1]).astype(BF16)
        old = jnp.where(lane == 2 * i, lses[0], lse[l, rows, :])
        lse[l, rows, :] = jnp.where(lane == 2 * i + 1, lses[1], old)
        return carry

    lax.fori_loop(0, pairs, body, 0)


def column(row_values):
    T = row_values.shape[1]
    at = lax.broadcasted_iota(jnp.int32, (T, T), 0) == lax.broadcasted_iota(jnp.int32, (T, T), 1)
    spread = jnp.where(at, jnp.broadcast_to(row_values, (T, T)), 0).astype(F32)
    return jnp.sum(spread, axis=1, keepdims=True).astype(jnp.int32)


def forward_kernel(C, m, T, D, F, ends, segs, g1, b1, g2, b2, qkv, wo, fc, fcb, proj, shared,
                   xall_o, q_o, k_o, v_o, o_o, lse_o, r_o, hr_o, hh_o, gp_o, act_o, y_o, yb_o, gy_o, sm_o, watt_o, wfc_o, wproj_o,
                   act_in_o, gm_in_o, kseg_o,
                   e, seg, segv, sm, wqk, wv, wout, wfc, wproj, xall, q, k, v, o, lse, r, hr, hh, gp, act, y, yb, wvt, bias,
                   br_s, br_r, ml_s, ml_r, dma):
    core, dp, z = lax.axis_index(SECTION), lax.axis_index(DP), lax.axis_index(CTX)
    N, L, H, FH = C // 2, C * T, D // 2, F // 2
    T2 = T // 2
    row = z // N
    lo = z + row * (C - 1 - 2 * z)
    hi = C - 1 - lo
    base = row * N
    pairs = H // 128
    sems = Sems(dma)
    sib = (1 - core, dp, z)
    mirror = (core, dp, C - 1 - z)
    top_bit = lax.div(dp, 1 << (m - 1))
    across = (core, dp + (1 - 2 * top_bit) * (1 << (m - 1)), z)
    owner = top_bit == core
    ahead = [(core, dp, base + lax.rem(z - base + n, N)) for n in range(1, N)]
    behind = [base + lax.rem(z - base + N - n, N) for n in range(1, N)]
    line = [(core, dp, lax.rem(z + n, C)) for n in range(1, C)]
    pos = lambda blk: lo + blk * (hi - lo)
    rows_at = lambda p: pl.ds(pl.multiple_of(p * T, T), T)
    saves = []

    def save(src, dst):
        cp = pltpu.make_async_copy(src, dst, sems.one())
        cp.start()
        saves.append(cp)

    e_load = pltpu.make_async_copy(ends.at[0, row], e.at[core, row], sems.one())
    e_load.start()
    qc = pl.ds(pl.multiple_of(core * H, 128), H)
    kc = pl.ds(pl.multiple_of(D + core * H, 128), H)
    qo = pl.ds(pl.multiple_of((1 - core) * H, 128), H)
    ko = pl.ds(pl.multiple_of(D + (1 - core) * H, 128), H)
    loads = [
        pltpu.make_async_copy(qkv.at[0, :, qc], wqk.at[core, :, pl.ds(0, H)], sems.one()),
        pltpu.make_async_copy(qkv.at[0, :, kc], wqk.at[core, :, pl.ds(H, H)], sems.one()),
        pltpu.make_async_copy(wo.at[0, pl.ds(pl.multiple_of(core * H, H), H), :], wout.at[core], sems.one()),
        pltpu.make_async_copy(fc.at[0, :, pl.ds(pl.multiple_of(core * FH, 128), FH)], wfc.at[core], sems.one()),
        pltpu.make_async_copy(proj.at[0, pl.ds(pl.multiple_of(core * FH, FH), FH), :], wproj.at[core], sems.one()),
    ]
    for cp in loads:
        cp.start()
    v_sem = sems.one()
    v_shared = pltpu.make_async_copy(shared, wv.at[0], v_sem)
    v_fresh = pltpu.make_async_copy(qkv.at[0, :, pl.ds(2 * D, H)], wv.at[1], v_sem)

    @pl.when(core == 0)
    def _():
        v_shared.start()

    @pl.when(core == 1)
    def _():
        v_fresh.start()

    segv[0] = segs[0:1, :]
    segv[1] = segs[1:2, :]
    seg[z] = segv[row]
    sm[core] = jnp.zeros_like(sm[core])
    sm[core, 0:1, :D] = g1[...]
    sm[core, 1:2, :D] = b1[...]
    sm[core, 2:3, :D] = g2[...]
    sm[core, 3:4, :D] = b2[...]
    sm[core, 4:5, :] = fcb[...]

    greet([sib, across] + line)

    own_s, own_r = sems.one(), sems.one()
    own_push = push(ends.at[0, row], e.at[core, row], own_s, own_r, sib)
    own_come = push(ends.at[0, row], e.at[1 - core, row], own_s, own_r, sib)
    seg_push = []
    for n in range(1, C):
        to = lax.rem(z + n, C)
        cp = push(segv.at[lax.div(to, N)], seg.at[z], sems.one(), sems.one(), line[n - 1])
        cp.start()
        seg_push.append(cp)
    far_push, far_come, fwd_push, fwd_come = [], [], [], []
    for h in range(2):
        part = pl.ds(h * T2, T2)
        far_s, far_r, fwd_s, fwd_r = sems.one(), sems.one(), sems.one(), sems.one()
        far_push.append(push(ends.at[0, 1 - row, part], e.at[core, row, part], far_s, far_r, mirror))
        far_come.append(push(ends.at[0, 1 - row, part], e.at[core, 1 - row, part], far_s, far_r, mirror))
        here, there = e.at[core, 1 - row, part], e.at[1 - core, 1 - row, part]
        fwd_push.append(push(here, here, fwd_s, fwd_r, sib))
        fwd_come.append(push(there, there, fwd_s, fwd_r, sib))

    @pl.when(core == 0)
    def _():
        for cp in far_push:
            cp.start()

    own_push.start()
    sm_push = push(sm.at[core], sm.at[core], sems.one(), sems.one(), sib)
    sm_push.start()
    qk_push = [
        push(qkv.at[0, :, qo], wqk.at[core, :, pl.ds(0, H)], sems.one(), sems.one(), sib),
        push(qkv.at[0, :, ko], wqk.at[core, :, pl.ds(H, H)], sems.one(), sems.one(), sib),
    ]
    for cp in qk_push:
        cp.start()
    v_push = push(qkv.at[0, :, pl.ds(2 * D, H)], wv.at[0], sems.one(), sems.one(), sib)

    @pl.when(core == 0)
    def _():
        v_push.start()

    rest_push = [
        push(wo.at[0, pl.ds(pl.multiple_of((1 - core) * H, H), H), :], wout.at[core], sems.one(), sems.one(), sib),
        push(fc.at[0, :, pl.ds(pl.multiple_of((1 - core) * FH, 128), FH)], wfc.at[core], sems.one(), sems.one(), sib),
        push(proj.at[0, pl.ds(pl.multiple_of((1 - core) * FH, FH), FH), :], wproj.at[core], sems.one(), sems.one(), sib),
    ]

    xh_sends = {}

    def route_block(l, turn, blk):
        p = pos(blk)
        for n in range(N - 1):
            part = xall.at[l, pl.ds(pl.multiple_of(p * T + core * T2, T2), T2), :]
            s, rsem = sems.one(), sems.one()
            cp = push(part, part, s, rsem, ahead[n])
            src = behind[n]
            slo = src + row * (C - 1 - 2 * src)
            sp = slo + blk * (C - 1 - 2 * slo)
            got = xall.at[l, pl.ds(pl.multiple_of(sp * T + core * T2, T2), T2), :]
            other = xall.at[l, pl.ds(pl.multiple_of(sp * T + (1 - core) * T2, T2), T2), :]
            come = push(got, got, s, rsem, ahead[n])
            fs, fr = sems.one(), sems.one()
            onward = push(got, got, fs, fr, sib)
            arrive = push(other, other, fs, fr, sib)
            xh_sends[(l, turn, n)] = (cp, come, onward, arrive, sp)

    def leave(l, turn):
        for n in range(N - 1):
            xh_sends[(l, turn, n)][0].start()

    def normed_block(l, turn, blk, values):
        xall[l, rows_at(pos(blk)), :] = layer_norm(values, sm[l, 0:1, :D], sm[l, 1:2, :D]).astype(BF16)
        route_block(l, turn, blk)
        leave(l, turn)

    def own_products(l, blk):
        p = pos(blk)
        xh = xall[l, rows_at(p), :]
        both = mm(xh, wqk[l])
        q[l, blk * T : (blk + 1) * T, :] = both[:, :H].astype(BF16)
        k[l, rows_at(p), :] = both[:, H:].astype(BF16)

    def value_products(l, p):
        src = l * core
        v[l, rows_at(p), :] = mm(xall[src, rows_at(p), :], wv[src]).astype(BF16)

    def key_products(l, p):
        k[l, rows_at(p), :] = mm(xall[l, rows_at(p), :], wqk[l, :, H:]).astype(BF16)

    def arrivals(l, turn):
        for n in range(N - 1):
            cp, come, onward, arrive, sp = xh_sends[(l, turn, n)]
            come.wait_recv()
            onward.start()

    def foreign_products(l, turn):
        for n in range(N - 1):
            cp, come, onward, arrive, sp = xh_sends[(l, turn, n)]
            arrive.wait_recv()
            key_products(l, sp)
            value_products(l, sp)

    act_push = [push(act.at[0, pl.ds(b * T, T), :], act_in_o.at[pl.ds(b * T, T), :], sems.one(), sems.one(), across) for b in range(2)]
    gm_push = [push(e.at[1, b], gm_in_o.at[b], sems.one(), sems.one(), across) for b in (row, 1 - row)]

    @pl.when(core == 0)
    def _():
        e_load.wait()

    @pl.when(core == 1)
    def _():
        own_come.wait_recv()

    sm_push.wait()
    blk = row
    r[0, pl.ds(pl.multiple_of(blk * T, T), T), :] = e[0, blk]
    normed_block(0, 0, blk, e[0, blk].astype(F32))

    @pl.when(core == 0)
    def _():
        loads[0].wait()
        loads[1].wait()
        v_shared.wait()

    @pl.when(core == 1)
    def _():
        for cp in qk_push:
            cp.wait_recv()
        v_push.wait_recv()

    def own_products_dynamic(l, blk):
        p = pos(blk)
        both = mm(xall[l, rows_at(p), :], wqk[l])
        q[l, pl.ds(pl.multiple_of(blk * T, T), T), :] = both[:, :H].astype(BF16)
        k[l, rows_at(p), :] = both[:, H:].astype(BF16)
        value_products(l, p)

    own_products_dynamic(0, blk)

    @pl.when(core == 1)
    def _():
        e_load.wait()

    @pl.when(core == 0)
    def _():
        own_come.wait_recv()

    when(jnp.logical_not(owner), gm_push[0].start)

    for n, cp in enumerate(seg_push):
        cp.wait()
    kseg = jnp.concatenate([seg[n] for n in range(C)], axis=1)
    kseg_o[...] = kseg
    for blk in range(2):
        rows = slice(blk * T, (blk + 1) * T)
        qpos = pos(blk) * T + lax.broadcasted_iota(jnp.int32, (T, L), 0)
        kpos = lax.broadcasted_iota(jnp.int32, (T, L), 1)
        allowed = (kpos <= qpos) & (kseg == column(seg[pos(blk)]))
        bias[rows, :] = jnp.where(allowed, 0.0, MASKED)

    blk = 1 - row

    route_block(0, 1, blk)
    for h in range(2):
        @pl.when(core == 0)
        def _():
            far_come[h].wait_recv()
            fwd_push[h].start()

        @pl.when(core == 1)
        def _():
            fwd_come[h].wait_recv()

        values = e[0, blk, h * T2 : (h + 1) * T2, :]
        r[0, pl.ds(pl.multiple_of(blk * T + h * T2, T2), T2), :] = values
        xall[0, pl.ds(pl.multiple_of(pos(blk) * T + h * T2, T2), T2), :] = layer_norm(
            values.astype(F32), sm[0, 0:1, :D], sm[0, 1:2, :D]).astype(BF16)

        @pl.when(core == h)
        def _():
            leave(0, 1)

    @pl.when(core == 1)
    def _():
        for cp in far_push:
            cp.start()

    own_products_dynamic(0, blk)

    def at_core(here, ours, theirs):
        @pl.when(here)
        def _():
            for cp in ours:
                cp.wait()

        @pl.when(jnp.logical_not(here))
        def _():
            for cp in theirs:
                cp.wait_recv()

    def branch(l, blk):
        rows = slice(blk * T, (blk + 1) * T)
        part = mm(o[l, rows, :], wout[l])
        hr[l, rows, :] = part
        br_s[l, rows, :] = part.astype(BF16)
        cp = push(br_s.at[l, rows, :], br_r.at[l, rows, :], sems.one(), sems.one(), sib)
        cp.start()
        return cp

    def hidden_units(l, blk, come):
        rows = slice(blk * T, (blk + 1) * T)
        come.wait_recv()
        hidden = r[l, rows, :].astype(F32) + hr[l, rows, :] + br_r[l, rows, :].astype(F32)
        hr[l, rows, :] = hidden
        normed2 = layer_norm(hidden, sm[l, 2:3, :D], sm[l, 3:4, :D]).astype(BF16)
        hh[l, rows, :] = normed2
        if l == 0 and blk == 0:
            at_core(core == 0, loads[3:5], rest_push[1:3])
        mine = pl.ds(pl.multiple_of(core * FH, 128), FH)
        u = mm(normed2, wfc[l]) + sm[l, 4:5, mine]
        a, slope = gelu_both(u)
        gp[l, rows, :] = slope.astype(BF16)
        act[l, rows, :] = a.astype(BF16)
        if l == 0:
            when(jnp.logical_not(owner), act_push[blk].start)

    def feed_out(l, blk):
        rows = slice(blk * T, (blk + 1) * T)
        part = mm(act[l, rows, :], wproj[l])
        y[rows, :] = part
        ml_s[l, rows, :] = part.astype(BF16)
        cp = push(ml_s.at[l, rows, :], ml_r.at[l, rows, :], sems.one(), sems.one(), sib)
        cp.start()
        return cp

    def block_out(l, blk, come):
        rows = slice(blk * T, (blk + 1) * T)
        come.wait_recv()
        out = hr[l, rows, :] + y[rows, :] + ml_r[l, rows, :].astype(F32)
        if l == 0:
            sent = out.astype(BF16)
            r[1, rows, :] = sent
            normed_block(1, blk, blk, sent.astype(F32))
        else:
            y[rows, :] = out
            yb[rows, :] = out.astype(BF16)

    def save_weights(l):
        wvt[l] = jnp.transpose(wv[l * core])
        save(wqk.at[l], watt_o.at[l, pl.ds(0, D)])
        save(wout.at[l], watt_o.at[l, pl.ds(D, H)])
        save(wvt.at[l], watt_o.at[l, pl.ds(D + H, H)])
        save(wfc.at[l], wfc_o.at[l])
        save(wproj.at[l], wproj_o.at[l])

    def middle(l):
        attention_block(l, 0, T, L // 2, pairs, q, k, v, o, lse, bias)
        if l == 0:
            at_core(core == 0, loads[2:3], rest_push[0:1])
        else:
            arrivals(1, 1)
        sends = [branch(l, 0)]
        if l == 1:
            foreign_products(1, 1)
        if l == 0:
            @pl.when(core == 1)
            def _():
                for h in range(2):
                    far_come[h].wait_recv()
                    fwd_push[h].start()
        attention_block(l, 1, T, L, pairs, q, k, v, o, lse, bias)
        sends.append(branch(l, 1))
        if l == 0:
            @pl.when(core == 0)
            def _():
                for cp in fwd_come:
                    cp.wait_recv()

            when(jnp.logical_not(owner), gm_push[1].start)
        save(q.at[l], q_o.at[l])
        save(k.at[l], k_o.at[l])
        save(v.at[l], v_o.at[l])
        save(o.at[l], o_o.at[l])
        save(lse.at[l], lse_o.at[l])
        save(xall.at[l], xall_o.at[l])
        hidden_units(l, 0, sends[0])
        mlps = [feed_out(l, 0)]
        hidden_units(l, 1, sends[1])
        save(hr.at[l], hr_o.at[l])
        save(hh.at[l], hh_o.at[l])
        save(gp.at[l], gp_o.at[l])
        save(act.at[l], act_o.at[l])
        block_out(l, 0, mlps[0])
        mlps.append(feed_out(l, 1))
        if l == 0:
            at_core(core == 1, loads[0:2] + [v_fresh], qk_push)
            own_products(1, 0)
            value_products(1, pos(0))
        block_out(l, 1, mlps[1])
        if l == 0:
            own_products(1, 1)
            value_products(1, pos(1))
            at_core(core == 1, loads[2:5], rest_push)
            save_weights(0)
            save_weights(1)
        return sends + mlps

    for turn in range(2):
        arrivals(0, turn)
    for turn in range(2):
        foreign_products(0, turn)

    for cp in rest_push:
        cp.start()
    pair_sends = middle(0)
    save(r, r_o)
    arrivals(1, 0)
    foreign_products(1, 0)

    save(e.at[1], gy_o)
    save(sm, sm_o)
    pair_sends += middle(1)
    save(y, y_o)
    save(yb, yb_o)

    def crossed():
        for cp in act_push + gm_push:
            cp.wait_recv()

    def crossing():
        for cp in act_push + gm_push:
            cp.wait_send()

    when(owner, crossed)
    when(jnp.logical_not(owner), crossing)
    own_push.wait_send()
    for cp in far_push + fwd_push + qk_push + rest_push + pair_sends:
        cp.wait_send()

    @pl.when(core == 0)
    def _():
        v_push.wait_send()

    for cp, come, onward, arrive, sp in xh_sends.values():
        cp.wait_send()
        onward.wait_send()
    for cp in saves:
        cp.wait()


def forward_pass(C, m, ends, segs, g1, b1, g2, b2, qkv, wo, fc, fcb, proj, shared):
    T, D, F = ends.shape[2], ends.shape[3], fc.shape[2]
    N, L, H, FH = C // 2, C * T, D // 2, F // 2
    R, pairs = 2 * T, D // 256
    S = jax.ShapeDtypeStruct
    outs = [S((2, L, D), BF16), S((2, R, H), BF16), S((2, L, H), BF16), S((2, L, H), BF16), S((2, R, H), BF16),
            S((2, R, 128), F32), S((2, R, D), BF16), S((2, R, D), F32), S((2, R, D), BF16), S((2, R, FH), BF16),
            S((2, R, FH), BF16), S((R, D), F32), S((R, D), BF16), S((2, T, D), BF16), S((2, 8, F), F32), S((2, 2 * D, D), BF16),
            S((2, D, FH), BF16), S((2, FH, D), BF16), S((R, FH), BF16), S((2, T, D), BF16), S((1, L), jnp.int32)]
    V = pltpu.VMEM
    scratch = [V((2, 2, T, D), BF16), V((C, 1, T), jnp.int32), V((2, 1, T), jnp.int32), V((2, 8, F), F32), V((2, D, D), BF16), V((2, D, H), BF16),
               V((2, H, D), BF16), V((2, D, FH), BF16), V((2, FH, D), BF16), V((2, L, D), BF16), V((2, R, H), BF16),
               V((2, L, H), BF16), V((2, L, H), BF16), V((2, R, H), BF16), V((2, R, 128), F32), V((2, R, D), BF16),
               V((2, R, D), F32), V((2, R, D), BF16), V((2, R, FH), BF16), V((2, R, FH), BF16), V((R, D), F32),
               V((R, D), BF16), V((2, H, D), BF16), V((R, L), F32), V((2, R, D), BF16), V((2, R, D), BF16), V((2, R, D), BF16), V((2, R, D), BF16),
               pltpu.SemaphoreType.DMA((90 + 16 * (N - 1) + 2 * (C - 1),))]
    return pl.pallas_call(
        functools.partial(forward_kernel, C, m, T, D, F),
        in_specs=[HBM, VM, VM, VM, VM, VM, HBM, HBM, HBM, VM, HBM, HBM],
        out_specs=[HBM] * 20 + [VM],
        out_shape=outs,
        scratch_shapes=scratch,
        compiler_params=pltpu.CompilerParams(collective_id=0, has_side_effects=True, vmem_limit_bytes=VMEM_LIMIT),
        name="forward_pass",
    )(ends, segs, g1, b1, g2, b2, qkv, wo, fc, fcb, proj, shared)


WHOLE, SIDED, SIDE_STEP = 0, 1, 2
JOBS = ("P0", "P1", "P2", "F0", "F1", "F2", "O", "Q", "K", "V")
PROJ_AT = (3, 3)
POLLS = (
    (), (), (113,), (), (), (), (), (114,), (), (13, 113, 115), (), (13,), (), (117,), (14, 113, 111, 114, 110),
    (15, 112, 17, 13, 113, 14, 114), (10, 110), (11, 111, 115, 13), (14, 114), (), (113,),
    (10, 103, 118, 110, 12, 112, 11), (14,), (13, 111, 114, 10, 15, 115), (12, 105, 112),
    (11, 104, 111, 14, 15, 115, 18, 12, 112), (3, 116, 11), (15, 12), (118,), (), (5, 103, 101, 119, 115, 100, 4),
    (18, 104, 102, 118, 3, 103, 16, 108, 15),
)
TAIL = (
    19, 1, 0, 105, 18, 3, 4, 103, 116, 106, 2, 101, 104, 102, 5, 119, 118, 110, 105, 8,
    108, 100, 3, 1, 4, 16, 101, 2, 103, 19, 107, 18, 109, 104, 5, 102, 10, 118, 0, 116,
    6, 119, 105, 1, 8, 4, 3, 101, 2, 106, 104, 117, 18, 102, 16, 19, 116, 5, 7, 119,
    105, 1, 4, 108, 100, 9, 109, 6, 2, 17, 107, 16, 116, 19, 5, 119, 8, 108, 117, 9,
    106, 109, 7, 0, 100, 16, 19, 8, 108, 17, 117, 107, 0, 6, 106, 9, 109, 8, 17, 117,
    7, 107, 6, 106, 9, 109, 17, 7, 107, 6, 9, 7,
)


class Job:
    def __init__(self, env, buf, lead, cols, order, sided, land, credits, active, earlier, prior):
        self.env, self.buf, self.lead, self.cols = env, buf, lead, cols
        self.sided, self.land, self.credits, self.active, self.prior = sided, land, credits, active, prior
        self.copies = {}
        self.earlier = earlier
        self.bits = list(range(env.m - 2 if sided else env.m - 1, -1, -1))
        self.fixed, self.z_done, self.steps, self.at, self.flying = {}, False, [], 0, False
        self.used, self.own_sems = 0, []
        if sided == SIDE_STEP:
            self.steps.append(("side", None, None))
        for item in order:
            if item == "z":
                for s in range(1, env.C):
                    self.steps.append(("z", s, dict(self.fixed)))
                self.z_done = True
            else:
                self.steps.append(("bit", item, (dict(self.fixed), self.z_done)))
                self.fixed[item] = env.bit(item)
        self.plans = [self.plan(i) for i in range(len(self.steps))]

    def view(self, fixed, zat):
        at = tuple(self.lead) + tuple(fixed.get(b, slice(None)) for b in self.bits)
        return at + (slice(None) if zat is None else zat, slice(None), self.cols)

    def plan(self, i):
        env = self.env
        kind, what, state = self.steps[i]
        moves = []
        if kind == "side":
            other = env.dp_xor(env.m - 1)
            moves.append((env.bit(env.m - 1) != env.core, self.view({}, None), other, env.bit(env.m - 1) == env.core,
                          self.view({}, None), other))
            return [self.bind(move, self.land[i]) for move in moves]
        active = self.active if not self.sided else (env.bit(env.m - 1) == env.core)
        if kind == "bit":
            fixed, z_done = state
            zat = env.z if z_done else None
            other = env.dp_xor(what)
            mine = env.bit(what)
            moves.append((active, self.view({**fixed, what: 1 - mine}, zat), other, active,
                          self.view({**fixed, what: mine}, zat), other))
            return [self.bind(move, self.land[i]) for move in moves]
        s, C, z = what, env.C, env.z
        zm = C - 1 - z
        for side, (p, sign) in enumerate(((z, 1), (zm, -1))):
            out_at = z + sign * (C - s)
            in_at = z + sign * (C - s - 1)
            moves.append((both(active, p < s), self.view(state, out_at), env.line(z + sign),
                          both(active, both(p >= 1, p <= s)), self.view(state, in_at), env.line(z - sign)))
        return [self.bind(move, self.land[i].at[side]) for side, move in enumerate(moves)]

    def bind(self, move, slot):
        send_if, src, to, recv_if, dst, source = move
        env = self.env
        if self.prior is None:
            sem_s, sem_r = env.sems.one(), env.sems.one()
            self.own_sems.append((sem_s, sem_r))
        else:
            sem_s, sem_r = self.prior.own_sems[self.used]
        credit = self.credits.at[self.used]
        self.used += 1
        return send_if, src, to, recv_if, dst, source, slot, sem_s, sem_r, credit

    def send(self, i):
        for n, (send_if, src, to, recv_if, dst, source, slot, sem_s, sem_r, credit) in enumerate(self.plans[i]):
            cp = self.copies[(i, n)] = push(self.buf.at[src], slot, sem_s, sem_r, to)

            def go():
                if self.prior is not None:
                    def empty():
                        pl.semaphore_wait(credit, 1)
                        self.prior.copies[(i, n)].wait_send()

                    when(self.earlier, empty)
                cp.start()

            when(send_if, go)
            if self.prior is not None:
                self.env.sent.append((send_if, cp))

    def take(self, i):
        for send_if, src, to, recv_if, dst, source, slot, sem_s, sem_r, credit in self.plans[i]:
            cp = push(slot, slot, sem_s, sem_r, to)

            def got():
                cp.wait_recv()
                self.buf[dst] = self.buf[dst] + slot[...]
                if self.prior is None:
                    pl.semaphore_signal(credit, inc=1, device_id=source, device_id_type=MESH)

            when(recv_if, got)

    def send_next(self):
        if not self.flying and self.at < len(self.steps):
            self.send(self.at)
            self.flying = True

    def take_next(self):
        if self.flying:
            self.take(self.at)
            self.at, self.flying = self.at + 1, False

    def finish(self):
        while self.at < len(self.steps):
            self.send_next()
            self.take_next()

    def own(self):
        return self.view(self.fixed, self.env.z)


def both(a, b):
    if a is True:
        return b
    if b is True:
        return a
    return jnp.logical_and(a, b)


def when(condition, fn):
    if condition is True:
        fn()
    else:
        pl.when(condition)(fn)


class Env:
    def __init__(self, C, m, core, dp, z, sems):
        self.C, self.m, self.core, self.dp, self.z, self.sems, self.sent = C, m, core, dp, z, sems, []

    def bit(self, b):
        return lax.rem(lax.div(self.dp, 1 << b), 2)

    def dp_xor(self, b):
        return (self.core, self.dp + (1 << b) * (1 - 2 * self.bit(b)), self.z)

    def line(self, z):
        return (self.core, self.dp, z)


def job_table(m):
    xs, ys = list(range(m)), list(range(m - 1, -1, -1))
    rest = list(range(m - 1))
    xz, yz = xs + ["z"], ys + ["z"]
    return {
        "P0": ("gproj", (0, 3), ["z"] + rest, SIDED), "P1": ("gproj", (1, 3), rest + ["z"], SIDED),
        "P2": ("gproj", (2, 3), rest + ["z"], SIDED),
        "F0": ("gfc", (0, 3), xs[:1] + ["z"] + xs[1:], WHOLE), "F1": ("gfc", (1, 3), xz, WHOLE), "F2": ("gfc", (2, 3), yz, WHOLE),
        "O": ("gout", (0, 1), rest + ["z"], SIDE_STEP),
        "Q": ("gq", (0, 1), xz, WHOLE), "K": ("gk", (0, 1), yz, WHOLE), "V": ("gv", (0, 1), yz, WHOLE),
    }


def grad_shapes(C, m, D, F):
    H, FH, J = D // 2, F // 2, C << m
    full, side = (2,) * m + (C,), (2,) * (m - 1) + (C,)
    return {"gproj": side + (F // J, D), "gfc": full + (D // J, FH), "gout": side + (D // J, D),
            "gq": full + (D // J, H), "gk": full + (D // J, H), "gv": full + (D // J, H)}


def landing_shapes(C, m, D, F):
    shapes = grad_shapes(C, m, D, F)
    result = {}
    for name, (buf, (at, parts), order, sided) in job_table(m).items():
        shape = list(shapes[buf])
        shape[-1] //= parts
        n = m - 1 if sided else m
        lead = {b: 2 for b in range(n)}
        tail = [shape[-2], shape[-1]]
        zdim = [C]
        steps = []
        if sided == SIDE_STEP:
            steps.append(tuple([2] * n + zdim + tail))
        for item in order:
            if item == "z":
                zdim = []
                for s in range(1, C):
                    steps.append(tuple([2] + [2] * len(lead) + tail))
            else:
                lead.pop(item)
                steps.append(tuple([2] * len(lead) + zdim + tail))
        result[name] = steps
    return result


def norm_grad(values, gain, grad):
    unit, rstd = unit_norm(values)
    scaled = grad * gain
    m1 = jnp.mean(scaled, axis=-1, keepdims=True)
    m2 = jnp.mean(scaled * unit, axis=-1, keepdims=True)
    back = rstd * (scaled - m1 - unit * m2)
    return back, jnp.sum(grad * unit, axis=0, keepdims=True), jnp.sum(grad, axis=0, keepdims=True)


def attention_back_pair(i, T, L, q, k, v, o, lse, goa, bias, dq, dk, dv, dv_at):
    cols = slice(i * 128, (i + 1) * 128)
    lane = lax.broadcasted_iota(jnp.int32, (T, 128), 1)
    scale = jnp.asarray(HEAD**-0.5, BF16)
    totals = None
    for blk in (1, 0):
        rows = slice(blk * T, (blk + 1) * T)
        keys = L if blk else L // 2
        q2, go2 = q[rows, cols] * scale, goa[rows, cols]
        prod = go2.astype(F32) * o[rows, cols].astype(F32)
        k2, v2 = k[:keys, cols], v[:keys, cols]
        dqs, dks, dvs = [], None, None
        for h in range(2):
            sel = (lane >= 64) == (h == 1)
            qh = jnp.where(sel, q2, jnp.zeros_like(q2))
            goh = jnp.where(sel, go2, jnp.zeros_like(go2))
            delta = jnp.sum(jnp.where(sel, prod, 0.0), axis=-1, keepdims=True)
            s = mm_nt(qh, k2) + bias[rows, :keys].astype(F32)
            prob = jnp.exp(s - lse[rows, 2 * i + h : 2 * i + h + 1])
            gp = mm_nt(goh, v2)
            gs = (prob * (gp - delta)).astype(BF16)
            dqs.append(mm(gs, k2))
            one_k = mm_tn(gs, qh)
            one_v = mm_tn(prob.astype(BF16), goh)
            dks = one_k if dks is None else dks + one_k
            dvs = one_v if dvs is None else dvs + one_v
        dq[rows, cols] = (jnp.where(lane < 64, dqs[0], dqs[1]) * HEAD**-0.5).astype(BF16)
        if blk:
            totals = (dks, dvs)
        else:
            dk[:keys, cols] = (totals[0][:keys] + dks).astype(BF16)
            dk[keys:, cols] = totals[0][keys:].astype(BF16)
            dv[dv_at, :keys, cols] = (totals[1][:keys] + dvs).astype(BF16)
            dv[dv_at, keys:, cols] = totals[1][keys:].astype(BF16)


LOADED = ("gp", "act", "hh", "hr", "o", "q", "k", "v", "lse", "xall", "r")


def backward_kernel(C, m, T, D, F, fused, names_in, *refs):
    n_in = len(names_in)
    hbm = dict(zip(names_in, refs[:n_in]))
    outs, (vm, dma, credits) = refs[n_in:-3], refs[-3:]
    ends_o, small_o = outs[:2]
    core, dp, z = lax.axis_index(SECTION), lax.axis_index(DP), lax.axis_index(CTX)
    N, L, H, FH = C // 2, C * T, D // 2, F // 2
    row = lax.div(z, N)
    lo = z + row * (C - 1 - 2 * z)
    hi = C - 1 - lo
    base = row * N
    pairs = H // 128
    sems = Sems(dma)
    env = Env(C, m, core, dp, z, sems)
    sib = (1 - core, dp, z)
    mirror = (core, dp, C - 1 - z)
    pos = lambda blk: lo + blk * (hi - lo)
    block = lambda at: pl.ds(pl.multiple_of(at * T, T), T)
    other_nodes = [base + lax.rem(z - base + n, N) for n in range(1, N)]
    sent = env.sent
    loads = {}

    def load(name, l, src=None, dst=None):
        cp = pltpu.make_async_copy(hbm[name].at[l] if src is None else src, vm[name] if dst is None else dst, sems.one())
        cp.start()
        loads[(name, l)] = cp

    def need(*names):
        for name in names:
            loads[name].wait()

    def pushed(src, dst, to, condition=True, until=sent):
        cp = push(src, dst, sems.one(), sems.one(), to)
        when(condition, cp.start)
        until.append((condition, cp))
        return cp

    load("gy", 1, hbm["gy"].at[0], vm["gm"].at[0])
    load("gy", 0, hbm["gy"].at[1], vm["gm"].at[1])
    load("wproj", 1, dst=vm["wa"])
    load("gp", 1)
    load("wfc", 1)
    load("act", 1)
    load("hh", 1)
    load("hr", 1)
    load("sm", 0, hbm["sm"], vm["sm"])
    for name in ("o", "q", "k", "v", "lse", "xall", "r"):
        load(name, 1)
    y_keep = pltpu.make_async_copy(hbm["y"].at[block(row)], ends_o.at[0, row], sems.one())
    when(core == 1, y_keep.start)

    kseg = hbm["kseg"]
    for blk in range(2):
        rows = slice(blk * T, (blk + 1) * T)
        qpos = pos(blk) * T + lax.broadcasted_iota(jnp.int32, (T, L), 0)
        kpos = lax.broadcasted_iota(jnp.int32, (T, L), 1)
        mine = kseg[0:1, 0:T]
        for n in range(1, C):
            mine = jnp.where(pos(blk) == n, kseg[0:1, n * T : (n + 1) * T], mine)
        allowed = (kpos <= qpos) & (kseg[...] == column(mine))
        vm["bias"][rows, :] = jnp.where(allowed, 0.0, MASKED).astype(BF16)

    greet([sib] + [env.line(lax.rem(z + n, C)) for n in range(1, C)] + [env.dp_xor(b) for b in range(m)])

    y_push = pushed(hbm["yb"].at[block(1 - row)], vm["far"], mirror, core == 1)
    top = env.bit(m - 1) == core
    aside = jnp.logical_not(top)
    across = env.dp_xor(m - 1)
    act_push = pushed(hbm["act"].at[1], vm["act_in"], across, aside)
    gm_in_load = pltpu.make_async_copy(hbm["gm_in"], vm["gm_in"].at[1], sems.one())
    act_in_load = pltpu.make_async_copy(hbm["act_in"], vm["act_in"], sems.one())
    when(top, gm_in_load.start)
    gm_push = push(vm["gm"], vm["gm_in"].at[0], sems.one(), sems.one(), across)

    table = job_table(m)
    jobs = {}

    def start(name, l):
        if not fused:
            return
        buf, (at, parts), order, sided = table[name]
        width = vm[buf].shape[-1] // parts
        earlier = True if name != "V" else core == 1
        active = True if l == 0 else earlier
        jobs[(name, l)] = Job(env, vm[buf], (l,), slice(at * width, (at + 1) * width), order, sided, vm["land"][name],
                              credits[name], active, earlier, jobs.get((name, 1)))

    def move(code):
        job = jobs.get((JOBS[code % 10], code // 10 % 10)) if fused else None
        if job is not None:
            job.send_next() if code >= 100 else job.take_next()

    gm, gp, go, ghh, wa, wfc = vm["gm"], vm["gp"], vm["go"], vm["ghh"], vm["wa"], vm["wfc"]
    sm, sg = vm["sm"], vm["sg"]

    def put(buf, l, cols, value):
        shape = vm[buf].shape[1:-1] + (value.shape[-1],)
        vm[buf][(l,) + (slice(None),) * (len(shape) - 1) + (cols,)] = value.astype(BF16).reshape(shape)

    polls = iter(POLLS)

    def poll():
        for code in next(polls):
            move(code)

    def layer_back(l):
        again = []

        def proj_phase():
            def proj_grad():
                if l == 1:
                    act_push.wait_recv()
                    gm_in_load.wait()
                else:
                    act_in_load.wait()
                    gm_push.wait_recv()
                third = D // 3
                for n in range(3):
                    cols = slice(n * third, (n + 1) * third)
                    total = mm_tn(vm["act_in"][...], vm["gm_in"][l, :, :, cols].reshape(2 * T, third))
                    for blk in range(2):
                        total += mm_tn(vm["act"][blk * T : (blk + 1) * T, :], gm[blk, :, cols])
                    put("gproj", l, cols, total)

            need(("act", l))
            when(top, proj_grad)
            for n in range(3):
                start("P%d" % n, l)
            if l == 1:
                load("act", 0)
                when(top, act_in_load.start)

        need(("wproj", l), ("gp", l))
        bias_sum = None
        for blk in range(2):
            rows = slice(blk * T, (blk + 1) * T)
            if l == 1:
                need(("gy", 1 - blk))
                go[rows, :] = gm[blk].astype(F32)
            gu = (gp[rows, :].astype(F32) * mm_nt(gm[blk], wa[...])).astype(BF16)
            gp[rows, :] = gu
            part = jnp.sum(gu.astype(F32), axis=0, keepdims=True)
            bias_sum = part if bias_sum is None else bias_sum + part
        sg[l, 4:5, :] = bias_sum
        load("watt", l, dst=wa)
        poll()
        need(("wfc", l))
        shares = []
        for blk in range(2):
            rows = slice(blk * T, (blk + 1) * T)
            part = mm_nt(gp[rows, :], wfc[...])
            ghh[rows, :] = part
            vm["a_s"][rows, :] = part.astype(BF16)
            shares.append(pushed(vm["a_s"].at[rows, :], vm["a_r"].at[rows, :], sib, until=[]))
        if l == 1:
            load("wfc", 0)
        poll()
        need(("hh", l))
        third = FH // 3
        for i in (0, 1, 2):
            cols = slice(i * third, (i + 1) * third)
            put("gfc", l, cols, mm_tn(vm["hh"][...], gp[:, cols]))
            start("F%d" % i, l)
            poll()
        if l == 1:
            load("hh", 0)
            load("gp", 0)
        need(("hr", l), ("watt", l))
        if l == 1:
            need(("sm", 0))
        sums = None
        for blk in range(2):
            rows = slice(blk * T, (blk + 1) * T)
            shares[blk].wait_recv()
            grad = ghh[rows, :] + vm["a_r"][rows, :].astype(F32)
            back, gain_sum, bias_sum = norm_grad(vm["hr"][rows, :], sm[l, 2:3, :D], grad)
            total = go[rows, :] + back
            go[rows, :] = total
            low = total.astype(BF16)
            vm["gb"][rows, :] = low
            vm["goa"][rows, :] = mm_nt(low, wa[D : D + H, :]).astype(BF16)
            sums = (gain_sum, bias_sum) if sums is None else (sums[0] + gain_sum, sums[1] + bias_sum)
        sg[l, 2:3, :D] = sums[0]
        sg[l, 3:4, :D] = sums[1]
        poll()
        if l == 1:
            load("hr", 0)
        need(("o", l))
        put("gout", l, slice(0, D), mm_tn(vm["o"][...], vm["gb"][...]))
        start("O", l)
        poll()
        need(("q", l), ("k", l), ("v", l), ("lse", l))
        for i in range(pairs):
            attention_back_pair(i, T, L, vm["q"], vm["k"], vm["v"], vm["o"], vm["lse"], vm["goa"], vm["bias"], vm["dq"],
                                vm["dk"], vm["dv"], l)
            if i == PROJ_AT[l]:
                proj_phase()
            poll()
        if l == 1:
            for name in ("o", "q", "k", "v", "lse"):
                load(name, 0)
        else:
            def merge():
                vm["dv"][0] = (vm["dv"][0].astype(F32) + vm["dv"][1].astype(F32)).astype(BF16)

            when(core == 0, merge)
        dk, dv, dq = vm["dk"], vm["dv"], vm["dq"]

        def key_part(at):
            part_v = dv[l, block(at), :]
            if l == 1:
                part_v = jnp.where(core == 1, part_v, jnp.zeros_like(part_v))
            return mm_nt(dk[block(at), :], wa[:D, H:]) + mm(part_v, wa[D + H :, :])

        crossing, gives = [], []
        for n, node in enumerate(other_nodes):
            dlo = node + row * (C - 1 - 2 * node)
            dhi = C - 1 - dlo
            vm["fs_s"][n] = key_part(dlo + (1 - core) * (dhi - dlo)).astype(BF16)
            gives.append(pushed(vm["fs_s"].at[n], vm["fs_r"].at[n], sib, until=again))
        for n, node in enumerate(other_nodes):
            dlo = node + row * (C - 1 - 2 * node)
            keep = key_part(dlo + core * (C - 1 - 2 * dlo))
            gives[n].wait_recv()
            vm["fx_s"][n] = (keep + vm["fs_r"][n].astype(F32)).astype(BF16)
            crossing.append(pushed(vm["fx_s"].at[n], vm["fx_r"].at[l, n], (core, dp, node), until=again))
        poll()
        for blk in range(2):
            rows = slice(blk * T, (blk + 1) * T)
            ghh[rows, :] = key_part(pos(blk)) + mm_nt(dq[rows, :], wa[:D, :H])
        for cp in shares:
            cp.wait_send()
        early = pl.ds(pl.multiple_of((1 - core) * T, T), T)
        late = pl.ds(pl.multiple_of(core * T, T), T)
        vm["a_s"][early, :] = ghh[early, :].astype(BF16)
        shares = [pushed(vm["a_s"].at[early, :], vm["b_r"].at[early, :], sib, until=again)]
        if l == 1:
            load("wproj", 0, dst=wa)
        poll()
        need(("xall", l))
        xall = vm["xall"]
        put("gk", l, slice(0, H), mm_tn(xall[...], dk[...]))
        start("K", l)
        poll()
        put("gq", l, slice(0, H), mm_tn(xall[block(lo), :], dq[:T, :]) + mm_tn(xall[block(hi), :], dq[T:, :]))
        start("Q", l)
        poll()
        put("gv", l, slice(0, H), mm_tn(xall[...], dv[l]))
        start("V", l)
        if PROJ_AT[l] == 3:
            proj_phase()
        poll()
        if l == 1:
            load("xall", 0)
        need(("r", l))
        for n in range(N - 1):
            crossing[n].wait_recv()
            ghh[late, :] += vm["fx_r"][l, n].astype(F32)
        vm["a_s"][late, :] = ghh[late, :].astype(BF16)
        shares.append(pushed(vm["a_s"].at[late, :], vm["b_r"].at[late, :], sib, until=again))
        for cp in shares:
            cp.wait_recv()
        sums = None
        for blk in range(2):
            rows = slice(blk * T, (blk + 1) * T)
            grad = ghh[rows, :] + vm["b_r"][rows, :].astype(F32)
            back, gain_sum, bias_sum = norm_grad(vm["r"][rows, :].astype(F32), sm[l, 0:1, :D], grad)
            total = go[rows, :] + back
            go[rows, :] = total
            if l == 1:
                gm[blk] = total.astype(BF16)
            sums = (gain_sum, bias_sum) if sums is None else (sums[0] + gain_sum, sums[1] + bias_sum)
        sg[l, 0:1, :D] = sums[0]
        sg[l, 1:2, :D] = sums[1]
        poll()
        if l == 1:
            load("r", 0)
            when(aside, gm_push.start)
            sent.append((aside, gm_push))
        for condition, cp in again:
            when(condition, cp.wait_send)

    layer_back(1)
    layer_back(0)

    keep = pl.ds(pl.multiple_of(row * T, T), T)
    away = pl.ds(pl.multiple_of((1 - row) * T, T), T)
    vm["gb"][:T, :] = go[away, :].astype(BF16)
    x_push = pushed(vm["gb"].at[pl.ds(0, T), :], vm["far"], mirror, core == 0)
    x_keep = pltpu.make_async_copy(go.at[keep, :], ends_o.at[0, row], sems.one())
    when(core == 0, x_keep.start)

    sv, sv_r = vm["sv"], vm["sv_r"]
    sv[0] = jnp.zeros_like(sv[0])
    sv[0, 0:4, :] = sg[core, 0:4, :]
    sv[0, 4:5, :] = sg[0, 4:5, :]
    sv[0, 5:6, :] = sg[1, 4:5, :]
    around = [env.dp_xor(b) for b in range(m)]
    b = 1
    while b < C:
        around.append(env.line(z + b * (1 - 2 * lax.rem(lax.div(z, b), 2))))
        b *= 2
    small_at = [0]
    small_cp = [pushed(sv.at[0], sv_r.at[0], around[0])]

    def small_step():
        i = small_at[0]
        small_cp[0].wait_recv()
        sv[i + 1] = sv[i] + sv_r[i]
        small_at[0] += 1
        if i + 1 < len(around):
            small_cp[0] = pushed(sv.at[i + 1], sv_r.at[i + 1], around[i + 1])

    def finish_ends():
        when(core == 0, x_push.wait_recv)
        when(core == 1, y_push.wait_recv)
        vm["ghh"][:T, :] = vm["far"][...].astype(F32)
        far_keep = pltpu.make_async_copy(vm["ghh"].at[pl.ds(0, T), :], ends_o.at[0, 1 - row], sems.one())
        far_keep.start()
        far_keep.wait()
        when(core == 0, x_keep.wait)
        when(core == 1, y_keep.wait)

    if fused:
        for at, code in enumerate(TAIL):
            move(code)
            if at % 8 == 7 and small_at[0] < len(around):
                small_step()
        for job in jobs.values():
            job.finish()
    while small_at[0] < len(around):
        small_step()
    last = len(around)

    if fused:
        hand_over(core, sib, env, vm, jobs, m, D, H, FH, pushed, sv, last)
        results = list(zip(vm["stage"], outs[2:]))
    else:
        results = [(vm[name], out) for name, out in zip(("gproj", "gfc", "gout", "gq", "gk", "gv"), outs[2:])]
    results.append((sv.at[last], small_o))
    results = [pltpu.make_async_copy(src, dst, sems.one()) for src, dst in results]
    for cp in results:
        cp.start()
    finish_ends()
    for condition, cp in sent:
        when(condition, cp.wait_send)
    for cp in results:
        cp.wait()


def hand_over(core, sib, env, vm, jobs, m, D, H, FH, pushed, sv, last):
    qkv_o, out_o, fc_o, proj_o, shared_o = vm["stage"]
    vm["fb_s"][...] = jnp.where(core == 0, sv[last, 5:6, :], sv[last, 4:5, :])
    fin = vm["fin"]
    top = env.bit(m - 1) == core
    own = lambda name, l: (l,) + jobs[(name, 0)].own()[1:]
    arrive = [
        pushed(vm["gfc"].at[own("F0", 1 - core)[:-1]], fin["fc"], sib),
        pushed(vm["gq"].at[own("Q", 1 - core)], fin["q"], sib),
        pushed(vm["gk"].at[own("K", 1 - core)], fin["k"], sib),
        pushed(vm["gv"].at[own("V", 0)], fin["v"], sib),
        pushed(vm["fb_s"], fin["fb"], sib),
    ]
    out_push = pushed(vm["gout"].at[own("O", 1 - core)], fin["out"], sib, top)
    proj_push = pushed(vm["gproj"].at[own("P0", 1 - core)[:-1]], fin["proj"], sib, top)

    here = pl.ds(pl.multiple_of(core * H, 128), H)
    there = pl.ds(pl.multiple_of((1 - core) * H, 128), H)
    here_k = pl.ds(pl.multiple_of(D + core * H, 128), H)
    there_k = pl.ds(pl.multiple_of(D + (1 - core) * H, 128), H)
    qkv_o[0, :, here] = vm["gq"][own("Q", core)].astype(F32)
    qkv_o[0, :, here_k] = vm["gk"][own("K", core)].astype(F32)
    fc_o[0, :, pl.ds(pl.multiple_of(core * FH, 128), FH)] = vm["gfc"][own("F0", core)[:-1]].astype(F32)

    def top_out():
        out_o[0] = vm["gout"][own("O", core)].astype(F32)
        proj_o[0] = vm["gproj"][own("P0", core)[:-1]].astype(F32)

    when(top, top_out)
    for cp in arrive:
        cp.wait_recv()

    def other_out():
        out_push.wait_recv()
        proj_push.wait_recv()
        out_o[0] = fin["out"][...].astype(F32)
        proj_o[0] = fin["proj"][...].astype(F32)

    when(jnp.logical_not(top), other_out)
    qkv_o[0, :, there] = fin["q"][...].astype(F32)
    qkv_o[0, :, there_k] = fin["k"][...].astype(F32)
    fc_o[0, :, pl.ds(pl.multiple_of((1 - core) * FH, 128), FH)] = fin["fc"][...].astype(F32)
    fresh = pl.ds(2 * D, H)

    def fresh_first():
        qkv_o[0, :, fresh] = fin["v"][...].astype(F32)
        shared_o[...] = vm["gv"][own("V", 0)].astype(F32)

    def fresh_second():
        qkv_o[0, :, fresh] = vm["gv"][own("V", 1)].astype(F32)
        shared_o[...] = fin["v"][...].astype(F32)

    when(core == 0, fresh_first)
    when(core == 1, fresh_second)
    sv[last, 6:7, :] = fin["fb"][...]


def backward_pass(C, m, T, D, F, inputs):
    N, L, H, FH, R, J = C // 2, C * T, D // 2, F // 2, 2 * T, C << m
    fused = (D // J) % 16 == 0 and (F // J) % 16 == 0 and m > 0
    pairs = H // 128
    S, V = jax.ShapeDtypeStruct, pltpu.VMEM
    names = tuple(inputs)
    outs, stage = [S((1, 2, T, D), F32), S((8, FH), F32)], []
    flat = {"gproj": (FH, D), "gfc": (D, FH), "gout": (H, D), "gq": (D, H), "gk": (D, H), "gv": (D, H)}
    if fused:
        outs += [S((1, D // J, 5 * H), F32), S((1, D // J, D), F32), S((1, D // J, F), F32), S((1, F // J, D), F32),
                 S((D // J, H), F32)]
        stage = [V(out.shape, F32) for out in outs[2:]]
        grads = grad_shapes(C, m, D, F)
        land = {name: [V(shape, BF16) for shape in steps] for name, steps in landing_shapes(C, m, D, F).items()}
    else:
        outs += [S((2,) + shape, BF16) for shape in flat.values()]
        grads, land = flat, {}
    stages = m + C.bit_length() - 1
    vm = dict(
        gm=V((2, T, D), BF16), gb=V((R, D), BF16), gm_in=V((2, 2, T, D), BF16), act_in=V((R, FH), BF16), gp=V((R, FH), BF16), act=V((R, FH), BF16), hh=V((R, D), BF16), hr=V((R, D), F32),
        o=V((R, H), BF16), q=V((R, H), BF16), k=V((L, H), BF16), v=V((L, H), BF16), lse=V((R, 128), F32),
        xall=V((L, D), BF16), r=V((R, D), BF16), sm=V((2, 8, F), F32), sg=V((2, 8, FH), F32), bias=V((R, L), BF16),
        wa=V((2 * D, D), BF16), wfc=V((D, FH), BF16), go=V((R, D), F32), ghh=V((R, D), F32), a_s=V((R, D), BF16),
        a_r=V((R, D), BF16), b_r=V((R, D), BF16), goa=V((R, H), BF16), dq=V((R, H), BF16),
        dk=V((L, H), BF16), dv=V((2, L, H), BF16), fs_s=V((N - 1, T, D), BF16), fs_r=V((N - 1, T, D), BF16),
        fx_s=V((N - 1, T, D), BF16), fx_r=V((2, N - 1, T, D), BF16), far=V((T, D), BF16),
        sv=V((stages + 1, 8, FH), F32), sv_r=V((stages, 8, FH), F32), fb_s=V((1, FH), F32),
        fin=dict(fc=V((D // J, FH), BF16), q=V((D // J, H), BF16), k=V((D // J, H), BF16), v=V((D // J, H), BF16),
                 out=V((D // J, D), BF16), proj=V((F // J, D), BF16), fb=V((1, FH), F32)),
        land=land, stage=stage, **{name: V((2,) + shape, BF16) for name, shape in grads.items()})
    moves = {name: len(order) - 1 + 2 * (C - 1) + (sided == SIDE_STEP) for name, (_, _, order, sided) in job_table(m).items()}
    credits = {name: pltpu.SemaphoreType.REGULAR((n,)) for name, n in moves.items()} if fused else {}
    semaphores = 60 + 2 * stages + 8 * (N - 1) + (20 + 2 * sum(moves.values()) if fused else 7)
    in_specs = [VM if name == "kseg" else HBM for name in names]
    return pl.pallas_call(
        functools.partial(backward_kernel, C, m, T, D, F, fused, names),
        in_specs=in_specs,
        out_specs=[HBM] * len(outs),
        out_shape=outs,
        scratch_shapes=[vm, pltpu.SemaphoreType.DMA((semaphores,)), credits],
        compiler_params=pltpu.CompilerParams(collective_id=1, has_side_effects=True, vmem_limit_bytes=VMEM_LIMIT),
        name="backward_pass",
    )(*inputs.values())


def xor_route(size, bit):
    return [(i, i ^ (1 << bit)) for i in range(size)]


def halve(grad, axis_name, bit, at):
    mine = (lax.axis_index(axis_name) >> bit) & 1
    keep = lax.dynamic_index_in_dim(grad, mine, at, keepdims=False)
    send = lax.dynamic_index_in_dim(grad, 1 - mine, at, keepdims=False)
    got = lax.ppermute(send, axis_name, xor_route(lax.axis_size(axis_name), bit))
    return (keep.astype(F32) + got.astype(F32)).astype(grad.dtype)


def bits_of(axis_name):
    return lax.axis_size(axis_name).bit_length() - 1


def scatter_sum(grad, order, skip_first=False):
    dims = [(DP, b) for b in reversed(range(bits_of(DP)))] + [(CTX, b) for b in reversed(range(bits_of(CTX)))]
    if skip_first:
        dims = dims[1:]
    parts = len(dims)
    rows, cols = grad.shape
    grad = grad.reshape((2,) * parts + (rows >> parts, cols))
    for item in order:
        at = dims.index(item)
        grad = halve(grad, item[0], item[1], at)
        dims.pop(at)
    return grad


def shards(ends, segment_ids, ln1_gain, ln1_bias, qkv_weight, out_weight, ln2_gain, ln2_bias, fc_weight, fc_bias,
           proj_weight, shared_weight):
    core = lax.axis_index(SECTION)
    first = core == 0
    C, m = lax.axis_size(CTX), bits_of(DP)
    J = C << m
    micros, T, D = ends.shape[1:]
    F = fc_weight.shape[2]
    half, FH = D // 2, F // 2
    names = ("xall", "q", "k", "v", "o", "lse", "r", "hr", "hh", "gp", "act", "y", "yb", "gy", "sm", "watt", "wfc", "wproj", "act_in", "gm_in", "kseg")
    kept = dict(zip(names, forward_pass(
        C, m, ends, segment_ids, ln1_gain, ln1_bias, ln2_gain, ln2_bias, qkv_weight, out_weight,
        fc_weight, fc_bias, proj_weight, shared_weight)))
    block, small, *grads = backward_pass(C, m, T, D, F, kept)
    if len(grads) != 5:
        small = small.at[6].set(swap(jnp.where(first, small[5], small[4])))
        grads = scattered(grads, core, m, half)
    fcb_out, *ln, block, qkv_out, out_out, fc_out, proj_out, shared_out = assemble(small, J, C, D, F, [block, *grads])
    return (block, qkv_out, out_out, fc_out, fcb_out, proj_out, shared_out, *ln)


def assemble_kernel(J, C, D, F, small_in, *refs):
    n = (len(refs) - 13) // 2
    ins, small_outs, outs, bounce = refs[:n], refs[n : n + 5], refs[n + 5 : -8], refs[-8]
    small, parts, dma = refs[-7], refs[-6:-1], refs[-1]
    come = [pltpu.make_async_copy(a, b, dma.at[i]) for i, (a, b) in enumerate(zip(ins, bounce))]
    first = pltpu.make_async_copy(small_in, small, dma.at[n])
    for cp in [first] + come:
        cp.start()
    first.wait()
    copies = []
    core = lax.axis_index(SECTION)
    j = lax.axis_index(DP) * C + lax.axis_index(CTX)

    def own_part(values):
        width = values.shape[1] // J
        at = lax.broadcasted_iota(jnp.int32, (values.shape[1], width), 0) - j * width
        pick = (at == lax.broadcasted_iota(jnp.int32, (values.shape[1], width), 1)).astype(F32)
        return jnp.dot(values, pick, precision=lax.Precision.HIGHEST, preferred_element_type=F32)

    ours = jnp.where(core == 0, small[4:5, :], small[5:6, :])
    theirs = small[6:7, :]
    bias = jnp.concatenate([jnp.where(core == 0, ours, theirs), jnp.where(core == 0, theirs, ours)], axis=1)
    parts[0][...] = own_part(jnp.broadcast_to(bias, (8, F)))[0:1, :]
    norms = own_part(small[:, :D])
    for i in range(4):
        parts[1 + i][...] = norms[i : i + 1, :]
    for i in range(5):
        copies.append(pltpu.make_async_copy(parts[i], small_outs[i], dma.at[n + 1 + i]))
        copies[-1].start()
    for i in range(n):
        come[i].wait()
        copies.append(pltpu.make_async_copy(bounce[i], outs[i], dma.at[i]))
        copies[-1].start()
    for cp in copies:
        cp.wait()


def assemble(small, J, C, D, F, arrays):
    S = jax.ShapeDtypeStruct
    return pl.pallas_call(
        functools.partial(assemble_kernel, J, C, D, F),
        in_specs=[HBM] * (1 + len(arrays)),
        out_specs=[HBM] * (5 + len(arrays)),
        out_shape=[S((1, F // J), F32)] + [S((1, D // J), F32)] * 4 + [S(a.shape, a.dtype) for a in arrays],
        scratch_shapes=[[pltpu.VMEM(a.shape, a.dtype) for a in arrays], pltpu.VMEM(small.shape, F32), pltpu.VMEM((1, F // J), F32)] + [pltpu.VMEM((1, D // J), F32)] * 4
        + [pltpu.SemaphoreType.DMA((len(arrays) + 6,))],
        compiler_params=pltpu.CompilerParams(vmem_limit_bytes=VMEM_LIMIT),
        name="assemble",
    )(small, *arrays)


def scattered(grads, core, m, half):
    gproj, gfc, gout, gq, gk, gv = grads
    first = core == 0
    x_first = [(DP, b) for b in range(m)] + [(CTX, b) for b in range(bits_of(CTX))]
    y_first = [(DP, b) for b in reversed(range(m))] + x_first[m:]

    def sided(grad):
        dp, size = lax.axis_index(DP), lax.axis_size(DP)
        top = size // 2
        route = [(c * size + d, c * size + (d ^ top)) for c in range(2) for d in range(size) if (d >= top) != (c == 1)]
        got = lax.ppermute(grad, (SECTION, DP), route)
        return scatter_sum((grad.astype(F32) + got.astype(F32)).astype(BF16), y_first[1:], skip_first=True)

    res = []
    for l in range(2):
        qkv = jnp.concatenate([gq[l], gk[l], gv[l]], axis=1)
        res.append((scatter_sum(qkv, x_first), sided(gout[l]), scatter_sum(gfc[l], x_first),
                    scatter_sum(gproj[l], y_first[1:], skip_first=True)))
    holder = jnp.where(lax.axis_index(DP) >= lax.axis_size(DP) // 2, 1, 0) == core
    mine = tuple(jnp.where(first, a, b) for a, b in zip(res[0], res[1]))
    got = tuple(swap(jnp.where(first, b, a)) for a, b in zip(res[0], res[1]))
    left, right = [jnp.where(first, a, b).astype(F32) for a, b in zip(mine, got)], [jnp.where(first, b, a).astype(F32) for a, b in zip(mine, got)]
    fresh0 = res[0][0][:, 2 * half :]
    fresh0_other = swap(fresh0)
    fresh = jnp.where(first, fresh0_other, res[1][0][:, 2 * half :]).astype(F32)
    qkv_out = jnp.concatenate([left[0][:, :half], right[0][:, :half], left[0][:, half : 2 * half], right[0][:, half : 2 * half], fresh], axis=1)
    fc_out = jnp.concatenate([left[2], right[2]], axis=1)
    out_out = jnp.where(holder, mine[1], got[1]).astype(F32)
    proj_out = jnp.where(holder, mine[3], got[3]).astype(F32)
    shared_out = jnp.where(first, fresh0, fresh0_other).astype(F32)
    return qkv_out[None], out_out[None], fc_out[None], proj_out[None], shared_out


def solution(mesh):
    placed = (
        P(SECTION, DP, CTX, None), P(DP, CTX), P(SECTION, None), P(SECTION, None),
        P(SECTION, None, None), P(SECTION, None, None), P(SECTION, None), P(SECTION, None),
        P(SECTION, None, None), P(SECTION, None), P(SECTION, None, None), P(),
    )
    both = (DP, CTX)
    return jax.shard_map(
        shards, mesh=mesh, in_specs=placed,
        out_specs=(P(SECTION, DP, CTX, None), P(SECTION, both, None), P(SECTION, both, None),
                   P(SECTION, both, None), P(SECTION, both), P(SECTION, both, None), P(both, None),
                   P(SECTION, both), P(SECTION, both), P(SECTION, both), P(SECTION, both)),
        check_vma=False,
    )
```

```python
import functools

import jax
import jax.numpy as jnp
from jax import lax
from jax.experimental import pallas as pl
from jax.experimental.pallas import tpu as pltpu
from jax.sharding import PartitionSpec as P

HEAD = 64
SECTION, DP, CTX = "section", "dp", "ctx"
EPSILON = 1e-05
MASKED = -1000000000.0
F32 = jnp.float32
BF16 = jnp.bfloat16
VMEM_LIMIT = 127 * 2**19


def mm(left, right):
    return jnp.dot(left, right, preferred_element_type=F32)


def mm_nt(left, right):
    return lax.dot_general(left, right, (((1,), (1,)), ((), ())), preferred_element_type=F32)


def mm_tn(left, right):
    return lax.dot_general(left, right, (((0,), (0,)), ((), ())), preferred_element_type=F32)


def unit_norm(values):
    mean = jnp.mean(values, axis=-1, keepdims=True)
    centred = values - mean
    rstd = lax.rsqrt(jnp.mean(centred * centred, axis=-1, keepdims=True) + EPSILON)
    return centred * rstd, rstd


def layer_norm(values, gain, bias):
    return unit_norm(values)[0] * gain + bias


def gelu_both(u):
    t = jnp.tanh(0.7978845608028654 * (u + 0.044715 * u * u * u))
    half = 0.5 * (1.0 + t)
    return u * half, half + 0.5 * u * (1.0 - t * t) * (0.7978845608028654 + 3 * 0.044715 * 0.7978845608028654 * u * u)


def swap(x):
    return lax.ppermute(x, SECTION, [(0, 1), (1, 0)])


MESH = pl.DeviceIdType.MESH
HBM = pl.BlockSpec(memory_space=pl.ANY)
VM = pl.BlockSpec(memory_space=pltpu.VMEM)


class Sems:
    def __init__(self, ref):
        self.ref, self.used = ref, 0

    def one(self):
        self.used += 1
        return self.ref.at[self.used - 1]


def push(src, dst, send, recv, to):
    return pltpu.make_async_remote_copy(src_ref=src, dst_ref=dst, send_sem=send, recv_sem=recv, device_id=to,
                                        device_id_type=MESH)


def greet(peers):
    barrier = pltpu.get_barrier_semaphore()
    for peer in peers:
        pl.semaphore_signal(barrier, inc=1, device_id=peer, device_id_type=MESH)
    pl.semaphore_wait(barrier, len(peers))


def attention_unit(first, l, blk, key_blocks, T, pairs, q, k, v, bias, acc, top_of, sum_of):
    rows = pl.ds(pl.multiple_of(blk * T, T), T)
    lane = lax.broadcasted_iota(jnp.int32, (T, 128), 1)
    blocks = [pl.ds(pl.multiple_of(at * T, T), T) for at in key_blocks]
    mask = jnp.concatenate([bias[rows, pl.ds(pl.multiple_of(at * T, 128), T)] for at in key_blocks], axis=1)

    def body(i, carry):
        cols = pl.ds(pl.multiple_of(i * 128, 128), 128)
        q2 = q[l, rows, cols] * jnp.asarray(HEAD**-0.5, BF16)
        k2 = jnp.concatenate([k[l, at, cols] for at in blocks], axis=0)
        v2 = jnp.concatenate([v[l, at, cols] for at in blocks], axis=0)
        v2 = jnp.concatenate([v2, jnp.ones_like(v2)], axis=1)
        sums, tops = [], []
        for h in range(2):
            qh = jnp.where((lane >= 64) == (h == 1), q2, jnp.zeros_like(q2))
            s = mm_nt(qh, k2) + mask
            top = jnp.max(s, axis=-1, keepdims=True)
            sums.append(mm(jnp.exp(s - top).astype(BF16), v2))
            tops.append(top)
        top = jnp.where(lane < 64, tops[0], tops[1])
        total = jnp.where(lane < 64, sums[0][:, 128:], sums[1][:, 128:])
        part = jnp.where(lane < 64, sums[0][:, :128], sums[1][:, :128])
        if not first:
            old = top_of[i, rows, :]
            new = jnp.maximum(old, top)
            keep, add = jnp.exp(old - new), jnp.exp(top - new)
            total = keep * sum_of[i, rows, :] + add * total
            part = keep * acc[i, rows, :] + add * part
            top = new
        top_of[i, rows, :] = top
        sum_of[i, rows, :] = total
        acc[i, rows, :] = part
        return carry

    lax.fori_loop(0, pairs, body, 0)


def attention_end(l, blk, T, pairs, o, lse, acc, top_of, sum_of):
    rows = slice(blk * T, (blk + 1) * T)
    lane = lax.broadcasted_iota(jnp.int32, (T, 128), 1)
    logs = jnp.zeros((T, 128), F32)
    for i in range(pairs):
        total = sum_of[i, rows, :]
        o[l, rows, i * 128 : (i + 1) * 128] = (acc[i, rows, :] / total).astype(BF16)
        log = top_of[i, rows, :] + jnp.log(total)
        logs = jnp.where(lane == 2 * i, log[:, 0:1], jnp.where(lane == 2 * i + 1, log[:, 64:65], logs))
    lse[l, rows, :] = logs


def column(row_values):
    T = row_values.shape[1]
    at = lax.broadcasted_iota(jnp.int32, (T, T), 0) == lax.broadcasted_iota(jnp.int32, (T, T), 1)
    spread = jnp.where(at, jnp.broadcast_to(row_values, (T, T)), 0).astype(F32)
    return jnp.sum(spread, axis=1, keepdims=True).astype(jnp.int32)


def forward_kernel(C, m, T, D, F, ends, segs, g1, b1, g2, b2, qkv, wo, fc, fcb, proj, shared,
                   xall_o, q_o, k_o, v_o, o_o, lse_o, r_o, hr_o, hh_o, gp_o, act_o, y_o, yb_o, gy_o, sm_o, watt_o, wfc_o, wproj_o,
                   act_in_o, gm_in_o, kseg_o,
                   e, seg, segv, sm, wqk, wv, wout, wfc, wproj, xall, q, k, v, o, lse, r, hr, hh, gp, act, y, yb, wvt, bias,
                   acc, top_of, sum_of, br_s, br_r, ml_s, ml_r, dma):
    core, dp, z = lax.axis_index(SECTION), lax.axis_index(DP), lax.axis_index(CTX)
    N, L, H, FH = C // 2, C * T, D // 2, F // 2
    T2 = T // 2
    row = z // N
    lo = z + row * (C - 1 - 2 * z)
    hi = C - 1 - lo
    base = row * N
    pairs = H // 128
    sems = Sems(dma)
    sib = (1 - core, dp, z)
    mirror = (core, dp, C - 1 - z)
    top_bit = lax.div(dp, 1 << (m - 1))
    across = (core, dp + (1 - 2 * top_bit) * (1 << (m - 1)), z)
    owner = top_bit == core
    ahead = [(core, dp, base + lax.rem(z - base + n, N)) for n in range(1, N)]
    behind = [base + lax.rem(z - base + N - n, N) for n in range(1, N)]
    line = [(core, dp, lax.rem(z + n, C)) for n in range(1, C)]
    pos = lambda blk: lo + blk * (hi - lo)
    rows_at = lambda p: pl.ds(pl.multiple_of(p * T, T), T)
    saves = []

    def save(src, dst):
        cp = pltpu.make_async_copy(src, dst, sems.one())
        cp.start()
        saves.append(cp)

    e_load = pltpu.make_async_copy(ends.at[0, row], e.at[core, row], sems.one())
    e_load.start()
    qc = pl.ds(pl.multiple_of(core * H, 128), H)
    kc = pl.ds(pl.multiple_of(D + core * H, 128), H)
    qo = pl.ds(pl.multiple_of((1 - core) * H, 128), H)
    ko = pl.ds(pl.multiple_of(D + (1 - core) * H, 128), H)
    loads = [
        pltpu.make_async_copy(qkv.at[0, :, qc], wqk.at[core, :, pl.ds(0, H)], sems.one()),
        pltpu.make_async_copy(qkv.at[0, :, kc], wqk.at[core, :, pl.ds(H, H)], sems.one()),
        pltpu.make_async_copy(wo.at[0, pl.ds(pl.multiple_of(core * H, H), H), :], wout.at[core], sems.one()),
        pltpu.make_async_copy(fc.at[0, :, pl.ds(pl.multiple_of(core * FH, 128), FH)], wfc.at[core], sems.one()),
        pltpu.make_async_copy(proj.at[0, pl.ds(pl.multiple_of(core * FH, FH), FH), :], wproj.at[core], sems.one()),
    ]
    for cp in loads:
        cp.start()
    v_sem = sems.one()
    v_shared = pltpu.make_async_copy(shared, wv.at[0], v_sem)
    v_fresh = pltpu.make_async_copy(qkv.at[0, :, pl.ds(2 * D, H)], wv.at[1], v_sem)

    @pl.when(core == 0)
    def _():
        v_shared.start()

    @pl.when(core == 1)
    def _():
        v_fresh.start()

    segv[0] = segs[0:1, :]
    segv[1] = segs[1:2, :]
    seg[z] = segv[row]
    sm[core] = jnp.zeros_like(sm[core])
    sm[core, 0:1, :D] = g1[...]
    sm[core, 1:2, :D] = b1[...]
    sm[core, 2:3, :D] = g2[...]
    sm[core, 3:4, :D] = b2[...]
    sm[core, 4:5, :] = fcb[...]

    greet([sib, across] + line)

    own_s, own_r = sems.one(), sems.one()
    own_push = push(ends.at[0, row], e.at[core, row], own_s, own_r, sib)
    own_come = push(ends.at[0, row], e.at[1 - core, row], own_s, own_r, sib)
    seg_push = []
    for n in range(1, C):
        to = lax.rem(z + n, C)
        cp = push(segv.at[lax.div(to, N)], seg.at[z], sems.one(), sems.one(), line[n - 1])
        cp.start()
        seg_push.append(cp)
    far_push, far_come, fwd_push, fwd_come = [], [], [], []
    for h in range(2):
        part = pl.ds(h * T2, T2)
        far_s, far_r, fwd_s, fwd_r = sems.one(), sems.one(), sems.one(), sems.one()
        far_push.append(push(ends.at[0, 1 - row, part], e.at[core, row, part], far_s, far_r, mirror))
        far_come.append(push(ends.at[0, 1 - row, part], e.at[core, 1 - row, part], far_s, far_r, mirror))
        here, there = e.at[core, 1 - row, part], e.at[1 - core, 1 - row, part]
        fwd_push.append(push(here, here, fwd_s, fwd_r, sib))
        fwd_come.append(push(there, there, fwd_s, fwd_r, sib))

    @pl.when(core == 0)
    def _():
        for cp in far_push:
            cp.start()

    own_push.start()
    sm_push = push(sm.at[core], sm.at[core], sems.one(), sems.one(), sib)
    sm_push.start()
    qk_push = [
        push(qkv.at[0, :, qo], wqk.at[core, :, pl.ds(0, H)], sems.one(), sems.one(), sib),
        push(qkv.at[0, :, ko], wqk.at[core, :, pl.ds(H, H)], sems.one(), sems.one(), sib),
    ]
    for cp in qk_push:
        cp.start()
    v_push = push(qkv.at[0, :, pl.ds(2 * D, H)], wv.at[0], sems.one(), sems.one(), sib)

    @pl.when(core == 0)
    def _():
        v_push.start()

    rest_push = [
        push(wo.at[0, pl.ds(pl.multiple_of((1 - core) * H, H), H), :], wout.at[core], sems.one(), sems.one(), sib),
        push(fc.at[0, :, pl.ds(pl.multiple_of((1 - core) * FH, 128), FH)], wfc.at[core], sems.one(), sems.one(), sib),
        push(proj.at[0, pl.ds(pl.multiple_of((1 - core) * FH, FH), FH), :], wproj.at[core], sems.one(), sems.one(), sib),
    ]

    xh_sends = {}

    def route_block(l, turn, blk):
        p = pos(blk)
        for n in range(N - 1):
            part = xall.at[l, pl.ds(pl.multiple_of(p * T + core * T2, T2), T2), :]
            s, rsem = sems.one(), sems.one()
            cp = push(part, part, s, rsem, ahead[n])
            src = behind[n]
            slo = src + row * (C - 1 - 2 * src)
            sp = slo + blk * (C - 1 - 2 * slo)
            got = xall.at[l, pl.ds(pl.multiple_of(sp * T + core * T2, T2), T2), :]
            other = xall.at[l, pl.ds(pl.multiple_of(sp * T + (1 - core) * T2, T2), T2), :]
            come = push(got, got, s, rsem, ahead[n])
            fs, fr = sems.one(), sems.one()
            onward = push(got, got, fs, fr, sib)
            arrive = push(other, other, fs, fr, sib)
            xh_sends[(l, turn, n)] = (cp, come, onward, arrive, sp)

    def leave(l, turn):
        for n in range(N - 1):
            xh_sends[(l, turn, n)][0].start()

    def normed_block(l, turn, blk, values):
        xall[l, rows_at(pos(blk)), :] = layer_norm(values, sm[l, 0:1, :D], sm[l, 1:2, :D]).astype(BF16)
        route_block(l, turn, blk)
        leave(l, turn)

    def own_products(l, blk):
        p = pos(blk)
        xh = xall[l, rows_at(p), :]
        both = mm(xh, wqk[l])
        q[l, blk * T : (blk + 1) * T, :] = both[:, :H].astype(BF16)
        k[l, rows_at(p), :] = both[:, H:].astype(BF16)

    def value_products(l, p):
        src = l * core
        v[l, rows_at(p), :] = mm(xall[src, rows_at(p), :], wv[src]).astype(BF16)

    def key_products(l, p):
        k[l, rows_at(p), :] = mm(xall[l, rows_at(p), :], wqk[l, :, H:]).astype(BF16)

    def arrivals(l, turn):
        for n in range(N - 1):
            cp, come, onward, arrive, sp = xh_sends[(l, turn, n)]
            come.wait_recv()
            onward.start()

    def foreign_products(l, turn):
        for n in range(N - 1):
            cp, come, onward, arrive, sp = xh_sends[(l, turn, n)]
            arrive.wait_recv()
            key_products(l, sp)
            value_products(l, sp)

    act_push = [push(act.at[0, pl.ds(b * T, T), :], act_in_o.at[pl.ds(b * T, T), :], sems.one(), sems.one(), across) for b in range(2)]
    gm_push = [push(e.at[1, b], gm_in_o.at[b], sems.one(), sems.one(), across) for b in (row, 1 - row)]

    @pl.when(core == 0)
    def _():
        e_load.wait()

    @pl.when(core == 1)
    def _():
        own_come.wait_recv()

    sm_push.wait()
    blk = row
    r[0, pl.ds(pl.multiple_of(blk * T, T), T), :] = e[0, blk]
    normed_block(0, 0, blk, e[0, blk].astype(F32))

    @pl.when(core == 0)
    def _():
        loads[0].wait()
        loads[1].wait()
        v_shared.wait()

    @pl.when(core == 1)
    def _():
        for cp in qk_push:
            cp.wait_recv()
        v_push.wait_recv()

    def own_products_dynamic(l, blk):
        p = pos(blk)
        both = mm(xall[l, rows_at(p), :], wqk[l])
        q[l, pl.ds(pl.multiple_of(blk * T, T), T), :] = both[:, :H].astype(BF16)
        k[l, rows_at(p), :] = both[:, H:].astype(BF16)
        value_products(l, p)

    own_products_dynamic(0, blk)

    @pl.when(core == 1)
    def _():
        e_load.wait()

    @pl.when(core == 0)
    def _():
        own_come.wait_recv()

    when(jnp.logical_not(owner), gm_push[0].start)

    for n, cp in enumerate(seg_push):
        cp.wait()
    kseg = jnp.concatenate([seg[n] for n in range(C)], axis=1)
    kseg_o[...] = kseg
    for blk in range(2):
        rows = slice(blk * T, (blk + 1) * T)
        qpos = pos(blk) * T + lax.broadcasted_iota(jnp.int32, (T, L), 0)
        kpos = lax.broadcasted_iota(jnp.int32, (T, L), 1)
        allowed = (kpos <= qpos) & (kseg == column(seg[pos(blk)]))
        bias[rows, :] = jnp.where(allowed, 0.0, MASKED)

    blk = 1 - row

    route_block(0, 1, blk)
    for h in range(2):
        @pl.when(core == 0)
        def _():
            far_come[h].wait_recv()
            fwd_push[h].start()

        @pl.when(core == 1)
        def _():
            fwd_come[h].wait_recv()

        values = e[0, blk, h * T2 : (h + 1) * T2, :]
        r[0, pl.ds(pl.multiple_of(blk * T + h * T2, T2), T2), :] = values
        xall[0, pl.ds(pl.multiple_of(pos(blk) * T + h * T2, T2), T2), :] = layer_norm(
            values.astype(F32), sm[0, 0:1, :D], sm[0, 1:2, :D]).astype(BF16)

        @pl.when(core == h)
        def _():
            leave(0, 1)

    @pl.when(core == 1)
    def _():
        for cp in far_push:
            cp.start()

    own_products_dynamic(0, blk)

    def at_core(here, ours, theirs):
        @pl.when(here)
        def _():
            for cp in ours:
                cp.wait()

        @pl.when(jnp.logical_not(here))
        def _():
            for cp in theirs:
                cp.wait_recv()

    def branch(l, blk):
        rows = slice(blk * T, (blk + 1) * T)
        part = mm(o[l, rows, :], wout[l])
        hr[l, rows, :] = part
        br_s[l, rows, :] = part.astype(BF16)
        cp = push(br_s.at[l, rows, :], br_r.at[l, rows, :], sems.one(), sems.one(), sib)
        cp.start()
        return cp

    def hidden_units(l, blk, come):
        rows = slice(blk * T, (blk + 1) * T)
        come.wait_recv()
        hidden = r[l, rows, :].astype(F32) + hr[l, rows, :] + br_r[l, rows, :].astype(F32)
        hr[l, rows, :] = hidden
        normed2 = layer_norm(hidden, sm[l, 2:3, :D], sm[l, 3:4, :D]).astype(BF16)
        hh[l, rows, :] = normed2
        if l == 0 and blk == 0:
            at_core(core == 0, loads[3:5], rest_push[1:3])
        mine = pl.ds(pl.multiple_of(core * FH, 128), FH)
        u = mm(normed2, wfc[l]) + sm[l, 4:5, mine]
        a, slope = gelu_both(u)
        gp[l, rows, :] = slope.astype(BF16)
        act[l, rows, :] = a.astype(BF16)
        if l == 0:
            when(jnp.logical_not(owner), act_push[blk].start)

    def feed_out(l, blk):
        rows = slice(blk * T, (blk + 1) * T)
        part = mm(act[l, rows, :], wproj[l])
        y[rows, :] = part
        ml_s[l, rows, :] = part.astype(BF16)
        cp = push(ml_s.at[l, rows, :], ml_r.at[l, rows, :], sems.one(), sems.one(), sib)
        cp.start()
        return cp

    def block_out(l, blk, come):
        rows = slice(blk * T, (blk + 1) * T)
        come.wait_recv()
        out = hr[l, rows, :] + y[rows, :] + ml_r[l, rows, :].astype(F32)
        if l == 0:
            sent = out.astype(BF16)
            r[1, rows, :] = sent
            normed_block(1, blk, blk, sent.astype(F32))
        else:
            y[rows, :] = out
            yb[rows, :] = out.astype(BF16)

    def save_weights(l):
        wvt[l] = jnp.transpose(wv[l * core])
        save(wqk.at[l], watt_o.at[l, pl.ds(0, D)])
        save(wout.at[l], watt_o.at[l, pl.ds(D, H)])
        save(wvt.at[l], watt_o.at[l, pl.ds(D + H, H)])
        save(wfc.at[l], wfc_o.at[l])
        save(wproj.at[l], wproj_o.at[l])

    def unit(first, l, blk, key_blocks):
        attention_unit(first, l, blk, key_blocks, T, pairs, q, k, v, bias, acc, top_of, sum_of)

    def middle(l):
        unit(True, l, 0, [lo])
        arrivals(l, 0)
        unit(True, l, 1, [lo, hi])
        if l == 0:
            arrivals(0, 1)
            for cp in rest_push:
                cp.start()
        foreign_products(l, 0)
        if l == 1:
            arrivals(1, 1)
        else:
            foreign_products(0, 1)
        order = [(slo, lax.div(lo - slo + N - 1, N)) for slo in [src + row * (C - 1 - 2 * src) for src in behind]]
        for slo, above in order:
            unit(False, l, 1, [slo])
        if l == 1:
            foreign_products(1, 1)
        for slo, above in order:
            unit(False, l, 1 - above, [slo + (1 - above) * (C - 1 - 2 * slo)])
        attention_end(l, 0, T, pairs, o, lse, acc, top_of, sum_of)
        if l == 0:
            at_core(core == 0, loads[2:3], rest_push[0:1])

            @pl.when(core == 1)
            def _():
                for h in range(2):
                    far_come[h].wait_recv()
                    fwd_push[h].start()
        sends = [branch(l, 0)]
        attention_end(l, 1, T, pairs, o, lse, acc, top_of, sum_of)
        sends.append(branch(l, 1))
        if l == 0:
            @pl.when(core == 0)
            def _():
                for cp in fwd_come:
                    cp.wait_recv()

            when(jnp.logical_not(owner), gm_push[1].start)
        save(q.at[l], q_o.at[l])
        save(k.at[l], k_o.at[l])
        save(v.at[l], v_o.at[l])
        save(o.at[l], o_o.at[l])
        save(lse.at[l], lse_o.at[l])
        save(xall.at[l], xall_o.at[l])
        hidden_units(l, 0, sends[0])
        mlps = [feed_out(l, 0)]
        hidden_units(l, 1, sends[1])
        save(hr.at[l], hr_o.at[l])
        save(hh.at[l], hh_o.at[l])
        save(gp.at[l], gp_o.at[l])
        save(act.at[l], act_o.at[l])
        block_out(l, 0, mlps[0])
        mlps.append(feed_out(l, 1))
        if l == 0:
            at_core(core == 1, loads[0:2] + [v_fresh], qk_push)
            own_products(1, 0)
            value_products(1, pos(0))
        block_out(l, 1, mlps[1])
        if l == 0:
            own_products(1, 1)
            value_products(1, pos(1))
            at_core(core == 1, loads[2:5], rest_push)
            save_weights(0)
            save_weights(1)
        return sends + mlps


    pair_sends = middle(0)
    save(r, r_o)

    save(e.at[1], gy_o)
    save(sm, sm_o)
    pair_sends += middle(1)
    save(y, y_o)
    save(yb, yb_o)

    def crossed():
        for cp in act_push + gm_push:
            cp.wait_recv()

    def crossing():
        for cp in act_push + gm_push:
            cp.wait_send()

    when(owner, crossed)
    when(jnp.logical_not(owner), crossing)
    own_push.wait_send()
    for cp in far_push + fwd_push + qk_push + rest_push + pair_sends:
        cp.wait_send()

    @pl.when(core == 0)
    def _():
        v_push.wait_send()

    for cp, come, onward, arrive, sp in xh_sends.values():
        cp.wait_send()
        onward.wait_send()
    for cp in saves:
        cp.wait()


def forward_pass(C, m, ends, segs, g1, b1, g2, b2, qkv, wo, fc, fcb, proj, shared):
    T, D, F = ends.shape[2], ends.shape[3], fc.shape[2]
    N, L, H, FH = C // 2, C * T, D // 2, F // 2
    R, pairs = 2 * T, D // 256
    S = jax.ShapeDtypeStruct
    outs = [S((2, L, D), BF16), S((2, R, H), BF16), S((2, L, H), BF16), S((2, L, H), BF16), S((2, R, H), BF16),
            S((2, R, 128), F32), S((2, R, D), BF16), S((2, R, D), F32), S((2, R, D), BF16), S((2, R, FH), BF16),
            S((2, R, FH), BF16), S((R, D), F32), S((R, D), BF16), S((2, T, D), BF16), S((2, 8, F), F32), S((2, 2 * D, D), BF16),
            S((2, D, FH), BF16), S((2, FH, D), BF16), S((R, FH), BF16), S((2, T, D), BF16), S((1, L), jnp.int32)]
    V = pltpu.VMEM
    scratch = [V((2, 2, T, D), BF16), V((C, 1, T), jnp.int32), V((2, 1, T), jnp.int32), V((2, 8, F), F32), V((2, D, D), BF16), V((2, D, H), BF16),
               V((2, H, D), BF16), V((2, D, FH), BF16), V((2, FH, D), BF16), V((2, L, D), BF16), V((2, R, H), BF16),
               V((2, L, H), BF16), V((2, L, H), BF16), V((2, R, H), BF16), V((2, R, 128), F32), V((2, R, D), BF16),
               V((2, R, D), F32), V((2, R, D), BF16), V((2, R, FH), BF16), V((2, R, FH), BF16), V((R, D), F32),
               V((R, D), BF16), V((2, H, D), BF16), V((R, L), F32), V((pairs, R, 128), F32), V((pairs, R, 128), F32),
               V((pairs, R, 128), F32), V((2, R, D), BF16), V((2, R, D), BF16), V((2, R, D), BF16), V((2, R, D), BF16),
               pltpu.SemaphoreType.DMA((90 + 16 * (N - 1) + 2 * (C - 1),))]
    return pl.pallas_call(
        functools.partial(forward_kernel, C, m, T, D, F),
        in_specs=[HBM, VM, VM, VM, VM, VM, HBM, HBM, HBM, VM, HBM, HBM],
        out_specs=[HBM] * 20 + [VM],
        out_shape=outs,
        scratch_shapes=scratch,
        compiler_params=pltpu.CompilerParams(collective_id=0, has_side_effects=True, vmem_limit_bytes=VMEM_LIMIT),
        name="forward_pass",
    )(ends, segs, g1, b1, g2, b2, qkv, wo, fc, fcb, proj, shared)


WHOLE, SIDED, SIDE_STEP = 0, 1, 2
SMALL = 200
JOBS = ("P0", "P1", "P2", "F0", "F1", "F2", "O", "Q", "K", "V")
PROJ_AT = (3, 3)
POLLS = (
    (), (), (113,), (), (), (), (), (), (), (115,), (), (), (), (13,), (113,), (), (116,), (), (), (), (15,),
    (13, 117), (115, 112, 113), (), (13, 114, 113, 16, 17, 117), (110,), (), (), (13, 113), (15, 115),
    (12, 112, 17, 117), (111,), (13,), (15, 115), (), (10, 110, 12, 112), (17, 116, 117), (), (15, 115, 14),
    (10, 110, 114, 11, 111, 12, 112), (17, 118, 105, 15, 10, 110, 16, 116), (11, 111, 12, 10), (16, 116, 14, 114),
    (11, 119), (), (16, 103, 14), (), (117,), (106,), (18, 111, 116, 5, 19, 114), (17, 118, 105), (11, 16),
    (14, 119, 114), (),
)
TAIL = (
    104, 3, 6, 14, 102, 18, 5, 118, 19, 119, 105, 200, 100, 19, 119, 103, 2, 102, 18, 118,
    19, 119, 5, 105, 101, 2, 102, 4, 108, 18, 118, 0, 100, 19, 200, 5, 107, 105, 2, 18,
    102, 3, 103, 0, 100, 200, 5, 109, 1, 101, 106, 2, 3, 103, 0, 100, 200, 7, 107, 104,
    8, 1, 101, 3, 103, 0, 108, 6, 106, 7, 107, 9, 1, 101, 3, 109, 6, 106, 7, 107,
    4, 104, 1, 6, 106, 8, 108, 7, 107, 4, 104, 9, 109, 6, 7, 8, 108, 4, 104, 9,
    109, 8, 108, 4, 9, 109, 8, 9,
)


class Job:
    def __init__(self, env, buf, lead, cols, order, sided, land, credits, active, earlier, prior):
        self.env, self.buf, self.lead, self.cols = env, buf, lead, cols
        self.sided, self.land, self.credits, self.active, self.prior = sided, land, credits, active, prior
        self.copies = {}
        self.earlier = earlier
        self.bits = list(range(env.m - 2 if sided else env.m - 1, -1, -1))
        self.fixed, self.z_done, self.steps, self.at, self.flying = {}, False, [], 0, False
        self.used, self.own_sems = 0, []
        if sided == SIDE_STEP:
            self.steps.append(("side", None, None))
        for item in order:
            if item == "z":
                for s in range(1, env.C):
                    self.steps.append(("z", s, dict(self.fixed)))
                self.z_done = True
            elif item == "d":
                self.steps.append(("d", None, dict(self.fixed)))
                self.z_done = True
            else:
                self.steps.append(("bit", item, (dict(self.fixed), self.z_done)))
                self.fixed[item] = env.bit(item)
        self.plans = [self.plan(i) for i in range(len(self.steps))]

    def view(self, fixed, zat):
        at = tuple(self.lead) + tuple(fixed.get(b, slice(None)) for b in self.bits)
        return at + (slice(None) if zat is None else zat, slice(None), self.cols)

    def plan(self, i):
        env = self.env
        kind, what, state = self.steps[i]
        moves = []
        if kind == "side":
            other = env.dp_xor(env.m - 1)
            moves.append((env.bit(env.m - 1) != env.core, self.view({}, None), other, env.bit(env.m - 1) == env.core,
                          self.view({}, None), other))
            return [self.bind(move, self.land[i]) for move in moves]
        active = self.active if not self.sided else (env.bit(env.m - 1) == env.core)
        if kind == "bit":
            fixed, z_done = state
            zat = env.z if z_done else None
            other = env.dp_xor(what)
            mine = env.bit(what)
            moves.append((active, self.view({**fixed, what: 1 - mine}, zat), other, active,
                          self.view({**fixed, what: mine}, zat), other))
            return [self.bind(move, self.land[i]) for move in moves]
        s, C, z = what, env.C, env.z
        if kind == "d":
            for n in range(1, C):
                to, source = lax.rem(z + n, C), lax.rem(z + C - n, C)
                moves.append((active, self.view(state, to), env.line(to), active, self.view(state, z), env.line(source)))
            return [self.bind(move, self.land[i].at[n]) for n, move in enumerate(moves)]
        zm = C - 1 - z
        for side, (p, sign) in enumerate(((z, 1), (zm, -1))):
            out_at = z + sign * (C - s)
            in_at = z + sign * (C - s - 1)
            moves.append((both(active, p < s), self.view(state, out_at), env.line(z + sign),
                          both(active, both(p >= 1, p <= s)), self.view(state, in_at), env.line(z - sign)))
        return [self.bind(move, self.land[i].at[side]) for side, move in enumerate(moves)]

    def bind(self, move, slot):
        send_if, src, to, recv_if, dst, source = move
        env = self.env
        if self.prior is None:
            sem_s, sem_r = env.sems.one(), env.sems.one()
            self.own_sems.append((sem_s, sem_r))
        else:
            sem_s, sem_r = self.prior.own_sems[self.used]
        credit = self.credits.at[self.used]
        self.used += 1
        return send_if, src, to, recv_if, dst, source, slot, sem_s, sem_r, credit

    def send(self, i):
        for n, (send_if, src, to, recv_if, dst, source, slot, sem_s, sem_r, credit) in enumerate(self.plans[i]):
            cp = self.copies[(i, n)] = push(self.buf.at[src], slot, sem_s, sem_r, to)

            def go():
                if self.prior is not None:
                    def empty():
                        pl.semaphore_wait(credit, 1)
                        self.prior.copies[(i, n)].wait_send()

                    when(self.earlier, empty)
                cp.start()

            when(send_if, go)
            if self.prior is not None:
                self.env.sent.append((send_if, cp))

    def take(self, i):
        direct = self.steps[i][0] == "d"
        groups = [self.plans[i]] if direct else [[plan] for plan in self.plans[i]]
        for group in groups:
            send_if, src, to, recv_if, dst = group[0][:5]

            def got():
                total = self.buf[dst].astype(F32) if direct else self.buf[dst]
                for _, _, to, _, _, source, slot, sem_s, sem_r, credit in group:
                    push(slot, slot, sem_s, sem_r, to).wait_recv()
                    total = total + slot[...].astype(total.dtype)
                self.buf[dst] = total.astype(BF16)
                if self.prior is None:
                    for _, _, _, _, _, source, _, _, _, credit in group:
                        pl.semaphore_signal(credit, inc=1, device_id=source, device_id_type=MESH)

            when(recv_if, got)

    def send_next(self):
        if not self.flying and self.at < len(self.steps):
            self.send(self.at)
            self.flying = True

    def take_next(self):
        if self.flying:
            self.take(self.at)
            self.at, self.flying = self.at + 1, False

    def finish(self):
        while self.at < len(self.steps):
            self.send_next()
            self.take_next()

    def own(self):
        return self.view(self.fixed, self.env.z)


def both(a, b):
    if a is True:
        return b
    if b is True:
        return a
    return jnp.logical_and(a, b)


def when(condition, fn):
    if condition is True:
        fn()
    else:
        pl.when(condition)(fn)


class Env:
    def __init__(self, C, m, core, dp, z, sems):
        self.C, self.m, self.core, self.dp, self.z, self.sems, self.sent = C, m, core, dp, z, sems, []

    def bit(self, b):
        return lax.rem(lax.div(self.dp, 1 << b), 2)

    def dp_xor(self, b):
        return (self.core, self.dp + (1 << b) * (1 - 2 * self.bit(b)), self.z)

    def line(self, z):
        return (self.core, self.dp, z)


def job_table(m):
    xs, ys = list(range(m)), list(range(m - 1, -1, -1))
    rest = list(range(m - 1))
    xz, yz = xs + ["z"], ys + ["z"]
    return {
        "P0": ("gproj", (0, 3), rest + ["z"], SIDED), "P1": ("gproj", (1, 3), rest + ["z"], SIDED),
        "P2": ("gproj", (2, 3), rest + ["z"], SIDED),
        "F0": ("gfc", (0, 3), xz, WHOLE), "F1": ("gfc", (1, 3), yz, WHOLE), "F2": ("gfc", (2, 3), xz, WHOLE),
        "O": ("gout", (0, 1), rest + ["z"], SIDE_STEP),
        "Q": ("gq", (0, 1), xs[:1] + ["z"] + xs[1:], WHOLE), "K": ("gk", (0, 1), yz, WHOLE), "V": ("gv", (0, 1), yz, WHOLE),
    }


def grad_shapes(C, m, D, F):
    H, FH, J = D // 2, F // 2, C << m
    full, side = (2,) * m + (C,), (2,) * (m - 1) + (C,)
    return {"gproj": side + (F // J, D), "gfc": full + (D // J, FH), "gout": side + (D // J, D),
            "gq": full + (D // J, H), "gk": full + (D // J, H), "gv": full + (D // J, H)}


def landing_shapes(C, m, D, F):
    shapes = grad_shapes(C, m, D, F)
    result = {}
    for name, (buf, (at, parts), order, sided) in job_table(m).items():
        shape = list(shapes[buf])
        shape[-1] //= parts
        n = m - 1 if sided else m
        lead = {b: 2 for b in range(n)}
        tail = [shape[-2], shape[-1]]
        zdim = [C]
        steps = []
        if sided == SIDE_STEP:
            steps.append(tuple([2] * n + zdim + tail))
        for item in order:
            if item == "z":
                zdim = []
                for s in range(1, C):
                    steps.append(tuple([2] + [2] * len(lead) + tail))
            elif item == "d":
                zdim = []
                steps.append(tuple([C - 1] + [2] * len(lead) + tail))
            else:
                lead.pop(item)
                steps.append(tuple([2] * len(lead) + zdim + tail))
        result[name] = steps
    return result


def norm_grad(values, gain, grad):
    unit, rstd = unit_norm(values)
    scaled = grad * gain
    m1 = jnp.mean(scaled, axis=-1, keepdims=True)
    m2 = jnp.mean(scaled * unit, axis=-1, keepdims=True)
    back = rstd * (scaled - m1 - unit * m2)
    return back, jnp.sum(grad * unit, axis=0, keepdims=True), jnp.sum(grad, axis=0, keepdims=True)


def attention_back_pair(i, T, L, q, k, v, o, lse, goa, bias, dq, dk, dv, dv_at):
    cols = slice(i * 128, (i + 1) * 128)
    lane = lax.broadcasted_iota(jnp.int32, (T, 128), 1)
    scale = jnp.asarray(HEAD**-0.5, BF16)
    totals = None
    for blk in (1, 0):
        rows = slice(blk * T, (blk + 1) * T)
        keys = L if blk else L // 2
        q2, go2 = q[rows, cols] * scale, goa[rows, cols]
        prod = go2.astype(F32) * o[rows, cols].astype(F32)
        k2, v2 = k[:keys, cols], v[:keys, cols]
        dqs, dks, dvs = [], None, None
        for h in range(2):
            sel = (lane >= 64) == (h == 1)
            qh = jnp.where(sel, q2, jnp.zeros_like(q2))
            goh = jnp.where(sel, go2, jnp.zeros_like(go2))
            delta = jnp.sum(jnp.where(sel, prod, 0.0), axis=-1, keepdims=True)
            s = mm_nt(qh, k2) + bias[rows, :keys].astype(F32)
            prob = jnp.exp(s - lse[rows, 2 * i + h : 2 * i + h + 1])
            gp = mm_nt(goh, v2)
            gs = (prob * (gp - delta)).astype(BF16)
            dqs.append(mm(gs, k2))
            one_k = mm_tn(gs, qh)
            one_v = mm_tn(prob.astype(BF16), goh)
            dks = one_k if dks is None else dks + one_k
            dvs = one_v if dvs is None else dvs + one_v
        dq[rows, cols] = (jnp.where(lane < 64, dqs[0], dqs[1]) * HEAD**-0.5).astype(BF16)
        if blk:
            totals = (dks, dvs)
        else:
            dk[:keys, cols] = (totals[0][:keys] + dks).astype(BF16)
            dk[keys:, cols] = totals[0][keys:].astype(BF16)
            dv[dv_at, :keys, cols] = (totals[1][:keys] + dvs).astype(BF16)
            dv[dv_at, keys:, cols] = totals[1][keys:].astype(BF16)


LOADED = ("gp", "act", "hh", "hr", "o", "q", "k", "v", "lse", "xall", "r")


def backward_kernel(C, m, T, D, F, fused, names_in, *refs):
    n_in = len(names_in)
    hbm = dict(zip(names_in, refs[:n_in]))
    outs, (vm, dma, credits) = refs[n_in:-3], refs[-3:]
    ends_o, small_o = outs[:2]
    core, dp, z = lax.axis_index(SECTION), lax.axis_index(DP), lax.axis_index(CTX)
    N, L, H, FH = C // 2, C * T, D // 2, F // 2
    row = lax.div(z, N)
    lo = z + row * (C - 1 - 2 * z)
    hi = C - 1 - lo
    base = row * N
    pairs = H // 128
    sems = Sems(dma)
    env = Env(C, m, core, dp, z, sems)
    sib = (1 - core, dp, z)
    mirror = (core, dp, C - 1 - z)
    pos = lambda blk: lo + blk * (hi - lo)
    block = lambda at: pl.ds(pl.multiple_of(at * T, T), T)
    other_nodes = [base + lax.rem(z - base + n, N) for n in range(1, N)]
    sent = env.sent
    loads = {}

    def load(name, l, src=None, dst=None):
        cp = pltpu.make_async_copy(hbm[name].at[l] if src is None else src, vm[name] if dst is None else dst, sems.one())
        cp.start()
        loads[(name, l)] = cp

    def need(*names):
        for name in names:
            loads[name].wait()

    def pushed(src, dst, to, condition=True, until=sent):
        cp = push(src, dst, sems.one(), sems.one(), to)
        when(condition, cp.start)
        until.append((condition, cp))
        return cp

    load("gy", 1, hbm["gy"].at[0], vm["gm"].at[0])
    load("gy", 0, hbm["gy"].at[1], vm["gm"].at[1])
    load("wproj", 1, dst=vm["wa"])
    load("gp", 1)
    load("wfc", 1)
    load("act", 1)
    load("hh", 1)
    load("hr", 1)
    load("sm", 0, hbm["sm"], vm["sm"])
    for name in ("o", "q", "k", "v", "lse", "xall", "r"):
        load(name, 1)
    y_keep = pltpu.make_async_copy(hbm["y"].at[block(row)], ends_o.at[0, row], sems.one())
    when(core == 1, y_keep.start)

    kseg = hbm["kseg"]
    for blk in range(2):
        rows = slice(blk * T, (blk + 1) * T)
        qpos = pos(blk) * T + lax.broadcasted_iota(jnp.int32, (T, L), 0)
        kpos = lax.broadcasted_iota(jnp.int32, (T, L), 1)
        mine = kseg[0:1, 0:T]
        for n in range(1, C):
            mine = jnp.where(pos(blk) == n, kseg[0:1, n * T : (n + 1) * T], mine)
        allowed = (kpos <= qpos) & (kseg[...] == column(mine))
        vm["bias"][rows, :] = jnp.where(allowed, 0.0, MASKED).astype(BF16)

    greet([sib] + [env.line(lax.rem(z + n, C)) for n in range(1, C)] + [env.dp_xor(b) for b in range(m)])

    y_push = pushed(hbm["yb"].at[block(1 - row)], vm["far"], mirror, core == 1)
    top = env.bit(m - 1) == core
    aside = jnp.logical_not(top)
    across = env.dp_xor(m - 1)
    act_push = pushed(hbm["act"].at[1], vm["act_in"], across, aside)
    gm_in_load = pltpu.make_async_copy(hbm["gm_in"], vm["gm_in"].at[1], sems.one())
    act_in_load = pltpu.make_async_copy(hbm["act_in"], vm["act_in"], sems.one())
    when(top, gm_in_load.start)
    gm_push = push(vm["gm"], vm["gm_in"].at[0], sems.one(), sems.one(), across)

    table = job_table(m)
    jobs = {}

    def start(name, l):
        if not fused:
            return
        buf, (at, parts), order, sided = table[name]
        width = vm[buf].shape[-1] // parts
        earlier = True if name != "V" else core == 1
        active = True if l == 0 else earlier
        jobs[(name, l)] = Job(env, vm[buf], (l,), slice(at * width, (at + 1) * width), order, sided, vm["land"][name],
                              credits[name], active, earlier, jobs.get((name, 1)))

    def move(code):
        job = jobs.get((JOBS[code % 10], code // 10 % 10)) if fused else None
        if job is not None:
            job.send_next() if code >= 100 else job.take_next()

    gm, gp, go, ghh, wa, wfc = vm["gm"], vm["gp"], vm["go"], vm["ghh"], vm["wa"], vm["wfc"]
    sm, sg = vm["sm"], vm["sg"]

    def put(buf, l, cols, value):
        shape = vm[buf].shape[1:-1] + (value.shape[-1],)
        vm[buf][(l,) + (slice(None),) * (len(shape) - 1) + (cols,)] = value.astype(BF16).reshape(shape)

    polls = iter(POLLS)

    def poll():
        for code in next(polls):
            move(code)

    def layer_back(l):
        again = []

        def proj_phase():
            def proj_grad():
                if l == 1:
                    act_push.wait_recv()
                    gm_in_load.wait()
                else:
                    act_in_load.wait()
                    gm_push.wait_recv()
                third = D // 3
                for n in range(3):
                    cols = slice(n * third, (n + 1) * third)
                    total = mm_tn(vm["act_in"][...], vm["gm_in"][l, :, :, cols].reshape(2 * T, third))
                    for blk in range(2):
                        total += mm_tn(vm["act"][blk * T : (blk + 1) * T, :], gm[blk, :, cols])
                    put("gproj", l, cols, total)

            need(("act", l))
            when(top, proj_grad)
            for n in range(3):
                start("P%d" % n, l)
            if l == 1:
                load("act", 0)
                when(top, act_in_load.start)

        need(("wproj", l), ("gp", l))
        bias_sum = None
        for blk in range(2):
            rows = slice(blk * T, (blk + 1) * T)
            if l == 1:
                need(("gy", 1 - blk))
                go[rows, :] = gm[blk].astype(F32)
            gu = (gp[rows, :].astype(F32) * mm_nt(gm[blk], wa[...])).astype(BF16)
            gp[rows, :] = gu
            part = jnp.sum(gu.astype(F32), axis=0, keepdims=True)
            bias_sum = part if bias_sum is None else bias_sum + part
            if blk == 0:
                poll()
        sg[l, 4:5, :] = bias_sum
        load("watt", l, dst=wa)
        poll()
        need(("hh", l))
        third = FH // 3
        for i in (0, 1, 2):
            cols = slice(i * third, (i + 1) * third)
            put("gfc", l, cols, mm_tn(vm["hh"][...], gp[:, cols]))
            start("F%d" % i, l)
            poll()
        need(("wfc", l))
        shares = []
        for blk in range(2):
            rows = slice(blk * T, (blk + 1) * T)
            part = mm_nt(gp[rows, :], wfc[...])
            ghh[rows, :] = part
            vm["a_s"][rows, :] = part.astype(BF16)
            shares.append(pushed(vm["a_s"].at[rows, :], vm["a_r"].at[rows, :], sib, until=[]))
            poll()
        if l == 1:
            load("wfc", 0)
        poll()
        if l == 1:
            load("hh", 0)
            load("gp", 0)
        need(("hr", l), ("watt", l))
        if l == 1:
            need(("sm", 0))
        sums = None
        for blk in range(2):
            rows = slice(blk * T, (blk + 1) * T)
            shares[blk].wait_recv()
            grad = ghh[rows, :] + vm["a_r"][rows, :].astype(F32)
            back, gain_sum, bias_sum = norm_grad(vm["hr"][rows, :], sm[l, 2:3, :D], grad)
            total = go[rows, :] + back
            go[rows, :] = total
            low = total.astype(BF16)
            vm["gb"][rows, :] = low
            vm["goa"][rows, :] = mm_nt(low, wa[D : D + H, :]).astype(BF16)
            poll()
            sums = (gain_sum, bias_sum) if sums is None else (sums[0] + gain_sum, sums[1] + bias_sum)
        sg[l, 2:3, :D] = sums[0]
        sg[l, 3:4, :D] = sums[1]
        poll()
        if l == 1:
            load("hr", 0)
        need(("o", l))
        put("gout", l, slice(0, D), mm_tn(vm["o"][...], vm["gb"][...]))
        start("O", l)
        poll()
        need(("q", l), ("k", l), ("v", l), ("lse", l))
        for i in range(pairs):
            attention_back_pair(i, T, L, vm["q"], vm["k"], vm["v"], vm["o"], vm["lse"], vm["goa"], vm["bias"], vm["dq"],
                                vm["dk"], vm["dv"], l)
            if i == PROJ_AT[l]:
                proj_phase()
            poll()
        if l == 1:
            for name in ("o", "q", "k", "v", "lse"):
                load(name, 0)
        else:
            def merge():
                vm["dv"][0] = (vm["dv"][0].astype(F32) + vm["dv"][1].astype(F32)).astype(BF16)

            when(core == 0, merge)
        dk, dv, dq = vm["dk"], vm["dv"], vm["dq"]

        def key_part(at):
            part_v = dv[l, block(at), :]
            if l == 1:
                part_v = jnp.where(core == 1, part_v, jnp.zeros_like(part_v))
            return mm_nt(dk[block(at), :], wa[:D, H:]) + mm(part_v, wa[D + H :, :])

        crossing, gives = [], []
        for n, node in enumerate(other_nodes):
            dlo = node + row * (C - 1 - 2 * node)
            dhi = C - 1 - dlo
            vm["fs_s"][n] = key_part(dlo + (1 - core) * (dhi - dlo)).astype(BF16)
            gives.append(pushed(vm["fs_s"].at[n], vm["fs_r"].at[n], sib, until=again))
        poll()
        for n, node in enumerate(other_nodes):
            dlo = node + row * (C - 1 - 2 * node)
            keep = key_part(dlo + core * (C - 1 - 2 * dlo))
            gives[n].wait_recv()
            vm["fx_s"][n] = (keep + vm["fs_r"][n].astype(F32)).astype(BF16)
            crossing.append(pushed(vm["fx_s"].at[n], vm["fx_r"].at[l, n], (core, dp, node), until=again))
        poll()
        for blk in range(2):
            rows = slice(blk * T, (blk + 1) * T)
            ghh[rows, :] = key_part(pos(blk)) + mm_nt(dq[rows, :], wa[:D, :H])
            poll()
        for cp in shares:
            cp.wait_send()
        early = pl.ds(pl.multiple_of((1 - core) * T, T), T)
        late = pl.ds(pl.multiple_of(core * T, T), T)
        vm["a_s"][early, :] = ghh[early, :].astype(BF16)
        shares = [pushed(vm["a_s"].at[early, :], vm["b_r"].at[early, :], sib, until=again)]
        if l == 1:
            load("wproj", 0, dst=wa)
        poll()
        need(("xall", l))
        xall = vm["xall"]
        put("gk", l, slice(0, H), mm_tn(xall[...], dk[...]))
        start("K", l)
        poll()
        put("gq", l, slice(0, H), mm_tn(xall[block(lo), :], dq[:T, :]) + mm_tn(xall[block(hi), :], dq[T:, :]))
        start("Q", l)
        poll()
        put("gv", l, slice(0, H), mm_tn(xall[...], dv[l]))
        start("V", l)
        if PROJ_AT[l] == 3:
            proj_phase()
        poll()
        if l == 1:
            load("xall", 0)
        need(("r", l))
        for n in range(N - 1):
            crossing[n].wait_recv()
            ghh[late, :] += vm["fx_r"][l, n].astype(F32)
        vm["a_s"][late, :] = ghh[late, :].astype(BF16)
        shares.append(pushed(vm["a_s"].at[late, :], vm["b_r"].at[late, :], sib, until=again))
        poll()
        for cp in shares:
            cp.wait_recv()
        sums = None
        for blk in range(2):
            rows = slice(blk * T, (blk + 1) * T)
            grad = ghh[rows, :] + vm["b_r"][rows, :].astype(F32)
            back, gain_sum, bias_sum = norm_grad(vm["r"][rows, :].astype(F32), sm[l, 0:1, :D], grad)
            total = go[rows, :] + back
            go[rows, :] = total
            if l == 1:
                gm[blk] = total.astype(BF16)
            poll()
            sums = (gain_sum, bias_sum) if sums is None else (sums[0] + gain_sum, sums[1] + bias_sum)
        sg[l, 0:1, :D] = sums[0]
        sg[l, 1:2, :D] = sums[1]
        poll()
        if l == 1:
            load("r", 0)
            when(aside, gm_push.start)
            sent.append((aside, gm_push))
        for condition, cp in again:
            when(condition, cp.wait_send)

    layer_back(1)
    layer_back(0)

    keep = pl.ds(pl.multiple_of(row * T, T), T)
    away = pl.ds(pl.multiple_of((1 - row) * T, T), T)
    vm["gb"][:T, :] = go[away, :].astype(BF16)
    x_push = pushed(vm["gb"].at[pl.ds(0, T), :], vm["far"], mirror, core == 0)
    x_keep = pltpu.make_async_copy(go.at[keep, :], ends_o.at[0, row], sems.one())
    when(core == 0, x_keep.start)

    sv, sv_r = vm["sv"], vm["sv_r"]
    sv[0] = jnp.zeros_like(sv[0])
    sv[0, 0:4, :] = sg[core, 0:4, :]
    sv[0, 4:5, :] = sg[0, 4:5, :]
    sv[0, 5:6, :] = sg[1, 4:5, :]
    around = [env.dp_xor(b) for b in range(m)]
    b = 1
    while b < C:
        around.append(env.line(z + b * (1 - 2 * lax.rem(lax.div(z, b), 2))))
        b *= 2
    small_at = [0]
    small_cp = [pushed(sv.at[0], sv_r.at[0], around[0])]

    last = len(around)

    def bias_halves():
        vm["fb_s"][...] = jnp.where(core == 0, sv[last, 5:6, :], sv[last, 4:5, :])
        cp = pushed(vm["fb_s"], vm["fin"]["fb"], sib)
        if not fused:
            cp.wait_recv()
            return
        ours = jnp.where(core == 0, sv[last, 4:5, :], sv[last, 5:6, :])
        j, J = dp * C + z, C << m
        norms = own_part(sv[last, :, :D], j, J)
        for i in range(4):
            vm["parts"][1 + i][...] = norms[i : i + 1, :]
        cp.wait_recv()
        theirs = vm["fin"]["fb"][...]
        bias = jnp.concatenate([jnp.where(core == 0, ours, theirs), jnp.where(core == 0, theirs, ours)], axis=1)
        vm["parts"][0][...] = own_part(jnp.broadcast_to(bias, (8, F)), j, J)[0:1, :]

    def small_step():
        i = small_at[0]
        if i == len(around):
            return
        small_cp[0].wait_recv()
        sv[i + 1] = sv[i] + sv_r[i]
        small_at[0] += 1
        if i + 1 < len(around):
            small_cp[0] = pushed(sv.at[i + 1], sv_r.at[i + 1], around[i + 1])
        else:
            bias_halves()

    def finish_ends():
        when(core == 0, x_push.wait_recv)
        when(core == 1, y_push.wait_recv)
        vm["ghh"][:T, :] = vm["far"][...].astype(F32)
        far_keep = pltpu.make_async_copy(vm["ghh"].at[pl.ds(0, T), :], ends_o.at[0, 1 - row], sems.one())
        far_keep.start()
        far_keep.wait()
        when(core == 0, x_keep.wait)
        when(core == 1, y_keep.wait)

    if fused:
        for code in TAIL:
            if code == SMALL:
                small_step()
            else:
                move(code)
        for job in jobs.values():
            job.finish()
    while small_at[0] < len(around):
        small_step()

    if fused:
        hand_over(core, sib, env, vm, jobs, m, D, H, FH, pushed, sv, last)
        results = list(zip(vm["stage"], outs[7:]))
    else:
        results = [(vm[name], out) for name, out in zip(("gproj", "gfc", "gout", "gq", "gk", "gv"), outs[7:])]
    results += [(sv.at[last], small_o)] + list(zip(vm["parts"], outs[2:7]))
    results = [pltpu.make_async_copy(src, dst, sems.one()) for src, dst in results]
    for cp in results:
        cp.start()
    finish_ends()
    for condition, cp in sent:
        when(condition, cp.wait_send)
    for cp in results:
        cp.wait()


def hand_over(core, sib, env, vm, jobs, m, D, H, FH, pushed, sv, last):
    qkv_o, out_o, fc_o, proj_o, shared_o = vm["stage"]
    fin = vm["fin"]
    top = env.bit(m - 1) == core
    own = lambda name, l: (l,) + jobs[(name, 0)].own()[1:]
    arrive = [
        pushed(vm["gfc"].at[own("F0", 1 - core)[:-1]], fin["fc"], sib),
        pushed(vm["gq"].at[own("Q", 1 - core)], fin["q"], sib),
        pushed(vm["gk"].at[own("K", 1 - core)], fin["k"], sib),
        pushed(vm["gv"].at[own("V", 0)], fin["v"], sib),
    ]
    out_push = pushed(vm["gout"].at[own("O", 1 - core)], fin["out"], sib, top)
    proj_push = pushed(vm["gproj"].at[own("P0", 1 - core)[:-1]], fin["proj"], sib, top)

    here = pl.ds(pl.multiple_of(core * H, 128), H)
    there = pl.ds(pl.multiple_of((1 - core) * H, 128), H)
    here_k = pl.ds(pl.multiple_of(D + core * H, 128), H)
    there_k = pl.ds(pl.multiple_of(D + (1 - core) * H, 128), H)
    qkv_o[0, :, here] = vm["gq"][own("Q", core)].astype(F32)
    qkv_o[0, :, here_k] = vm["gk"][own("K", core)].astype(F32)
    fc_o[0, :, pl.ds(pl.multiple_of(core * FH, 128), FH)] = vm["gfc"][own("F0", core)[:-1]].astype(F32)

    def top_out():
        out_o[0] = vm["gout"][own("O", core)].astype(F32)
        proj_o[0] = vm["gproj"][own("P0", core)[:-1]].astype(F32)

    when(top, top_out)
    for cp in arrive:
        cp.wait_recv()

    def other_out():
        out_push.wait_recv()
        proj_push.wait_recv()
        out_o[0] = fin["out"][...].astype(F32)
        proj_o[0] = fin["proj"][...].astype(F32)

    when(jnp.logical_not(top), other_out)
    qkv_o[0, :, there] = fin["q"][...].astype(F32)
    qkv_o[0, :, there_k] = fin["k"][...].astype(F32)
    fc_o[0, :, pl.ds(pl.multiple_of((1 - core) * FH, 128), FH)] = fin["fc"][...].astype(F32)
    fresh = pl.ds(2 * D, H)

    def fresh_first():
        qkv_o[0, :, fresh] = fin["v"][...].astype(F32)
        shared_o[...] = vm["gv"][own("V", 0)].astype(F32)

    def fresh_second():
        qkv_o[0, :, fresh] = vm["gv"][own("V", 1)].astype(F32)
        shared_o[...] = fin["v"][...].astype(F32)

    when(core == 0, fresh_first)
    when(core == 1, fresh_second)


def backward_pass(C, m, T, D, F, inputs):
    N, L, H, FH, R, J = C // 2, C * T, D // 2, F // 2, 2 * T, C << m
    fused = (D // J) % 16 == 0 and (F // J) % 16 == 0 and m > 0
    pairs = H // 128
    S, V = jax.ShapeDtypeStruct, pltpu.VMEM
    names = tuple(inputs)
    outs, stage = [S((1, 2, T, D), F32), S((8, FH), F32), S((1, F // J), F32)] + [S((1, D // J), F32)] * 4, []
    flat = {"gproj": (FH, D), "gfc": (D, FH), "gout": (H, D), "gq": (D, H), "gk": (D, H), "gv": (D, H)}
    if fused:
        outs += [S((1, D // J, 5 * H), F32), S((1, D // J, D), F32), S((1, D // J, F), F32), S((1, F // J, D), F32),
                 S((D // J, H), F32)]
        stage = [V(out.shape, F32) for out in outs[7:]]
        grads = grad_shapes(C, m, D, F)
        land = {name: [V(shape, BF16) for shape in steps] for name, steps in landing_shapes(C, m, D, F).items()}
    else:
        outs += [S((2,) + shape, BF16) for shape in flat.values()]
        grads, land = flat, {}
    stages = m + C.bit_length() - 1
    vm = dict(
        gm=V((2, T, D), BF16), gb=V((R, D), BF16), gm_in=V((2, 2, T, D), BF16), act_in=V((R, FH), BF16), gp=V((R, FH), BF16), act=V((R, FH), BF16), hh=V((R, D), BF16), hr=V((R, D), F32),
        o=V((R, H), BF16), q=V((R, H), BF16), k=V((L, H), BF16), v=V((L, H), BF16), lse=V((R, 128), F32),
        xall=V((L, D), BF16), r=V((R, D), BF16), sm=V((2, 8, F), F32), sg=V((2, 8, FH), F32), bias=V((R, L), BF16),
        wa=V((2 * D, D), BF16), wfc=V((D, FH), BF16), go=V((R, D), F32), ghh=V((R, D), F32), a_s=V((R, D), BF16),
        a_r=V((R, D), BF16), b_r=V((R, D), BF16), goa=V((R, H), BF16), dq=V((R, H), BF16),
        dk=V((L, H), BF16), dv=V((2, L, H), BF16), fs_s=V((N - 1, T, D), BF16), fs_r=V((N - 1, T, D), BF16),
        fx_s=V((N - 1, T, D), BF16), fx_r=V((2, N - 1, T, D), BF16), far=V((T, D), BF16),
        sv=V((stages + 1, 8, FH), F32), sv_r=V((stages, 8, FH), F32), fb_s=V((1, FH), F32),
        fin=dict(fc=V((D // J, FH), BF16), q=V((D // J, H), BF16), k=V((D // J, H), BF16), v=V((D // J, H), BF16),
                 out=V((D // J, D), BF16), proj=V((F // J, D), BF16), fb=V((1, FH), F32)),
        land=land, stage=stage, parts=[V(out.shape, F32) for out in outs[2:7]], **{name: V((2,) + shape, BF16) for name, shape in grads.items()})
    moves = {name: len(order) - 1 + ("z" in order) * (C - 1) + C - 1 + (sided == SIDE_STEP) for name, (_, _, order, sided) in job_table(m).items()}
    credits = {name: pltpu.SemaphoreType.REGULAR((n,)) for name, n in moves.items()} if fused else {}
    semaphores = 60 + 2 * stages + 8 * (N - 1) + (25 + 2 * sum(moves.values()) if fused else 14)
    in_specs = [VM if name == "kseg" else HBM for name in names]
    return pl.pallas_call(
        functools.partial(backward_kernel, C, m, T, D, F, fused, names),
        in_specs=in_specs,
        out_specs=[HBM] * len(outs),
        out_shape=outs,
        scratch_shapes=[vm, pltpu.SemaphoreType.DMA((semaphores,)), credits],
        compiler_params=pltpu.CompilerParams(collective_id=1, has_side_effects=True, vmem_limit_bytes=VMEM_LIMIT),
        name="backward_pass",
    )(*inputs.values())


def xor_route(size, bit):
    return [(i, i ^ (1 << bit)) for i in range(size)]


def halve(grad, axis_name, bit, at):
    mine = (lax.axis_index(axis_name) >> bit) & 1
    keep = lax.dynamic_index_in_dim(grad, mine, at, keepdims=False)
    send = lax.dynamic_index_in_dim(grad, 1 - mine, at, keepdims=False)
    got = lax.ppermute(send, axis_name, xor_route(lax.axis_size(axis_name), bit))
    return (keep.astype(F32) + got.astype(F32)).astype(grad.dtype)


def bits_of(axis_name):
    return lax.axis_size(axis_name).bit_length() - 1


def scatter_sum(grad, order, skip_first=False):
    dims = [(DP, b) for b in reversed(range(bits_of(DP)))] + [(CTX, b) for b in reversed(range(bits_of(CTX)))]
    if skip_first:
        dims = dims[1:]
    parts = len(dims)
    rows, cols = grad.shape
    grad = grad.reshape((2,) * parts + (rows >> parts, cols))
    for item in order:
        at = dims.index(item)
        grad = halve(grad, item[0], item[1], at)
        dims.pop(at)
    return grad


def shards(ends, segment_ids, ln1_gain, ln1_bias, qkv_weight, out_weight, ln2_gain, ln2_bias, fc_weight, fc_bias,
           proj_weight, shared_weight):
    core = lax.axis_index(SECTION)
    first = core == 0
    C, m = lax.axis_size(CTX), bits_of(DP)
    J = C << m
    micros, T, D = ends.shape[1:]
    F = fc_weight.shape[2]
    half, FH = D // 2, F // 2
    names = ("xall", "q", "k", "v", "o", "lse", "r", "hr", "hh", "gp", "act", "y", "yb", "gy", "sm", "watt", "wfc", "wproj", "act_in", "gm_in", "kseg")
    kept = dict(zip(names, forward_pass(
        C, m, ends, segment_ids, ln1_gain, ln1_bias, ln2_gain, ln2_bias, qkv_weight, out_weight,
        fc_weight, fc_bias, proj_weight, shared_weight)))
    block, small, fcb_out, *rest = backward_pass(C, m, T, D, F, kept)
    ln, grads = rest[:4], rest[4:]
    if len(grads) != 5:
        theirs = swap(jnp.where(first, small[5], small[4]))
        ours = jnp.where(first, small[4], small[5])
        bias = jnp.where(first, jnp.concatenate([ours, theirs]), jnp.concatenate([theirs, ours]))
        j = lax.axis_index(DP) * C + lax.axis_index(CTX)
        fcb_out = lax.dynamic_slice_in_dim(bias, j * (F // J), F // J, 0)[None]
        ln = [lax.dynamic_slice_in_dim(small[i : i + 1, :D], j * (D // J), D // J, 1) for i in range(4)]
        grads = scattered(grads, core, m, half)
    block, fcb_out, *rest = assemble([block, fcb_out, *ln, *grads])
    ln, (qkv_out, out_out, fc_out, proj_out, shared_out) = rest[:4], rest[4:]
    return (block, qkv_out, out_out, fc_out, fcb_out, proj_out, shared_out, *ln)


def own_part(values, j, J):
    width = values.shape[1] // J
    at = lax.broadcasted_iota(jnp.int32, (values.shape[1], width), 0) - j * width
    pick = (at == lax.broadcasted_iota(jnp.int32, (values.shape[1], width), 1)).astype(F32)
    return jnp.dot(values, pick, precision=lax.Precision.HIGHEST, preferred_element_type=F32)


def assemble_kernel(*refs):
    n = (len(refs) - 2) // 2
    ins, outs, bounce, dma = refs[:n], refs[n:-2], refs[-2], refs[-1]
    come = [pltpu.make_async_copy(a, b, dma.at[i]) for i, (a, b) in enumerate(zip(ins, bounce))]
    for cp in come:
        cp.start()
    copies = []
    for i in range(n):
        come[i].wait()
        copies.append(pltpu.make_async_copy(bounce[i], outs[i], dma.at[i]))
        copies[-1].start()
    for cp in copies:
        cp.wait()


def assemble(arrays):
    return pl.pallas_call(
        assemble_kernel,
        in_specs=[HBM] * len(arrays),
        out_specs=[HBM] * len(arrays),
        out_shape=[jax.ShapeDtypeStruct(a.shape, a.dtype) for a in arrays],
        scratch_shapes=[[pltpu.VMEM(a.shape, a.dtype) for a in arrays], pltpu.SemaphoreType.DMA((len(arrays),))],
        compiler_params=pltpu.CompilerParams(vmem_limit_bytes=VMEM_LIMIT),
        name="assemble",
    )(*arrays)


def scattered(grads, core, m, half):
    gproj, gfc, gout, gq, gk, gv = grads
    first = core == 0
    x_first = [(DP, b) for b in range(m)] + [(CTX, b) for b in range(bits_of(CTX))]
    y_first = [(DP, b) for b in reversed(range(m))] + x_first[m:]

    def sided(grad):
        dp, size = lax.axis_index(DP), lax.axis_size(DP)
        top = size // 2
        route = [(c * size + d, c * size + (d ^ top)) for c in range(2) for d in range(size) if (d >= top) != (c == 1)]
        got = lax.ppermute(grad, (SECTION, DP), route)
        return scatter_sum((grad.astype(F32) + got.astype(F32)).astype(BF16), y_first[1:], skip_first=True)

    res = []
    for l in range(2):
        qkv = jnp.concatenate([gq[l], gk[l], gv[l]], axis=1)
        res.append((scatter_sum(qkv, x_first), sided(gout[l]), scatter_sum(gfc[l], x_first),
                    scatter_sum(gproj[l], y_first[1:], skip_first=True)))
    holder = jnp.where(lax.axis_index(DP) >= lax.axis_size(DP) // 2, 1, 0) == core
    mine = tuple(jnp.where(first, a, b) for a, b in zip(res[0], res[1]))
    got = tuple(swap(jnp.where(first, b, a)) for a, b in zip(res[0], res[1]))
    left, right = [jnp.where(first, a, b).astype(F32) for a, b in zip(mine, got)], [jnp.where(first, b, a).astype(F32) for a, b in zip(mine, got)]
    fresh0 = res[0][0][:, 2 * half :]
    fresh0_other = swap(fresh0)
    fresh = jnp.where(first, fresh0_other, res[1][0][:, 2 * half :]).astype(F32)
    qkv_out = jnp.concatenate([left[0][:, :half], right[0][:, :half], left[0][:, half : 2 * half], right[0][:, half : 2 * half], fresh], axis=1)
    fc_out = jnp.concatenate([left[2], right[2]], axis=1)
    out_out = jnp.where(holder, mine[1], got[1]).astype(F32)
    proj_out = jnp.where(holder, mine[3], got[3]).astype(F32)
    shared_out = jnp.where(first, fresh0, fresh0_other).astype(F32)
    return qkv_out[None], out_out[None], fc_out[None], proj_out[None], shared_out


def solution(mesh):
    placed = (
        P(SECTION, DP, CTX, None), P(DP, CTX), P(SECTION, None), P(SECTION, None),
        P(SECTION, None, None), P(SECTION, None, None), P(SECTION, None), P(SECTION, None),
        P(SECTION, None, None), P(SECTION, None), P(SECTION, None, None), P(),
    )
    both = (DP, CTX)
    return jax.shard_map(
        shards, mesh=mesh, in_specs=placed,
        out_specs=(P(SECTION, DP, CTX, None), P(SECTION, both, None), P(SECTION, both, None),
                   P(SECTION, both, None), P(SECTION, both), P(SECTION, both, None), P(both, None),
                   P(SECTION, both), P(SECTION, both), P(SECTION, both), P(SECTION, both)),
        check_vma=False,
    )
```

```python
import functools

import jax
import jax.numpy as jnp
from jax import lax
from jax.experimental import pallas as pl
from jax.experimental.pallas import tpu as pltpu
from jax.sharding import PartitionSpec as P

HEAD = 64
SECTION, DP, CTX = "section", "dp", "ctx"
EPSILON = 1e-05
MASKED = -1000000000.0
F32 = jnp.float32
BF16 = jnp.bfloat16
VMEM_LIMIT = 127 * 2**19


def mm(left, right):
    return jnp.dot(left, right, preferred_element_type=F32)


def mm_nt(left, right):
    return lax.dot_general(left, right, (((1,), (1,)), ((), ())), preferred_element_type=F32)


def mm_tn(left, right):
    return lax.dot_general(left, right, (((0,), (0,)), ((), ())), preferred_element_type=F32)


def unit_norm(values):
    mean = jnp.mean(values, axis=-1, keepdims=True)
    centred = values - mean
    rstd = lax.rsqrt(jnp.mean(centred * centred, axis=-1, keepdims=True) + EPSILON)
    return centred * rstd, rstd


def layer_norm(values, gain, bias):
    return unit_norm(values)[0] * gain + bias


def gelu_both(u):
    t = jnp.tanh(0.7978845608028654 * (u + 0.044715 * u * u * u))
    half = 0.5 * (1.0 + t)
    return u * half, half + 0.5 * u * (1.0 - t * t) * (0.7978845608028654 + 3 * 0.044715 * 0.7978845608028654 * u * u)


def swap(x):
    return lax.ppermute(x, SECTION, [(0, 1), (1, 0)])


MESH = pl.DeviceIdType.MESH
HBM = pl.BlockSpec(memory_space=pl.ANY)
VM = pl.BlockSpec(memory_space=pltpu.VMEM)


class Sems:
    def __init__(self, ref):
        self.ref, self.used = ref, 0

    def one(self):
        self.used += 1
        return self.ref.at[self.used - 1]


def push(src, dst, send, recv, to):
    return pltpu.make_async_remote_copy(src_ref=src, dst_ref=dst, send_sem=send, recv_sem=recv, device_id=to,
                                        device_id_type=MESH)


def greet(peers):
    barrier = pltpu.get_barrier_semaphore()
    for peer in peers:
        pl.semaphore_signal(barrier, inc=1, device_id=peer, device_id_type=MESH)
    pl.semaphore_wait(barrier, len(peers))


def attention_unit(first, l, blk, key_blocks, T, pairs, q, k, v, bias, acc, top_of, sum_of):
    rows = pl.ds(pl.multiple_of(blk * T, T), T)
    lane = lax.broadcasted_iota(jnp.int32, (T, 128), 1)
    blocks = [pl.ds(pl.multiple_of(at * T, T), T) for at in key_blocks]
    mask = jnp.concatenate([bias[rows, pl.ds(pl.multiple_of(at * T, 128), T)] for at in key_blocks], axis=1)

    def body(i, carry):
        cols = pl.ds(pl.multiple_of(i * 128, 128), 128)
        q2 = q[l, rows, cols] * jnp.asarray(HEAD**-0.5, BF16)
        k2 = jnp.concatenate([k[l, at, cols] for at in blocks], axis=0)
        v2 = jnp.concatenate([v[l, at, cols] for at in blocks], axis=0)
        v2 = jnp.concatenate([v2, jnp.ones_like(v2)], axis=1)
        sums, tops = [], []
        for h in range(2):
            qh = jnp.where((lane >= 64) == (h == 1), q2, jnp.zeros_like(q2))
            s = mm_nt(qh, k2) + mask
            top = jnp.max(s, axis=-1, keepdims=True)
            sums.append(mm(jnp.exp(s - top).astype(BF16), v2))
            tops.append(top)
        top = jnp.where(lane < 64, tops[0], tops[1])
        total = jnp.where(lane < 64, sums[0][:, 128:], sums[1][:, 128:])
        part = jnp.where(lane < 64, sums[0][:, :128], sums[1][:, :128])
        if not first:
            old = top_of[i, rows, :]
            new = jnp.maximum(old, top)
            keep, add = jnp.exp(old - new), jnp.exp(top - new)
            total = keep * sum_of[i, rows, :] + add * total
            part = keep * acc[i, rows, :] + add * part
            top = new
        top_of[i, rows, :] = top
        sum_of[i, rows, :] = total
        acc[i, rows, :] = part
        return carry

    lax.fori_loop(0, pairs, body, 0)


def attention_end(l, blk, T, pairs, o, lse, acc, top_of, sum_of):
    rows = slice(blk * T, (blk + 1) * T)
    lane = lax.broadcasted_iota(jnp.int32, (T, 128), 1)
    logs = jnp.zeros((T, 128), F32)
    for i in range(pairs):
        total = sum_of[i, rows, :]
        o[l, rows, i * 128 : (i + 1) * 128] = (acc[i, rows, :] / total).astype(BF16)
        log = top_of[i, rows, :] + jnp.log(total)
        logs = jnp.where(lane == 2 * i, log[:, 0:1], jnp.where(lane == 2 * i + 1, log[:, 64:65], logs))
    lse[l, rows, :] = logs


def column(row_values):
    T = row_values.shape[1]
    at = lax.broadcasted_iota(jnp.int32, (T, T), 0) == lax.broadcasted_iota(jnp.int32, (T, T), 1)
    spread = jnp.where(at, jnp.broadcast_to(row_values, (T, T)), 0).astype(F32)
    return jnp.sum(spread, axis=1, keepdims=True).astype(jnp.int32)


def forward_kernel(C, m, T, D, F, ends, segs, g1, b1, g2, b2, qkv, wo, fc, fcb, proj, shared,
                   xall_o, q_o, k_o, v_o, o_o, lse_o, r_o, hr_o, hh_o, gp_o, act_o, y_o, yb_o, gy_o, sm_o, watt_o, wfc_o, wproj_o,
                   act_in_o, gm_in_o, kseg_o,
                   e, seg, segv, sm, wqk, wv, wout, wfc, wproj, xall, q, k, v, o, lse, r, hr, hh, gp, act, y, yb, wvt, bias,
                   acc, top_of, sum_of, br_s, br_r, ml_s, ml_r, dma):
    core, dp, z = lax.axis_index(SECTION), lax.axis_index(DP), lax.axis_index(CTX)
    N, L, H, FH = C // 2, C * T, D // 2, F // 2
    T2 = T // 2
    row = z // N
    lo = z + row * (C - 1 - 2 * z)
    hi = C - 1 - lo
    base = row * N
    pairs = H // 128
    sems = Sems(dma)
    sib = (1 - core, dp, z)
    mirror = (core, dp, C - 1 - z)
    top_bit = lax.div(dp, 1 << (m - 1))
    across = (core, dp + (1 - 2 * top_bit) * (1 << (m - 1)), z)
    owner = top_bit == core
    ahead = [(core, dp, base + lax.rem(z - base + n, N)) for n in range(1, N)]
    behind = [base + lax.rem(z - base + N - n, N) for n in range(1, N)]
    line = [(core, dp, lax.rem(z + n, C)) for n in range(1, C)]
    pos = lambda blk: lo + blk * (hi - lo)
    rows_at = lambda p: pl.ds(pl.multiple_of(p * T, T), T)
    saves = []

    def save(src, dst):
        cp = pltpu.make_async_copy(src, dst, sems.one())
        cp.start()
        saves.append(cp)

    e_load = pltpu.make_async_copy(ends.at[0, row], e.at[core, row], sems.one())
    e_load.start()
    qc = pl.ds(pl.multiple_of(core * H, 128), H)
    kc = pl.ds(pl.multiple_of(D + core * H, 128), H)
    qo = pl.ds(pl.multiple_of((1 - core) * H, 128), H)
    ko = pl.ds(pl.multiple_of(D + (1 - core) * H, 128), H)
    loads = [
        pltpu.make_async_copy(qkv.at[0, :, qc], wqk.at[core, :, pl.ds(0, H)], sems.one()),
        pltpu.make_async_copy(qkv.at[0, :, kc], wqk.at[core, :, pl.ds(H, H)], sems.one()),
        pltpu.make_async_copy(wo.at[0, pl.ds(pl.multiple_of(core * H, H), H), :], wout.at[core], sems.one()),
        pltpu.make_async_copy(fc.at[0, :, pl.ds(pl.multiple_of(core * FH, 128), FH)], wfc.at[core], sems.one()),
        pltpu.make_async_copy(proj.at[0, pl.ds(pl.multiple_of(core * FH, FH), FH), :], wproj.at[core], sems.one()),
    ]
    for cp in loads:
        cp.start()
    v_sem = sems.one()
    v_shared = pltpu.make_async_copy(shared, wv.at[0], v_sem)
    v_fresh = pltpu.make_async_copy(qkv.at[0, :, pl.ds(2 * D, H)], wv.at[1], v_sem)

    @pl.when(core == 0)
    def _():
        v_shared.start()

    @pl.when(core == 1)
    def _():
        v_fresh.start()

    segv[0] = segs[0:1, :]
    segv[1] = segs[1:2, :]
    seg[z] = segv[row]
    sm[core] = jnp.zeros_like(sm[core])
    sm[core, 0:1, :D] = g1[...]
    sm[core, 1:2, :D] = b1[...]
    sm[core, 2:3, :D] = g2[...]
    sm[core, 3:4, :D] = b2[...]
    sm[core, 4:5, :] = fcb[...]

    greet([sib, across] + line)

    own_s, own_r = sems.one(), sems.one()
    own_push = push(ends.at[0, row], e.at[core, row], own_s, own_r, sib)
    own_come = push(ends.at[0, row], e.at[1 - core, row], own_s, own_r, sib)
    seg_push = []
    for n in range(1, C):
        to = lax.rem(z + n, C)
        cp = push(segv.at[lax.div(to, N)], seg.at[z], sems.one(), sems.one(), line[n - 1])
        cp.start()
        seg_push.append(cp)
    far_push, far_come, fwd_push, fwd_come = [], [], [], []
    for h in range(2):
        part = pl.ds(h * T2, T2)
        far_s, far_r, fwd_s, fwd_r = sems.one(), sems.one(), sems.one(), sems.one()
        far_push.append(push(ends.at[0, 1 - row, part], e.at[core, row, part], far_s, far_r, mirror))
        far_come.append(push(ends.at[0, 1 - row, part], e.at[core, 1 - row, part], far_s, far_r, mirror))
        here, there = e.at[core, 1 - row, part], e.at[1 - core, 1 - row, part]
        fwd_push.append(push(here, here, fwd_s, fwd_r, sib))
        fwd_come.append(push(there, there, fwd_s, fwd_r, sib))

    @pl.when(core == 0)
    def _():
        for cp in far_push:
            cp.start()

    own_push.start()
    sm_push = push(sm.at[core], sm.at[core], sems.one(), sems.one(), sib)
    sm_push.start()
    qk_push = [
        push(qkv.at[0, :, qo], wqk.at[core, :, pl.ds(0, H)], sems.one(), sems.one(), sib),
        push(qkv.at[0, :, ko], wqk.at[core, :, pl.ds(H, H)], sems.one(), sems.one(), sib),
    ]
    for cp in qk_push:
        cp.start()
    v_push = push(qkv.at[0, :, pl.ds(2 * D, H)], wv.at[0], sems.one(), sems.one(), sib)

    @pl.when(core == 0)
    def _():
        v_push.start()

    rest_push = [
        push(wo.at[0, pl.ds(pl.multiple_of((1 - core) * H, H), H), :], wout.at[core], sems.one(), sems.one(), sib),
        push(fc.at[0, :, pl.ds(pl.multiple_of((1 - core) * FH, 128), FH)], wfc.at[core], sems.one(), sems.one(), sib),
        push(proj.at[0, pl.ds(pl.multiple_of((1 - core) * FH, FH), FH), :], wproj.at[core], sems.one(), sems.one(), sib),
    ]

    xh_sends = {}

    def route_block(l, turn, blk):
        p = pos(blk)
        for n in range(N - 1):
            part = xall.at[l, pl.ds(pl.multiple_of(p * T + core * T2, T2), T2), :]
            s, rsem = sems.one(), sems.one()
            cp = push(part, part, s, rsem, ahead[n])
            src = behind[n]
            slo = src + row * (C - 1 - 2 * src)
            sp = slo + blk * (C - 1 - 2 * slo)
            got = xall.at[l, pl.ds(pl.multiple_of(sp * T + core * T2, T2), T2), :]
            other = xall.at[l, pl.ds(pl.multiple_of(sp * T + (1 - core) * T2, T2), T2), :]
            come = push(got, got, s, rsem, ahead[n])
            fs, fr = sems.one(), sems.one()
            onward = push(got, got, fs, fr, sib)
            arrive = push(other, other, fs, fr, sib)
            xh_sends[(l, turn, n)] = (cp, come, onward, arrive, sp)

    def leave(l, turn):
        for n in range(N - 1):
            xh_sends[(l, turn, n)][0].start()

    def normed_block(l, turn, blk, values):
        xall[l, rows_at(pos(blk)), :] = layer_norm(values, sm[l, 0:1, :D], sm[l, 1:2, :D]).astype(BF16)
        route_block(l, turn, blk)
        leave(l, turn)

    def own_products(l, blk):
        p = pos(blk)
        xh = xall[l, rows_at(p), :]
        both = mm(xh, wqk[l])
        q[l, blk * T : (blk + 1) * T, :] = both[:, :H].astype(BF16)
        k[l, rows_at(p), :] = both[:, H:].astype(BF16)

    def value_products(l, p):
        src = l * core
        v[l, rows_at(p), :] = mm(xall[src, rows_at(p), :], wv[src]).astype(BF16)

    def key_products(l, p):
        k[l, rows_at(p), :] = mm(xall[l, rows_at(p), :], wqk[l, :, H:]).astype(BF16)

    def arrivals(l, turn):
        for n in range(N - 1):
            cp, come, onward, arrive, sp = xh_sends[(l, turn, n)]
            come.wait_recv()
            onward.start()

    def foreign_products(l, turn):
        for n in range(N - 1):
            cp, come, onward, arrive, sp = xh_sends[(l, turn, n)]
            arrive.wait_recv()
            key_products(l, sp)
            value_products(l, sp)

    act_push = [push(act.at[0, pl.ds(b * T, T), :], act_in_o.at[pl.ds(b * T, T), :], sems.one(), sems.one(), across) for b in range(2)]
    gm_push = [push(e.at[1, b], gm_in_o.at[b], sems.one(), sems.one(), across) for b in (row, 1 - row)]

    @pl.when(core == 0)
    def _():
        e_load.wait()

    @pl.when(core == 1)
    def _():
        own_come.wait_recv()

    sm_push.wait()
    blk = row
    r[0, pl.ds(pl.multiple_of(blk * T, T), T), :] = e[0, blk]
    normed_block(0, 0, blk, e[0, blk].astype(F32))

    @pl.when(core == 0)
    def _():
        loads[0].wait()
        loads[1].wait()
        v_shared.wait()

    @pl.when(core == 1)
    def _():
        for cp in qk_push:
            cp.wait_recv()
        v_push.wait_recv()

    def own_products_dynamic(l, blk):
        p = pos(blk)
        both = mm(xall[l, rows_at(p), :], wqk[l])
        q[l, pl.ds(pl.multiple_of(blk * T, T), T), :] = both[:, :H].astype(BF16)
        k[l, rows_at(p), :] = both[:, H:].astype(BF16)
        value_products(l, p)

    own_products_dynamic(0, blk)

    @pl.when(core == 1)
    def _():
        e_load.wait()

    @pl.when(core == 0)
    def _():
        own_come.wait_recv()

    when(jnp.logical_not(owner), gm_push[0].start)

    for n, cp in enumerate(seg_push):
        cp.wait()
    kseg = jnp.concatenate([seg[n] for n in range(C)], axis=1)
    kseg_o[...] = kseg
    for blk in range(2):
        rows = slice(blk * T, (blk + 1) * T)
        qpos = pos(blk) * T + lax.broadcasted_iota(jnp.int32, (T, L), 0)
        kpos = lax.broadcasted_iota(jnp.int32, (T, L), 1)
        allowed = (kpos <= qpos) & (kseg == column(seg[pos(blk)]))
        bias[rows, :] = jnp.where(allowed, 0.0, MASKED)

    blk = 1 - row

    route_block(0, 1, blk)
    for h in range(2):
        @pl.when(core == 0)
        def _():
            far_come[h].wait_recv()
            fwd_push[h].start()

        @pl.when(core == 1)
        def _():
            fwd_come[h].wait_recv()

        values = e[0, blk, h * T2 : (h + 1) * T2, :]
        r[0, pl.ds(pl.multiple_of(blk * T + h * T2, T2), T2), :] = values
        xall[0, pl.ds(pl.multiple_of(pos(blk) * T + h * T2, T2), T2), :] = layer_norm(
            values.astype(F32), sm[0, 0:1, :D], sm[0, 1:2, :D]).astype(BF16)

        @pl.when(core == h)
        def _():
            leave(0, 1)

    @pl.when(core == 1)
    def _():
        for cp in far_push:
            cp.start()

    own_products_dynamic(0, blk)

    def at_core(here, ours, theirs):
        @pl.when(here)
        def _():
            for cp in ours:
                cp.wait()

        @pl.when(jnp.logical_not(here))
        def _():
            for cp in theirs:
                cp.wait_recv()

    def branch(l, blk):
        rows = slice(blk * T, (blk + 1) * T)
        part = mm(o[l, rows, :], wout[l])
        hr[l, rows, :] = part
        br_s[l, rows, :] = part.astype(BF16)
        cp = push(br_s.at[l, rows, :], br_r.at[l, rows, :], sems.one(), sems.one(), sib)
        cp.start()
        return cp

    def hidden_units(l, blk, come):
        rows = slice(blk * T, (blk + 1) * T)
        come.wait_recv()
        hidden = r[l, rows, :].astype(F32) + hr[l, rows, :] + br_r[l, rows, :].astype(F32)
        hr[l, rows, :] = hidden
        normed2 = layer_norm(hidden, sm[l, 2:3, :D], sm[l, 3:4, :D]).astype(BF16)
        hh[l, rows, :] = normed2
        if l == 0 and blk == 0:
            at_core(core == 0, loads[3:5], rest_push[1:3])
        mine = pl.ds(pl.multiple_of(core * FH, 128), FH)
        u = mm(normed2, wfc[l]) + sm[l, 4:5, mine]
        a, slope = gelu_both(u)
        gp[l, rows, :] = slope.astype(BF16)
        act[l, rows, :] = a.astype(BF16)
        if l == 0:
            when(jnp.logical_not(owner), act_push[blk].start)

    def feed_out(l, blk):
        rows = slice(blk * T, (blk + 1) * T)
        part = mm(act[l, rows, :], wproj[l])
        y[rows, :] = part
        ml_s[l, rows, :] = part.astype(BF16)
        cp = push(ml_s.at[l, rows, :], ml_r.at[l, rows, :], sems.one(), sems.one(), sib)
        cp.start()
        return cp

    def block_out(l, blk, come):
        rows = slice(blk * T, (blk + 1) * T)
        come.wait_recv()
        out = hr[l, rows, :] + y[rows, :] + ml_r[l, rows, :].astype(F32)
        if l == 0:
            sent = out.astype(BF16)
            r[1, rows, :] = sent
            normed_block(1, blk, blk, sent.astype(F32))
        else:
            y[rows, :] = out
            yb[rows, :] = out.astype(BF16)

    def save_weights(l):
        wvt[l] = jnp.transpose(wv[l * core])
        save(wqk.at[l], watt_o.at[l, pl.ds(0, D)])
        save(wout.at[l], watt_o.at[l, pl.ds(D, H)])
        save(wvt.at[l], watt_o.at[l, pl.ds(D + H, H)])
        save(wfc.at[l], wfc_o.at[l])
        save(wproj.at[l], wproj_o.at[l])

    def unit(first, l, blk, key_blocks):
        attention_unit(first, l, blk, key_blocks, T, pairs, q, k, v, bias, acc, top_of, sum_of)

    def middle(l):
        unit(True, l, 0, [lo])
        if l == 0:
            arrivals(0, 0)
        unit(True, l, 1, [lo, hi])
        if l == 1:
            arrivals(1, 0)
        else:
            arrivals(0, 1)
            for cp in rest_push:
                cp.start()
        foreign_products(l, 0)
        if l == 1:
            arrivals(1, 1)
        else:
            foreign_products(0, 1)
        order = [(slo, lax.div(lo - slo + N - 1, N)) for slo in [src + row * (C - 1 - 2 * src) for src in behind]]
        for slo, above in order:
            unit(False, l, 1, [slo])
        if l == 1:
            foreign_products(1, 1)
        for slo, above in order:
            unit(False, l, 1 - above, [slo + (1 - above) * (C - 1 - 2 * slo)])
        attention_end(l, 0, T, pairs, o, lse, acc, top_of, sum_of)
        if l == 0:
            at_core(core == 0, loads[2:3], rest_push[0:1])

            @pl.when(core == 1)
            def _():
                for h in range(2):
                    far_come[h].wait_recv()
                    fwd_push[h].start()
        sends = [branch(l, 0)]
        attention_end(l, 1, T, pairs, o, lse, acc, top_of, sum_of)
        sends.append(branch(l, 1))
        if l == 0:
            @pl.when(core == 0)
            def _():
                for cp in fwd_come:
                    cp.wait_recv()

            when(jnp.logical_not(owner), gm_push[1].start)
        save(q.at[l], q_o.at[l])
        save(k.at[l], k_o.at[l])
        save(v.at[l], v_o.at[l])
        save(o.at[l], o_o.at[l])
        save(lse.at[l], lse_o.at[l])
        save(xall.at[l], xall_o.at[l])
        hidden_units(l, 0, sends[0])
        mlps = [feed_out(l, 0)]
        hidden_units(l, 1, sends[1])
        save(hr.at[l], hr_o.at[l])
        save(hh.at[l], hh_o.at[l])
        save(gp.at[l], gp_o.at[l])
        save(act.at[l], act_o.at[l])
        block_out(l, 0, mlps[0])
        mlps.append(feed_out(l, 1))
        if l == 0:
            at_core(core == 1, loads[0:2] + [v_fresh], qk_push)
            own_products(1, 0)
            value_products(1, pos(0))
        block_out(l, 1, mlps[1])
        if l == 0:
            own_products(1, 1)
            value_products(1, pos(1))
            at_core(core == 1, loads[2:5], rest_push)
            save_weights(0)
            save_weights(1)
        return sends + mlps


    pair_sends = middle(0)
    save(r, r_o)

    save(e.at[1], gy_o)
    save(sm, sm_o)
    pair_sends += middle(1)
    save(y, y_o)
    save(yb, yb_o)

    def crossed():
        for cp in act_push + gm_push:
            cp.wait_recv()

    def crossing():
        for cp in act_push + gm_push:
            cp.wait_send()

    when(owner, crossed)
    when(jnp.logical_not(owner), crossing)
    own_push.wait_send()
    for cp in far_push + fwd_push + qk_push + rest_push + pair_sends:
        cp.wait_send()

    @pl.when(core == 0)
    def _():
        v_push.wait_send()

    for cp, come, onward, arrive, sp in xh_sends.values():
        cp.wait_send()
        onward.wait_send()
    for cp in saves:
        cp.wait()


def forward_pass(C, m, ends, segs, g1, b1, g2, b2, qkv, wo, fc, fcb, proj, shared):
    T, D, F = ends.shape[2], ends.shape[3], fc.shape[2]
    N, L, H, FH = C // 2, C * T, D // 2, F // 2
    R, pairs = 2 * T, D // 256
    S = jax.ShapeDtypeStruct
    outs = [S((2, L, D), BF16), S((2, R, H), BF16), S((2, L, H), BF16), S((2, L, H), BF16), S((2, R, H), BF16),
            S((2, R, 128), F32), S((2, R, D), BF16), S((2, R, D), F32), S((2, R, D), BF16), S((2, R, FH), BF16),
            S((2, R, FH), BF16), S((R, D), F32), S((R, D), BF16), S((2, T, D), BF16), S((2, 8, F), F32), S((2, 2 * D, D), BF16),
            S((2, D, FH), BF16), S((2, FH, D), BF16), S((R, FH), BF16), S((2, T, D), BF16), S((1, L), jnp.int32)]
    V = pltpu.VMEM
    scratch = [V((2, 2, T, D), BF16), V((C, 1, T), jnp.int32), V((2, 1, T), jnp.int32), V((2, 8, F), F32), V((2, D, D), BF16), V((2, D, H), BF16),
               V((2, H, D), BF16), V((2, D, FH), BF16), V((2, FH, D), BF16), V((2, L, D), BF16), V((2, R, H), BF16),
               V((2, L, H), BF16), V((2, L, H), BF16), V((2, R, H), BF16), V((2, R, 128), F32), V((2, R, D), BF16),
               V((2, R, D), F32), V((2, R, D), BF16), V((2, R, FH), BF16), V((2, R, FH), BF16), V((R, D), F32),
               V((R, D), BF16), V((2, H, D), BF16), V((R, L), F32), V((pairs, R, 128), F32), V((pairs, R, 128), F32),
               V((pairs, R, 128), F32), V((2, R, D), BF16), V((2, R, D), BF16), V((2, R, D), BF16), V((2, R, D), BF16),
               pltpu.SemaphoreType.DMA((90 + 16 * (N - 1) + 2 * (C - 1),))]
    return pl.pallas_call(
        functools.partial(forward_kernel, C, m, T, D, F),
        in_specs=[HBM, VM, VM, VM, VM, VM, HBM, HBM, HBM, VM, HBM, HBM],
        out_specs=[HBM] * 20 + [VM],
        out_shape=outs,
        scratch_shapes=scratch,
        compiler_params=pltpu.CompilerParams(collective_id=0, has_side_effects=True, vmem_limit_bytes=VMEM_LIMIT),
        name="forward_pass",
    )(ends, segs, g1, b1, g2, b2, qkv, wo, fc, fcb, proj, shared)


WHOLE, SIDED, SIDE_STEP = 0, 1, 2
SMALL = 200
JOBS = ("P0", "P1", "P2", "F0", "F1", "F2", "O", "Q", "K", "V")
PROJ_AT = (3, 3)
POLLS = (
    (), (), (113,), (), (), (), (), (), (), (115,), (), (), (), (13,), (113,), (), (116,), (), (), (), (15,),
    (13, 117), (115, 112, 113), (), (13, 114, 113, 16, 17, 117), (110,), (), (), (13, 113), (15, 115),
    (12, 112, 17, 117), (111,), (13,), (15, 115), (), (10, 110, 12, 112), (17, 116, 117), (), (15, 115, 14),
    (10, 110, 114, 11, 111, 12, 112), (17, 118, 105, 15, 10, 110, 16, 116), (11, 111, 12, 10), (16, 116, 14, 114),
    (11, 119), (), (16, 103, 14), (), (117,), (106,), (18, 111, 116, 5, 19, 114), (17, 118, 105), (11, 16),
    (14, 119, 114), (),
)
TAIL = (
    104, 3, 6, 14, 102, 18, 5, 118, 19, 119, 105, 200, 100, 19, 119, 103, 2, 102, 18, 118,
    19, 119, 5, 105, 101, 2, 102, 4, 108, 18, 118, 0, 100, 19, 200, 5, 107, 105, 2, 18,
    102, 3, 103, 0, 100, 200, 5, 109, 1, 101, 106, 2, 3, 103, 0, 100, 200, 7, 107, 104,
    8, 1, 101, 3, 103, 0, 108, 6, 106, 7, 107, 9, 1, 101, 3, 109, 6, 106, 7, 107,
    4, 104, 1, 6, 106, 8, 108, 7, 107, 4, 104, 9, 109, 6, 7, 8, 108, 4, 104, 9,
    109, 8, 108, 4, 9, 109, 8, 9,
)


class Job:
    def __init__(self, env, buf, lead, cols, order, sided, land, credits, active, earlier, prior):
        self.env, self.buf, self.lead, self.cols = env, buf, lead, cols
        self.sided, self.land, self.credits, self.active, self.prior = sided, land, credits, active, prior
        self.copies = {}
        self.earlier = earlier
        self.bits = list(range(env.m - 2 if sided else env.m - 1, -1, -1))
        self.fixed, self.z_done, self.steps, self.at, self.flying = {}, False, [], 0, False
        self.used, self.own_sems = 0, []
        if sided == SIDE_STEP:
            self.steps.append(("side", None, None))
        for item in order:
            if item == "z":
                for s in range(1, env.C):
                    self.steps.append(("z", s, dict(self.fixed)))
                self.z_done = True
            elif item == "d":
                self.steps.append(("d", None, dict(self.fixed)))
                self.z_done = True
            else:
                self.steps.append(("bit", item, (dict(self.fixed), self.z_done)))
                self.fixed[item] = env.bit(item)
        self.plans = [self.plan(i) for i in range(len(self.steps))]

    def view(self, fixed, zat):
        at = tuple(self.lead) + tuple(fixed.get(b, slice(None)) for b in self.bits)
        return at + (slice(None) if zat is None else zat, slice(None), self.cols)

    def plan(self, i):
        env = self.env
        kind, what, state = self.steps[i]
        moves = []
        if kind == "side":
            other = env.dp_xor(env.m - 1)
            moves.append((env.bit(env.m - 1) != env.core, self.view({}, None), other, env.bit(env.m - 1) == env.core,
                          self.view({}, None), other))
            return [self.bind(move, self.land[i]) for move in moves]
        active = self.active if not self.sided else (env.bit(env.m - 1) == env.core)
        if kind == "bit":
            fixed, z_done = state
            zat = env.z if z_done else None
            other = env.dp_xor(what)
            mine = env.bit(what)
            moves.append((active, self.view({**fixed, what: 1 - mine}, zat), other, active,
                          self.view({**fixed, what: mine}, zat), other))
            return [self.bind(move, self.land[i]) for move in moves]
        s, C, z = what, env.C, env.z
        if kind == "d":
            for n in range(1, C):
                to, source = lax.rem(z + n, C), lax.rem(z + C - n, C)
                moves.append((active, self.view(state, to), env.line(to), active, self.view(state, z), env.line(source)))
            return [self.bind(move, self.land[i].at[n]) for n, move in enumerate(moves)]
        zm = C - 1 - z
        for side, (p, sign) in enumerate(((z, 1), (zm, -1))):
            out_at = z + sign * (C - s)
            in_at = z + sign * (C - s - 1)
            moves.append((both(active, p < s), self.view(state, out_at), env.line(z + sign),
                          both(active, both(p >= 1, p <= s)), self.view(state, in_at), env.line(z - sign)))
        return [self.bind(move, self.land[i].at[side]) for side, move in enumerate(moves)]

    def bind(self, move, slot):
        send_if, src, to, recv_if, dst, source = move
        env = self.env
        if self.prior is None:
            sem_s, sem_r = env.sems.one(), env.sems.one()
            self.own_sems.append((sem_s, sem_r))
        else:
            sem_s, sem_r = self.prior.own_sems[self.used]
        credit = self.credits.at[self.used]
        self.used += 1
        return send_if, src, to, recv_if, dst, source, slot, sem_s, sem_r, credit

    def send(self, i):
        for n, (send_if, src, to, recv_if, dst, source, slot, sem_s, sem_r, credit) in enumerate(self.plans[i]):
            cp = self.copies[(i, n)] = push(self.buf.at[src], slot, sem_s, sem_r, to)

            def go():
                if self.prior is not None:
                    def empty():
                        pl.semaphore_wait(credit, 1)
                        self.prior.copies[(i, n)].wait_send()

                    when(self.earlier, empty)
                cp.start()

            when(send_if, go)
            if self.prior is not None:
                self.env.sent.append((send_if, cp))

    def take(self, i):
        direct = self.steps[i][0] == "d"
        groups = [self.plans[i]] if direct else [[plan] for plan in self.plans[i]]
        for group in groups:
            send_if, src, to, recv_if, dst = group[0][:5]

            def got():
                total = self.buf[dst].astype(F32) if direct else self.buf[dst]
                for _, _, to, _, _, source, slot, sem_s, sem_r, credit in group:
                    push(slot, slot, sem_s, sem_r, to).wait_recv()
                    total = total + slot[...].astype(total.dtype)
                self.buf[dst] = total.astype(BF16)
                if self.prior is None:
                    for _, _, _, _, _, source, _, _, _, credit in group:
                        pl.semaphore_signal(credit, inc=1, device_id=source, device_id_type=MESH)

            when(recv_if, got)

    def send_next(self):
        if not self.flying and self.at < len(self.steps):
            self.send(self.at)
            self.flying = True

    def take_next(self):
        if self.flying:
            self.take(self.at)
            self.at, self.flying = self.at + 1, False

    def finish(self):
        while self.at < len(self.steps):
            self.send_next()
            self.take_next()

    def own(self):
        return self.view(self.fixed, self.env.z)


def both(a, b):
    if a is True:
        return b
    if b is True:
        return a
    return jnp.logical_and(a, b)


def when(condition, fn):
    if condition is True:
        fn()
    else:
        pl.when(condition)(fn)


class Env:
    def __init__(self, C, m, core, dp, z, sems):
        self.C, self.m, self.core, self.dp, self.z, self.sems, self.sent = C, m, core, dp, z, sems, []

    def bit(self, b):
        return lax.rem(lax.div(self.dp, 1 << b), 2)

    def dp_xor(self, b):
        return (self.core, self.dp + (1 << b) * (1 - 2 * self.bit(b)), self.z)

    def line(self, z):
        return (self.core, self.dp, z)


def job_table(m):
    xs, ys = list(range(m)), list(range(m - 1, -1, -1))
    rest = list(range(m - 1))
    xz, yz = xs + ["z"], ys + ["z"]
    return {
        "P0": ("gproj", (0, 3), rest + ["z"], SIDED), "P1": ("gproj", (1, 3), rest + ["z"], SIDED),
        "P2": ("gproj", (2, 3), rest + ["z"], SIDED),
        "F0": ("gfc", (0, 3), xz, WHOLE), "F1": ("gfc", (1, 3), yz, WHOLE), "F2": ("gfc", (2, 3), xz, WHOLE),
        "O": ("gout", (0, 1), rest + ["z"], SIDE_STEP),
        "Q": ("gq", (0, 1), xs[:1] + ["z"] + xs[1:], WHOLE), "K": ("gk", (0, 1), yz, WHOLE), "V": ("gv", (0, 1), yz, WHOLE),
    }


def grad_shapes(C, m, D, F):
    H, FH, J = D // 2, F // 2, C << m
    full, side = (2,) * m + (C,), (2,) * (m - 1) + (C,)
    return {"gproj": side + (F // J, D), "gfc": full + (D // J, FH), "gout": side + (D // J, D),
            "gq": full + (D // J, H), "gk": full + (D // J, H), "gv": full + (D // J, H)}


def landing_shapes(C, m, D, F):
    shapes = grad_shapes(C, m, D, F)
    result = {}
    for name, (buf, (at, parts), order, sided) in job_table(m).items():
        shape = list(shapes[buf])
        shape[-1] //= parts
        n = m - 1 if sided else m
        lead = {b: 2 for b in range(n)}
        tail = [shape[-2], shape[-1]]
        zdim = [C]
        steps = []
        if sided == SIDE_STEP:
            steps.append(tuple([2] * n + zdim + tail))
        for item in order:
            if item == "z":
                zdim = []
                for s in range(1, C):
                    steps.append(tuple([2] + [2] * len(lead) + tail))
            elif item == "d":
                zdim = []
                steps.append(tuple([C - 1] + [2] * len(lead) + tail))
            else:
                lead.pop(item)
                steps.append(tuple([2] * len(lead) + zdim + tail))
        result[name] = steps
    return result


def norm_grad(values, gain, grad):
    unit, rstd = unit_norm(values)
    scaled = grad * gain
    m1 = jnp.mean(scaled, axis=-1, keepdims=True)
    m2 = jnp.mean(scaled * unit, axis=-1, keepdims=True)
    back = rstd * (scaled - m1 - unit * m2)
    return back, jnp.sum(grad * unit, axis=0, keepdims=True), jnp.sum(grad, axis=0, keepdims=True)


def attention_back_pair(i, T, L, q, k, v, o, lse, goa, bias, dq, dk, dv, dv_at):
    cols = slice(i * 128, (i + 1) * 128)
    lane = lax.broadcasted_iota(jnp.int32, (T, 128), 1)
    scale = jnp.asarray(HEAD**-0.5, BF16)
    totals = None
    for blk in (1, 0):
        rows = slice(blk * T, (blk + 1) * T)
        keys = L if blk else L // 2
        q2, go2 = q[rows, cols] * scale, goa[rows, cols]
        prod = go2.astype(F32) * o[rows, cols].astype(F32)
        k2, v2 = k[:keys, cols], v[:keys, cols]
        dqs, dks, dvs = [], None, None
        for h in range(2):
            sel = (lane >= 64) == (h == 1)
            qh = jnp.where(sel, q2, jnp.zeros_like(q2))
            goh = jnp.where(sel, go2, jnp.zeros_like(go2))
            delta = jnp.sum(jnp.where(sel, prod, 0.0), axis=-1, keepdims=True)
            s = mm_nt(qh, k2) + bias[rows, :keys].astype(F32)
            prob = jnp.exp(s - lse[rows, 2 * i + h : 2 * i + h + 1])
            gp = mm_nt(goh, v2)
            gs = (prob * (gp - delta)).astype(BF16)
            dqs.append(mm(gs, k2))
            one_k = mm_tn(gs, qh)
            one_v = mm_tn(prob.astype(BF16), goh)
            dks = one_k if dks is None else dks + one_k
            dvs = one_v if dvs is None else dvs + one_v
        dq[rows, cols] = (jnp.where(lane < 64, dqs[0], dqs[1]) * HEAD**-0.5).astype(BF16)
        if blk:
            totals = (dks, dvs)
        else:
            dk[:keys, cols] = (totals[0][:keys] + dks).astype(BF16)
            dk[keys:, cols] = totals[0][keys:].astype(BF16)
            dv[dv_at, :keys, cols] = (totals[1][:keys] + dvs).astype(BF16)
            dv[dv_at, keys:, cols] = totals[1][keys:].astype(BF16)


LOADED = ("gp", "act", "hh", "hr", "o", "q", "k", "v", "lse", "xall", "r")


def backward_kernel(C, m, T, D, F, fused, names_in, *refs):
    n_in = len(names_in)
    hbm = dict(zip(names_in, refs[:n_in]))
    outs, (vm, dma, credits) = refs[n_in:-3], refs[-3:]
    ends_o, small_o = outs[:2]
    core, dp, z = lax.axis_index(SECTION), lax.axis_index(DP), lax.axis_index(CTX)
    N, L, H, FH = C // 2, C * T, D // 2, F // 2
    row = lax.div(z, N)
    lo = z + row * (C - 1 - 2 * z)
    hi = C - 1 - lo
    base = row * N
    pairs = H // 128
    sems = Sems(dma)
    env = Env(C, m, core, dp, z, sems)
    sib = (1 - core, dp, z)
    mirror = (core, dp, C - 1 - z)
    pos = lambda blk: lo + blk * (hi - lo)
    block = lambda at: pl.ds(pl.multiple_of(at * T, T), T)
    other_nodes = [base + lax.rem(z - base + n, N) for n in range(1, N)]
    sent = env.sent
    loads = {}

    def load(name, l, src=None, dst=None):
        cp = pltpu.make_async_copy(hbm[name].at[l] if src is None else src, vm[name] if dst is None else dst, sems.one())
        cp.start()
        loads[(name, l)] = cp

    def need(*names):
        for name in names:
            loads[name].wait()

    def pushed(src, dst, to, condition=True, until=sent):
        cp = push(src, dst, sems.one(), sems.one(), to)
        when(condition, cp.start)
        until.append((condition, cp))
        return cp

    load("gy", 1, hbm["gy"].at[0], vm["gm"].at[0])
    load("gy", 0, hbm["gy"].at[1], vm["gm"].at[1])
    load("wproj", 1, dst=vm["wa"])
    load("gp", 1)
    load("wfc", 1)
    load("act", 1)
    load("hh", 1)
    load("hr", 1)
    load("sm", 0, hbm["sm"], vm["sm"])
    for name in ("o", "q", "k", "v", "lse", "xall", "r"):
        load(name, 1)
    y_keep = pltpu.make_async_copy(hbm["y"].at[block(row)], ends_o.at[0, row], sems.one())
    when(core == 1, y_keep.start)

    kseg = hbm["kseg"]
    for blk in range(2):
        rows = slice(blk * T, (blk + 1) * T)
        qpos = pos(blk) * T + lax.broadcasted_iota(jnp.int32, (T, L), 0)
        kpos = lax.broadcasted_iota(jnp.int32, (T, L), 1)
        mine = kseg[0:1, 0:T]
        for n in range(1, C):
            mine = jnp.where(pos(blk) == n, kseg[0:1, n * T : (n + 1) * T], mine)
        allowed = (kpos <= qpos) & (kseg[...] == column(mine))
        vm["bias"][rows, :] = jnp.where(allowed, 0.0, MASKED).astype(BF16)

    greet([sib] + [env.line(lax.rem(z + n, C)) for n in range(1, C)] + [env.dp_xor(b) for b in range(m)])

    y_push = pushed(hbm["yb"].at[block(1 - row)], vm["far"], mirror, core == 1)
    top = env.bit(m - 1) == core
    aside = jnp.logical_not(top)
    across = env.dp_xor(m - 1)
    act_push = pushed(hbm["act"].at[1], vm["act_in"], across, aside)
    gm_in_load = pltpu.make_async_copy(hbm["gm_in"], vm["gm_in"].at[1], sems.one())
    act_in_load = pltpu.make_async_copy(hbm["act_in"], vm["act_in"], sems.one())
    when(top, gm_in_load.start)
    gm_push = push(vm["gm"], vm["gm_in"].at[0], sems.one(), sems.one(), across)

    table = job_table(m)
    jobs = {}

    def start(name, l):
        if not fused:
            return
        buf, (at, parts), order, sided = table[name]
        width = vm[buf].shape[-1] // parts
        earlier = True if name != "V" else core == 1
        active = True if l == 0 else earlier
        jobs[(name, l)] = Job(env, vm[buf], (l,), slice(at * width, (at + 1) * width), order, sided, vm["land"][name],
                              credits[name], active, earlier, jobs.get((name, 1)))

    def move(code):
        job = jobs.get((JOBS[code % 10], code // 10 % 10)) if fused else None
        if job is not None:
            job.send_next() if code >= 100 else job.take_next()

    gm, gp, go, ghh, wa, wfc = vm["gm"], vm["gp"], vm["go"], vm["ghh"], vm["wa"], vm["wfc"]
    sm, sg = vm["sm"], vm["sg"]

    def put(buf, l, cols, value):
        shape = vm[buf].shape[1:-1] + (value.shape[-1],)
        vm[buf][(l,) + (slice(None),) * (len(shape) - 1) + (cols,)] = value.astype(BF16).reshape(shape)

    polls = iter(POLLS)

    def poll():
        for code in next(polls):
            move(code)

    def layer_back(l):
        again = []

        def proj_phase():
            def proj_grad():
                if l == 1:
                    act_push.wait_recv()
                    gm_in_load.wait()
                else:
                    act_in_load.wait()
                    gm_push.wait_recv()
                third = D // 3
                for n in range(3):
                    cols = slice(n * third, (n + 1) * third)
                    total = mm_tn(vm["act_in"][...], vm["gm_in"][l, :, :, cols].reshape(2 * T, third))
                    for blk in range(2):
                        total += mm_tn(vm["act"][blk * T : (blk + 1) * T, :], gm[blk, :, cols])
                    put("gproj", l, cols, total)

            need(("act", l))
            when(top, proj_grad)
            for n in range(3):
                start("P%d" % n, l)
            if l == 1:
                load("act", 0)
                when(top, act_in_load.start)

        need(("wproj", l), ("gp", l))
        bias_sum = None
        for blk in range(2):
            rows = slice(blk * T, (blk + 1) * T)
            if l == 1:
                need(("gy", 1 - blk))
                go[rows, :] = gm[blk].astype(F32)
            gu = (gp[rows, :].astype(F32) * mm_nt(gm[blk], wa[...])).astype(BF16)
            gp[rows, :] = gu
            part = jnp.sum(gu.astype(F32), axis=0, keepdims=True)
            bias_sum = part if bias_sum is None else bias_sum + part
            if blk == 0:
                poll()
        sg[l, 4:5, :] = bias_sum
        load("watt", l, dst=wa)
        poll()
        need(("hh", l))
        third = FH // 3
        for i in (0, 1, 2):
            cols = slice(i * third, (i + 1) * third)
            put("gfc", l, cols, mm_tn(vm["hh"][...], gp[:, cols]))
            start("F%d" % i, l)
            poll()
        need(("wfc", l))
        shares = []
        for blk in range(2):
            rows = slice(blk * T, (blk + 1) * T)
            part = mm_nt(gp[rows, :], wfc[...])
            ghh[rows, :] = part
            vm["a_s"][rows, :] = part.astype(BF16)
            shares.append(pushed(vm["a_s"].at[rows, :], vm["a_r"].at[rows, :], sib, until=[]))
            poll()
        if l == 1:
            load("wfc", 0)
        poll()
        if l == 1:
            load("hh", 0)
            load("gp", 0)
        need(("hr", l), ("watt", l))
        if l == 1:
            need(("sm", 0))
        sums = None
        for blk in range(2):
            rows = slice(blk * T, (blk + 1) * T)
            shares[blk].wait_recv()
            grad = ghh[rows, :] + vm["a_r"][rows, :].astype(F32)
            back, gain_sum, bias_sum = norm_grad(vm["hr"][rows, :], sm[l, 2:3, :D], grad)
            total = go[rows, :] + back
            go[rows, :] = total
            low = total.astype(BF16)
            vm["gb"][rows, :] = low
            vm["goa"][rows, :] = mm_nt(low, wa[D : D + H, :]).astype(BF16)
            poll()
            sums = (gain_sum, bias_sum) if sums is None else (sums[0] + gain_sum, sums[1] + bias_sum)
        sg[l, 2:3, :D] = sums[0]
        sg[l, 3:4, :D] = sums[1]
        poll()
        if l == 1:
            load("hr", 0)
        need(("o", l))
        put("gout", l, slice(0, D), mm_tn(vm["o"][...], vm["gb"][...]))
        start("O", l)
        poll()
        need(("q", l), ("k", l), ("v", l), ("lse", l))
        for i in range(pairs):
            attention_back_pair(i, T, L, vm["q"], vm["k"], vm["v"], vm["o"], vm["lse"], vm["goa"], vm["bias"], vm["dq"],
                                vm["dk"], vm["dv"], l)
            if i == PROJ_AT[l]:
                proj_phase()
            poll()
        if l == 1:
            for name in ("o", "q", "k", "v", "lse"):
                load(name, 0)
        else:
            def merge():
                vm["dv"][0] = (vm["dv"][0].astype(F32) + vm["dv"][1].astype(F32)).astype(BF16)

            when(core == 0, merge)
        dk, dv, dq = vm["dk"], vm["dv"], vm["dq"]

        def key_part(at):
            part_v = dv[l, block(at), :]
            if l == 1:
                part_v = jnp.where(core == 1, part_v, jnp.zeros_like(part_v))
            return mm_nt(dk[block(at), :], wa[:D, H:]) + mm(part_v, wa[D + H :, :])

        crossing, gives = [], []
        for n, node in enumerate(other_nodes):
            dlo = node + row * (C - 1 - 2 * node)
            dhi = C - 1 - dlo
            vm["fs_s"][n] = key_part(dlo + (1 - core) * (dhi - dlo)).astype(BF16)
            gives.append(pushed(vm["fs_s"].at[n], vm["fs_r"].at[n], sib, until=again))
        poll()
        for n, node in enumerate(other_nodes):
            dlo = node + row * (C - 1 - 2 * node)
            keep = key_part(dlo + core * (C - 1 - 2 * dlo))
            gives[n].wait_recv()
            vm["fx_s"][n] = (keep + vm["fs_r"][n].astype(F32)).astype(BF16)
            crossing.append(pushed(vm["fx_s"].at[n], vm["fx_r"].at[l, n], (core, dp, node), until=again))
        poll()
        for blk in range(2):
            rows = slice(blk * T, (blk + 1) * T)
            ghh[rows, :] = key_part(pos(blk)) + mm_nt(dq[rows, :], wa[:D, :H])
            poll()
        for cp in shares:
            cp.wait_send()
        early = pl.ds(pl.multiple_of((1 - core) * T, T), T)
        late = pl.ds(pl.multiple_of(core * T, T), T)
        vm["a_s"][early, :] = ghh[early, :].astype(BF16)
        shares = [pushed(vm["a_s"].at[early, :], vm["b_r"].at[early, :], sib, until=again)]
        if l == 1:
            load("wproj", 0, dst=wa)
        poll()
        need(("xall", l))
        xall = vm["xall"]
        put("gk", l, slice(0, H), mm_tn(xall[...], dk[...]))
        start("K", l)
        poll()
        put("gq", l, slice(0, H), mm_tn(xall[block(lo), :], dq[:T, :]) + mm_tn(xall[block(hi), :], dq[T:, :]))
        start("Q", l)
        poll()
        put("gv", l, slice(0, H), mm_tn(xall[...], dv[l]))
        start("V", l)
        if PROJ_AT[l] == 3:
            proj_phase()
        poll()
        if l == 1:
            load("xall", 0)
        need(("r", l))
        for n in range(N - 1):
            crossing[n].wait_recv()
            ghh[late, :] += vm["fx_r"][l, n].astype(F32)
        vm["a_s"][late, :] = ghh[late, :].astype(BF16)
        shares.append(pushed(vm["a_s"].at[late, :], vm["b_r"].at[late, :], sib, until=again))
        poll()
        for cp in shares:
            cp.wait_recv()
        sums = None
        for blk in range(2):
            rows = slice(blk * T, (blk + 1) * T)
            grad = ghh[rows, :] + vm["b_r"][rows, :].astype(F32)
            back, gain_sum, bias_sum = norm_grad(vm["r"][rows, :].astype(F32), sm[l, 0:1, :D], grad)
            total = go[rows, :] + back
            go[rows, :] = total
            if l == 1:
                gm[blk] = total.astype(BF16)
            poll()
            sums = (gain_sum, bias_sum) if sums is None else (sums[0] + gain_sum, sums[1] + bias_sum)
        sg[l, 0:1, :D] = sums[0]
        sg[l, 1:2, :D] = sums[1]
        poll()
        if l == 1:
            load("r", 0)
            when(aside, gm_push.start)
            sent.append((aside, gm_push))
        for condition, cp in again:
            when(condition, cp.wait_send)

    layer_back(1)
    layer_back(0)

    keep = pl.ds(pl.multiple_of(row * T, T), T)
    away = pl.ds(pl.multiple_of((1 - row) * T, T), T)
    vm["gb"][:T, :] = go[away, :].astype(BF16)
    x_push = pushed(vm["gb"].at[pl.ds(0, T), :], vm["far"], mirror, core == 0)
    x_keep = pltpu.make_async_copy(go.at[keep, :], ends_o.at[0, row], sems.one())
    when(core == 0, x_keep.start)

    sv, sv_r = vm["sv"], vm["sv_r"]
    sv[0] = jnp.zeros_like(sv[0])
    sv[0, 0:4, :] = sg[core, 0:4, :]
    sv[0, 4:5, :] = sg[0, 4:5, :]
    sv[0, 5:6, :] = sg[1, 4:5, :]
    around = [env.dp_xor(b) for b in range(m)]
    b = 1
    while b < C:
        around.append(env.line(z + b * (1 - 2 * lax.rem(lax.div(z, b), 2))))
        b *= 2
    small_at = [0]
    small_cp = [pushed(sv.at[0], sv_r.at[0], around[0])]

    last = len(around)

    def bias_halves():
        vm["fb_s"][...] = jnp.where(core == 0, sv[last, 5:6, :], sv[last, 4:5, :])
        cp = pushed(vm["fb_s"], vm["fin"]["fb"], sib)
        if not fused:
            cp.wait_recv()
            return
        ours = jnp.where(core == 0, sv[last, 4:5, :], sv[last, 5:6, :])
        j, J = dp * C + z, C << m
        norms = own_part(sv[last, :, :D], j, J)
        for i in range(4):
            vm["parts"][1 + i][...] = norms[i : i + 1, :]
        cp.wait_recv()
        theirs = vm["fin"]["fb"][...]
        bias = jnp.concatenate([jnp.where(core == 0, ours, theirs), jnp.where(core == 0, theirs, ours)], axis=1)
        vm["parts"][0][...] = own_part(jnp.broadcast_to(bias, (8, F)), j, J)[0:1, :]

    def small_step():
        i = small_at[0]
        if i == len(around):
            return
        small_cp[0].wait_recv()
        sv[i + 1] = sv[i] + sv_r[i]
        small_at[0] += 1
        if i + 1 < len(around):
            small_cp[0] = pushed(sv.at[i + 1], sv_r.at[i + 1], around[i + 1])
        else:
            bias_halves()

    def finish_ends():
        when(core == 0, x_push.wait_recv)
        when(core == 1, y_push.wait_recv)
        vm["ghh"][:T, :] = vm["far"][...].astype(F32)
        far_keep = pltpu.make_async_copy(vm["ghh"].at[pl.ds(0, T), :], ends_o.at[0, 1 - row], sems.one())
        far_keep.start()
        far_keep.wait()
        when(core == 0, x_keep.wait)
        when(core == 1, y_keep.wait)

    if fused:
        for code in TAIL:
            if code == SMALL:
                small_step()
            else:
                move(code)
        for job in jobs.values():
            job.finish()
    while small_at[0] < len(around):
        small_step()

    if fused:
        hand_over(core, sib, env, vm, jobs, m, D, H, FH, pushed, sv, last)
        results = list(zip(vm["stage"], outs[7:]))
    else:
        results = [(vm[name], out) for name, out in zip(("gproj", "gfc", "gout", "gq", "gk", "gv"), outs[7:])]
    results += [(sv.at[last], small_o)] + list(zip(vm["parts"], outs[2:7]))
    results = [pltpu.make_async_copy(src, dst, sems.one()) for src, dst in results]
    for cp in results:
        cp.start()
    finish_ends()
    for condition, cp in sent:
        when(condition, cp.wait_send)
    for cp in results:
        cp.wait()


def hand_over(core, sib, env, vm, jobs, m, D, H, FH, pushed, sv, last):
    qkv_o, out_o, fc_o, proj_o, shared_o = vm["stage"]
    fin = vm["fin"]
    top = env.bit(m - 1) == core
    own = lambda name, l: (l,) + jobs[(name, 0)].own()[1:]
    arrive = [
        pushed(vm["gfc"].at[own("F0", 1 - core)[:-1]], fin["fc"], sib),
        pushed(vm["gq"].at[own("Q", 1 - core)], fin["q"], sib),
        pushed(vm["gk"].at[own("K", 1 - core)], fin["k"], sib),
        pushed(vm["gv"].at[own("V", 0)], fin["v"], sib),
    ]
    out_push = pushed(vm["gout"].at[own("O", 1 - core)], fin["out"], sib, top)
    proj_push = pushed(vm["gproj"].at[own("P0", 1 - core)[:-1]], fin["proj"], sib, top)

    here = pl.ds(pl.multiple_of(core * H, 128), H)
    there = pl.ds(pl.multiple_of((1 - core) * H, 128), H)
    here_k = pl.ds(pl.multiple_of(D + core * H, 128), H)
    there_k = pl.ds(pl.multiple_of(D + (1 - core) * H, 128), H)
    qkv_o[0, :, here] = vm["gq"][own("Q", core)].astype(F32)
    qkv_o[0, :, here_k] = vm["gk"][own("K", core)].astype(F32)
    fc_o[0, :, pl.ds(pl.multiple_of(core * FH, 128), FH)] = vm["gfc"][own("F0", core)[:-1]].astype(F32)

    def top_out():
        out_o[0] = vm["gout"][own("O", core)].astype(F32)
        proj_o[0] = vm["gproj"][own("P0", core)[:-1]].astype(F32)

    when(top, top_out)
    for cp in arrive:
        cp.wait_recv()

    def other_out():
        out_push.wait_recv()
        proj_push.wait_recv()
        out_o[0] = fin["out"][...].astype(F32)
        proj_o[0] = fin["proj"][...].astype(F32)

    when(jnp.logical_not(top), other_out)
    qkv_o[0, :, there] = fin["q"][...].astype(F32)
    qkv_o[0, :, there_k] = fin["k"][...].astype(F32)
    fc_o[0, :, pl.ds(pl.multiple_of((1 - core) * FH, 128), FH)] = fin["fc"][...].astype(F32)
    fresh = pl.ds(2 * D, H)

    def fresh_first():
        qkv_o[0, :, fresh] = fin["v"][...].astype(F32)
        shared_o[...] = vm["gv"][own("V", 0)].astype(F32)

    def fresh_second():
        qkv_o[0, :, fresh] = vm["gv"][own("V", 1)].astype(F32)
        shared_o[...] = fin["v"][...].astype(F32)

    when(core == 0, fresh_first)
    when(core == 1, fresh_second)


def backward_pass(C, m, T, D, F, inputs):
    N, L, H, FH, R, J = C // 2, C * T, D // 2, F // 2, 2 * T, C << m
    fused = (D // J) % 16 == 0 and (F // J) % 16 == 0 and m > 0
    pairs = H // 128
    S, V = jax.ShapeDtypeStruct, pltpu.VMEM
    names = tuple(inputs)
    outs, stage = [S((1, 2, T, D), F32), S((8, FH), F32), S((1, F // J), F32)] + [S((1, D // J), F32)] * 4, []
    flat = {"gproj": (FH, D), "gfc": (D, FH), "gout": (H, D), "gq": (D, H), "gk": (D, H), "gv": (D, H)}
    if fused:
        outs += [S((1, D // J, 5 * H), F32), S((1, D // J, D), F32), S((1, D // J, F), F32), S((1, F // J, D), F32),
                 S((D // J, H), F32)]
        stage = [V(out.shape, F32) for out in outs[7:]]
        grads = grad_shapes(C, m, D, F)
        land = {name: [V(shape, BF16) for shape in steps] for name, steps in landing_shapes(C, m, D, F).items()}
    else:
        outs += [S((2,) + shape, BF16) for shape in flat.values()]
        grads, land = flat, {}
    stages = m + C.bit_length() - 1
    vm = dict(
        gm=V((2, T, D), BF16), gb=V((R, D), BF16), gm_in=V((2, 2, T, D), BF16), act_in=V((R, FH), BF16), gp=V((R, FH), BF16), act=V((R, FH), BF16), hh=V((R, D), BF16), hr=V((R, D), F32),
        o=V((R, H), BF16), q=V((R, H), BF16), k=V((L, H), BF16), v=V((L, H), BF16), lse=V((R, 128), F32),
        xall=V((L, D), BF16), r=V((R, D), BF16), sm=V((2, 8, F), F32), sg=V((2, 8, FH), F32), bias=V((R, L), BF16),
        wa=V((2 * D, D), BF16), wfc=V((D, FH), BF16), go=V((R, D), F32), ghh=V((R, D), F32), a_s=V((R, D), BF16),
        a_r=V((R, D), BF16), b_r=V((R, D), BF16), goa=V((R, H), BF16), dq=V((R, H), BF16),
        dk=V((L, H), BF16), dv=V((2, L, H), BF16), fs_s=V((N - 1, T, D), BF16), fs_r=V((N - 1, T, D), BF16),
        fx_s=V((N - 1, T, D), BF16), fx_r=V((2, N - 1, T, D), BF16), far=V((T, D), BF16),
        sv=V((stages + 1, 8, FH), F32), sv_r=V((stages, 8, FH), F32), fb_s=V((1, FH), F32),
        fin=dict(fc=V((D // J, FH), BF16), q=V((D // J, H), BF16), k=V((D // J, H), BF16), v=V((D // J, H), BF16),
                 out=V((D // J, D), BF16), proj=V((F // J, D), BF16), fb=V((1, FH), F32)),
        land=land, stage=stage, parts=[V(out.shape, F32) for out in outs[2:7]], **{name: V((2,) + shape, BF16) for name, shape in grads.items()})
    moves = {name: len(order) - 1 + ("z" in order) * (C - 1) + C - 1 + (sided == SIDE_STEP) for name, (_, _, order, sided) in job_table(m).items()}
    credits = {name: pltpu.SemaphoreType.REGULAR((n,)) for name, n in moves.items()} if fused else {}
    semaphores = 60 + 2 * stages + 8 * (N - 1) + (25 + 2 * sum(moves.values()) if fused else 14)
    in_specs = [VM if name == "kseg" else HBM for name in names]
    return pl.pallas_call(
        functools.partial(backward_kernel, C, m, T, D, F, fused, names),
        in_specs=in_specs,
        out_specs=[HBM] * len(outs),
        out_shape=outs,
        scratch_shapes=[vm, pltpu.SemaphoreType.DMA((semaphores,)), credits],
        compiler_params=pltpu.CompilerParams(collective_id=1, has_side_effects=True, vmem_limit_bytes=VMEM_LIMIT),
        name="backward_pass",
    )(*inputs.values())


def xor_route(size, bit):
    return [(i, i ^ (1 << bit)) for i in range(size)]


def halve(grad, axis_name, bit, at):
    mine = (lax.axis_index(axis_name) >> bit) & 1
    keep = lax.dynamic_index_in_dim(grad, mine, at, keepdims=False)
    send = lax.dynamic_index_in_dim(grad, 1 - mine, at, keepdims=False)
    got = lax.ppermute(send, axis_name, xor_route(lax.axis_size(axis_name), bit))
    return (keep.astype(F32) + got.astype(F32)).astype(grad.dtype)


def bits_of(axis_name):
    return lax.axis_size(axis_name).bit_length() - 1


def scatter_sum(grad, order, skip_first=False):
    dims = [(DP, b) for b in reversed(range(bits_of(DP)))] + [(CTX, b) for b in reversed(range(bits_of(CTX)))]
    if skip_first:
        dims = dims[1:]
    parts = len(dims)
    rows, cols = grad.shape
    grad = grad.reshape((2,) * parts + (rows >> parts, cols))
    for item in order:
        at = dims.index(item)
        grad = halve(grad, item[0], item[1], at)
        dims.pop(at)
    return grad


def shards(ends, segment_ids, ln1_gain, ln1_bias, qkv_weight, out_weight, ln2_gain, ln2_bias, fc_weight, fc_bias,
           proj_weight, shared_weight):
    core = lax.axis_index(SECTION)
    first = core == 0
    C, m = lax.axis_size(CTX), bits_of(DP)
    J = C << m
    micros, T, D = ends.shape[1:]
    F = fc_weight.shape[2]
    half, FH = D // 2, F // 2
    names = ("xall", "q", "k", "v", "o", "lse", "r", "hr", "hh", "gp", "act", "y", "yb", "gy", "sm", "watt", "wfc", "wproj", "act_in", "gm_in", "kseg")
    kept = dict(zip(names, forward_pass(
        C, m, ends, segment_ids, ln1_gain, ln1_bias, ln2_gain, ln2_bias, qkv_weight, out_weight,
        fc_weight, fc_bias, proj_weight, shared_weight)))
    block, small, fcb_out, *rest = backward_pass(C, m, T, D, F, kept)
    ln, grads = rest[:4], rest[4:]
    if len(grads) != 5:
        theirs = swap(jnp.where(first, small[5], small[4]))
        ours = jnp.where(first, small[4], small[5])
        bias = jnp.where(first, jnp.concatenate([ours, theirs]), jnp.concatenate([theirs, ours]))
        j = lax.axis_index(DP) * C + lax.axis_index(CTX)
        fcb_out = lax.dynamic_slice_in_dim(bias, j * (F // J), F // J, 0)[None]
        ln = [lax.dynamic_slice_in_dim(small[i : i + 1, :D], j * (D // J), D // J, 1) for i in range(4)]
        grads = scattered(grads, core, m, half)
    block, fcb_out, *rest = assemble([block, fcb_out, *ln, *grads])
    ln, (qkv_out, out_out, fc_out, proj_out, shared_out) = rest[:4], rest[4:]
    return (block, qkv_out, out_out, fc_out, fcb_out, proj_out, shared_out, *ln)


def own_part(values, j, J):
    width = values.shape[1] // J
    at = lax.broadcasted_iota(jnp.int32, (values.shape[1], width), 0) - j * width
    pick = (at == lax.broadcasted_iota(jnp.int32, (values.shape[1], width), 1)).astype(F32)
    return jnp.dot(values, pick, precision=lax.Precision.HIGHEST, preferred_element_type=F32)


def assemble_kernel(*refs):
    n = (len(refs) - 2) // 2
    ins, outs, bounce, dma = refs[:n], refs[n:-2], refs[-2], refs[-1]
    come = [pltpu.make_async_copy(a, b, dma.at[i]) for i, (a, b) in enumerate(zip(ins, bounce))]
    for cp in come:
        cp.start()
    copies = []
    for i in range(n):
        come[i].wait()
        copies.append(pltpu.make_async_copy(bounce[i], outs[i], dma.at[i]))
        copies[-1].start()
    for cp in copies:
        cp.wait()


def assemble(arrays):
    return pl.pallas_call(
        assemble_kernel,
        in_specs=[HBM] * len(arrays),
        out_specs=[HBM] * len(arrays),
        out_shape=[jax.ShapeDtypeStruct(a.shape, a.dtype) for a in arrays],
        scratch_shapes=[[pltpu.VMEM(a.shape, a.dtype) for a in arrays], pltpu.SemaphoreType.DMA((len(arrays),))],
        compiler_params=pltpu.CompilerParams(vmem_limit_bytes=VMEM_LIMIT),
        name="assemble",
    )(*arrays)


def scattered(grads, core, m, half):
    gproj, gfc, gout, gq, gk, gv = grads
    first = core == 0
    x_first = [(DP, b) for b in range(m)] + [(CTX, b) for b in range(bits_of(CTX))]
    y_first = [(DP, b) for b in reversed(range(m))] + x_first[m:]

    def sided(grad):
        dp, size = lax.axis_index(DP), lax.axis_size(DP)
        top = size // 2
        route = [(c * size + d, c * size + (d ^ top)) for c in range(2) for d in range(size) if (d >= top) != (c == 1)]
        got = lax.ppermute(grad, (SECTION, DP), route)
        return scatter_sum((grad.astype(F32) + got.astype(F32)).astype(BF16), y_first[1:], skip_first=True)

    res = []
    for l in range(2):
        qkv = jnp.concatenate([gq[l], gk[l], gv[l]], axis=1)
        res.append((scatter_sum(qkv, x_first), sided(gout[l]), scatter_sum(gfc[l], x_first),
                    scatter_sum(gproj[l], y_first[1:], skip_first=True)))
    holder = jnp.where(lax.axis_index(DP) >= lax.axis_size(DP) // 2, 1, 0) == core
    mine = tuple(jnp.where(first, a, b) for a, b in zip(res[0], res[1]))
    got = tuple(swap(jnp.where(first, b, a)) for a, b in zip(res[0], res[1]))
    left, right = [jnp.where(first, a, b).astype(F32) for a, b in zip(mine, got)], [jnp.where(first, b, a).astype(F32) for a, b in zip(mine, got)]
    fresh0 = res[0][0][:, 2 * half :]
    fresh0_other = swap(fresh0)
    fresh = jnp.where(first, fresh0_other, res[1][0][:, 2 * half :]).astype(F32)
    qkv_out = jnp.concatenate([left[0][:, :half], right[0][:, :half], left[0][:, half : 2 * half], right[0][:, half : 2 * half], fresh], axis=1)
    fc_out = jnp.concatenate([left[2], right[2]], axis=1)
    out_out = jnp.where(holder, mine[1], got[1]).astype(F32)
    proj_out = jnp.where(holder, mine[3], got[3]).astype(F32)
    shared_out = jnp.where(first, fresh0, fresh0_other).astype(F32)
    return qkv_out[None], out_out[None], fc_out[None], proj_out[None], shared_out


def solution(mesh):
    placed = (
        P(SECTION, DP, CTX, None), P(DP, CTX), P(SECTION, None), P(SECTION, None),
        P(SECTION, None, None), P(SECTION, None, None), P(SECTION, None), P(SECTION, None),
        P(SECTION, None, None), P(SECTION, None), P(SECTION, None, None), P(),
    )
    both = (DP, CTX)
    return jax.shard_map(
        shards, mesh=mesh, in_specs=placed,
        out_specs=(P(SECTION, DP, CTX, None), P(SECTION, both, None), P(SECTION, both, None),
                   P(SECTION, both, None), P(SECTION, both), P(SECTION, both, None), P(both, None),
                   P(SECTION, both), P(SECTION, both), P(SECTION, both), P(SECTION, both)),
        check_vma=False,
    )
```
